512 devices in a mesh: tile: 128 (over z, y, x_hi), depth: 4 (over x_lo, core).
Axes of the slice: x: 4 (x_hi: 2, x_lo: 2; x = x_hi * 2 + x_lo), y: 8, z: 8, core: 2. Of those that a mesh axis runs over, the one named last changes fastest.
Arguments:
- positions: float32 [3, 262144], P(None, 'tile'), may hold values from -4 to 4
- log_scales: float32 [3, 262144], P(None, 'tile'), may hold values from -2 to 0
- opacity_logits: float32 [1, 262144], P(None, 'tile'), may hold values from -3 to 1.5
- colors: float32 [3, 262144], P(None, 'tile'), may hold values from 0 to 1
- first_moment: float32 [10, 262144], P(None, 'tile'), may hold values from -3 to 3
- second_moment: float32 [10, 262144], P(None, 'tile'), may hold values from 0.01 to 1
- cameras: float32 [4, 2, 4], replicated, may hold values from -6.4 to 6.4
- background: float32 [3], replicated, may hold values from 0 to 1
- target: float32 [512, 3, 1024], P('tile'), may hold values from 0 to 1
- tile_view: int32 [512], P('tile'), may hold values from 0 to 3
- tile_length: int32 [512], P('tile'), may hold values from 128 to 512
- list_owner: int32 [4, 512, 128, 1], P('depth', 'tile'), may hold values from 0 to 127; in each aligned block of 512 rows (0 to 511, 512 to 1023, ..., all dimensions but the last counted through in order) at most 10 rows name the same one
- list_row: int32 [4, 512, 128], P('depth', 'tile'), may hold values from 0 to 2047
Outputs:
- image: float32 [512, 3, 1024], P('tile')
- new_params: float32 [10, 262144], P(None, 'tile')
- new_first: float32 [10, 262144], P(None, 'tile')
- new_second: float32 [10, 262144], P(None, 'tile')
The draws below stay inside these ranges and needn't reach their ends.
Inputs may be any that keep to these rules, and one draw needn't show every extreme that they name: `list_owner`: within the entries of one device's block (one depth slab of the tiles of one tile index), no owner is named more than 10 times, a bound that some block reaches.
All inputs are finite; a program needn't handle non-finite values.
Results may differ from the reference program's by a relative error of at most 0.00008.
Values sent between devices are 32-bit elements; how exact they have to be, the bound alone decides.
No kernel may reach another device: no remote copies, remote signals or barrier semaphores. Data moves between devices by JAX's collectives and lax.ppermute only.
A program may use at most 64 MiB of HBM per device.

```python
import math
import jax
import jax.numpy as jnp
import numpy as np
from jax import lax

TILE_SIDE = 32
PIX = 1024
LIST = 512
VIEWS = 4
TILES_DEV = 4
G_DEV = 2048
TILES = 512
SPLATS = 262144
SLAB = 128
CAP = 10
N_TILE = 128
N_DEPTH = 4


def with_ends(drawn, rng, smallest, top_value):
    spot = [jax.random.randint(jax.random.fold_in(rng, axis), (), 0, length) for axis, length in enumerate(drawn.shape)]
    main_axis = drawn.shape.index(max(drawn.shape))
    neighbour = spot[:main_axis] + [(spot[main_axis] + 1) % drawn.shape[main_axis]] + spot[main_axis + 1:]
    return drawn.at[tuple(spot)].set(smallest).at[tuple(neighbour)].set(top_value)


def shard_levels(rng, extent, shards, least, top_value):
    level = 1.0
    for dim, blocks in shards:
        draws = jax.random.uniform(jax.random.fold_in(jax.random.fold_in(rng, 6), dim), (blocks,), jnp.float32, least / len(shards), top_value / len(shards))
        level = level * jnp.repeat(jnp.exp(draws), extent[dim] // blocks).reshape((-1,) + (1,) * (len(extent) - 1 - dim))
    return level


def deal_out(key, own, number, rows, count, top, limit, slope):
    order = jax.random.permutation(key, count)
    crowded, usual = portions_of(count, rows * top, limit, slope, True), portions_of(count, rows * top, limit, slope, False)
    places = jnp.arange(count)

    def named(tallies, turn):
        used = int((tallies > 0).sum())
        fixed = max(1, used // 4)
        passed = fixed + (places - fixed + turn * (used - fixed)) % max(1, count - fixed)
        return jnp.zeros((count,), jnp.int32).at[order[jnp.where(places < fixed, places, passed)]].set(jnp.asarray(tallies, jnp.int32))

    tallies = jnp.where(number % 4 == 0, named(crowded, number // 4), named(usual, number - number // 4 - 1))
    mixed = jax.random.permutation(jax.random.fold_in(own, 3), count)
    donor, sink = mixed[0:count // 2 * 2:2], mixed[1:count // 2 * 2:2]
    margin = jnp.minimum(tallies[donor] - 1, limit - tallies[sink]) // 2
    margin = jnp.where((donor == order[0]) | (sink == order[0]) | (tallies[sink] == 0), 0, jnp.maximum(margin, 0))
    passed = jax.random.randint(jax.random.fold_in(own, 4), (count // 2,), 0, 1 << 20) % (margin + 1)
    tallies = tallies.at[donor].add(-passed).at[sink].add(passed)
    labels = jnp.searchsorted(jnp.cumsum(tallies), jnp.arange(rows * top), side="right").astype(jnp.int32)
    table = labels.reshape(top, rows).T
    table = table[jax.random.permutation(jax.random.fold_in(own, 1), rows)]
    turn = jax.random.randint(jax.random.fold_in(own, 2), (rows, 1), 0, top)
    return jnp.take_along_axis(table, (jnp.arange(top)[None, :] + turn) % top, axis=1)


def portions_of(number_of, total, bound, lean, full):
    loads = [(1 << 20) // math.isqrt(standing ** lean) + 1 for standing in range(1, number_of + 1)]
    largest = bound if full else min(bound, max(-(-total // number_of), total * loads[0] // sum(loads)))
    least = 1 if total - largest >= number_of - 1 else 0
    given, surplus = [largest] + [least] * (number_of - 1), total - largest - least * (number_of - 1)
    while surplus > 0:
        movable = [i for i in range(1, number_of) if given[i] < largest] or [i for i in range(1, number_of) if given[i] < bound]
        whole, budget = sum([loads[i] for i in movable]), surplus
        for i in movable:
            extra = min(bound - given[i], max(1, budget * loads[i] // whole), surplus)
            given[i] = given[i] + extra
            surplus = surplus - extra
    return np.array(given)


def normal_values(key, shape, scale, most, split=(), kind=jnp.bfloat16):
    values = scale * jax.random.normal(key, shape, jnp.float32)
    if split:
        values = values * shard_levels(key, shape, split, -0.22, 0.18)
    return jnp.clip(values, -most, most).astype(kind)


def setup_inputs(seed: int = 0) -> dict:
    seeds = jax.random.split(jax.random.key(seed), 14)
    positions = normal_values(seeds[0], (3, SPLATS), 1.0, 4.0, ((1, 128),), jnp.float32)
    log_scales = jnp.clip(-2.0 + 2.0 * jax.random.uniform(seeds[1], (3, SPLATS), jnp.float32) ** shard_levels(seeds[1], (3, SPLATS), ((1, 128),), -0.2, 0.2), -2.0, 0.0)
    opacity_logits = jnp.clip(-3.0 + 4.5 * jax.random.uniform(seeds[2], (1, SPLATS), jnp.float32) ** shard_levels(seeds[2], (1, SPLATS), ((1, 128),), -0.2, 0.2), -3.0, 1.5)
    colors = jnp.clip(1.0 * jax.random.uniform(seeds[3], (3, SPLATS), jnp.float32) ** shard_levels(seeds[3], (3, SPLATS), ((1, 128),), -0.2, 0.2), 0.0, 1.0)
    first_moment = normal_values(seeds[4], (10, SPLATS), 0.5, 3.0, ((1, 128),), jnp.float32)
    second_moment = jnp.clip(jnp.exp(math.log(1.0) - 4.6051702 * jax.random.uniform(seeds[5], (10, SPLATS), jnp.float32) ** shard_levels(seeds[5], (10, SPLATS), ((1, 128),), -0.2, 0.2)), 0.01, 1.0)
    cameras = jnp.clip(jax.random.uniform(seeds[6], (VIEWS, 2, 4), jnp.float32, -6.4, 6.4), -6.4, 6.4)
    background = jnp.clip(jax.random.uniform(seeds[7], (3,), jnp.float32, 0.0, 1.0), 0.0, 1.0)
    target = jnp.clip(1.0 * jax.random.uniform(seeds[8], (TILES, 3, PIX), jnp.float32) ** shard_levels(seeds[8], (TILES, 3, PIX), ((0, 128),), -0.2, 0.2), 0.0, 1.0)
    tile_view = with_ends(jax.random.randint(seeds[9], (TILES,), 0, VIEWS), jax.random.fold_in(seeds[9], 1), 0, VIEWS - 1).astype(jnp.int32)
    tile_length = with_ends(jax.random.randint(seeds[10], (TILES,), LIST // 4, LIST + 1), jax.random.fold_in(seeds[10], 1), LIST // 4, LIST).astype(jnp.int32)
    list_owner_keys = jax.random.split(jax.random.fold_in(seeds[11], 1), N_DEPTH * TILES * SLAB // (TILES_DEV * SLAB))
    list_owner_turns = jax.random.permutation(jax.random.fold_in(seeds[11], 3), N_DEPTH * TILES * SLAB // (TILES_DEV * SLAB))
    list_owner = jax.vmap(lambda own, number: deal_out(jax.random.fold_in(seeds[11], 2), own, number, TILES_DEV * SLAB, N_TILE, 1, CAP, 2))(list_owner_keys, list_owner_turns).reshape((N_DEPTH, TILES, SLAB, 1))
    list_row = with_ends(jax.random.randint(seeds[12], (N_DEPTH, TILES, SLAB), 0, G_DEV), jax.random.fold_in(seeds[12], 1), 0, G_DEV - 1).astype(jnp.int32)
    return dict(positions=positions, log_scales=log_scales, opacity_logits=opacity_logits, colors=colors, first_moment=first_moment, second_moment=second_moment, cameras=cameras, background=background, target=target, tile_view=tile_view, tile_length=tile_length, list_owner=list_owner, list_row=list_row)


def project(params, cams):
    position = params[0:3]
    variance = jnp.exp(2.0 * params[3:6])
    first_row = cams[:, 0, 0:3].T
    second_row = cams[:, 1, 0:3].T
    center_x = lax.optimization_barrier(jnp.sum(first_row * position, axis=0)) + cams[:, 0, 3] + 0.5 * TILE_SIDE
    center_y = lax.optimization_barrier(jnp.sum(second_row * position, axis=0)) + cams[:, 1, 3] + 0.5 * TILE_SIDE
    cov_xx = lax.optimization_barrier(jnp.sum(first_row * first_row * variance, axis=0)) + 0.3
    cov_xy = lax.optimization_barrier(jnp.sum(first_row * second_row * variance, axis=0))
    cov_yy = lax.optimization_barrier(jnp.sum(second_row * second_row * variance, axis=0)) + 0.3
    determinant = cov_xx * cov_yy - cov_xy * cov_xy
    return jnp.stack([center_x, center_y, cov_yy / determinant, -cov_xy / determinant, cov_xx / determinant, jax.nn.sigmoid(params[6]), params[7], params[8], params[9]])

def render_tile(screen, alive, background):
    pixel = jnp.arange(PIX, dtype=jnp.int32)
    pixel_x = (pixel % TILE_SIDE).astype(jnp.float32) + 0.5
    pixel_y = (pixel // TILE_SIDE).astype(jnp.float32) + 0.5
    offset_x = pixel_x[:, None] - screen[0][None, :]
    offset_y = pixel_y[:, None] - screen[1][None, :]
    quadric = screen[2][None, :] * offset_x * offset_x + 2.0 * screen[3][None, :] * offset_x * offset_y + screen[4][None, :] * offset_y * offset_y
    alpha = screen[5][None, :] * jnp.exp(-0.5 * quadric) * alive[None, :]
    leak = jnp.log1p(-alpha)
    before = jnp.cumsum(leak, axis=1) - leak
    weight = alpha * jnp.exp(before)
    color = jnp.einsum('ck,pk->cp', screen[6:9], weight, precision=lax.Precision.HIGHEST)
    return color + jnp.exp(lax.optimization_barrier(jnp.sum(leak, axis=1)))[None, :] * background[:, None]

def reference(positions, log_scales, opacity_logits, colors, first_moment, second_moment, cameras, background, target, tile_view, tile_length, list_owner, list_row):
    params = jnp.concatenate([positions, log_scales, opacity_logits, colors], axis=0)
    ident = (list_owner[..., 0] * G_DEV + list_row).astype(jnp.int32)
    ident = jnp.transpose(ident, (1, 0, 2)).reshape(TILES, LIST)
    live = (jnp.arange(LIST, dtype=jnp.int32)[None, :] < tile_length[:, None]).astype(jnp.float32)

    def render(values):

        def single(args):
            names, view, alive = args
            cams = jnp.broadcast_to(cameras[view], (LIST, 2, 4))
            screen = project(values[:, names], cams)
            return render_tile(screen, alive, background)
        return lax.map(jax.checkpoint(single), (ident, tile_view, live))
    image, pullback = jax.vjp(render, params)
    gradient, = pullback(image - target)
    new_first = 0.9 * first_moment + 0.1 * gradient
    new_second = 0.999 * second_moment + 0.001 * gradient * gradient
    corrected = new_first / (1.0 - 0.9 ** 10) / (jnp.sqrt(new_second / (1.0 - 0.999 ** 10)) + 1e-08)
    new_params = params - 0.05 * corrected
    return (image, new_params, new_first, new_second)
```

```python
import math

import jax
import jax.numpy as jnp
from jax import lax
from jax.experimental import pallas as pl
from jax.experimental.pallas import tpu as pltpu
from jax.sharding import PartitionSpec as P

LANES = 128
TILES = 4
SLAB = 128
DEPTHS = 4
SLOTS = 10
PARAMS = 10
BLOCKS = 16
LOG2E = math.log2(math.e)
VMEM = pl.BlockSpec(memory_space=pltpu.VMEM)
SMEM = pl.BlockSpec(memory_space=pltpu.SMEM)
F32 = jnp.float32
BF16 = jnp.bfloat16
I32 = jnp.int32
NT = (((1,), (1,)), ((), ()))
NN = (((1,), (0,)), ((), ()))


def iota(shape, dim):
    return lax.broadcasted_iota(I32, shape, dim)


def pieces(x):
    high = x.astype(BF16)
    rest = x - high.astype(F32)
    middle = rest.astype(BF16)
    low = (rest - middle.astype(F32)).astype(BF16)
    return high, middle, low


def side_by_side(x):
    return jnp.concatenate(pieces(x), axis=1)


def dot(a, b, dims):
    return lax.dot_general(a, b, dims, preferred_element_type=F32)


def onehot(index, rows):
    return jnp.where(iota((rows, LANES), 0) == index, 1.0, 0.0)


def request_kernel(owner_ref, row_ref, request_ref, rank_ref):
    earlier = jnp.where(iota((SLAB, SLAB), 0) < iota((SLAB, SLAB), 1), 1.0, 0.0).astype(BF16)
    before = jnp.zeros((LANES, 1), F32)
    total = jnp.zeros((LANES, LANES), F32)
    for b in range(TILES):
        named = onehot(owner_ref[b : b + 1, :], LANES)
        named_16 = named.astype(BF16)
        count = dot(named_16, earlier, NN) + before
        before = before + jnp.sum(named, axis=1, keepdims=True)
        rank = jnp.sum(named * count, axis=0, keepdims=True).astype(I32)
        rank_ref[b : b + 1, :] = rank
        row = row_ref[b : b + 1, :]
        here = iota((LANES, SLAB), 0) == rank
        high = jnp.where(here, row >> 4, 0).astype(F32).astype(BF16)
        low = jnp.where(here, row & 15, 0).astype(F32).astype(BF16)
        total = total + 16.0 * dot(named_16, high, NT) + dot(named_16, low, NT)
    request_ref[...] = total.astype(I32)


def reply_kernel(asked_ref, params_ref, reply_ref, columns, held):
    columns[...] = asked_ref[...].T
    table = jnp.concatenate(
        [
            jnp.concatenate(
                [
                    params_ref[:, a * LANES : (a + 1) * LANES],
                    jnp.zeros((16 - PARAMS, LANES), F32),
                ],
                axis=0,
            )
            for a in range(BLOCKS)
        ],
        axis=0,
    )
    table = side_by_side(table)
    for r in range(SLOTS):
        row = columns[r : r + 1, :]
        pick = onehot(row & (LANES - 1), LANES).astype(BF16)
        found = dot(table, jnp.concatenate([pick, pick, pick], axis=0), NN)
        block = row >> 7
        value = jnp.zeros((16, LANES), F32)
        for a in range(BLOCKS):
            value = value + jnp.where(block == a, found[a * 16 : (a + 1) * 16], 0.0)
        held[r * PARAMS : r * PARAMS + 16, :] = value
    held[SLOTS * PARAMS :, :] = jnp.zeros((LANES - SLOTS * PARAMS, LANES), F32)
    reply_ref[...] = held[...].T


def per_tile(values):
    place = iota((TILES, LANES), 0)
    out = jnp.full((TILES, LANES), values[0], F32)
    for b in range(1, TILES):
        out = jnp.where(place == b, values[b], out)
    return out


def camera_rows(view_ref, cams_ref):
    return [
        [per_tile([cams_ref[view_ref[b] * 8 + i * 4 + j] for b in range(TILES)]) for j in range(4)]
        for i in range(2)
    ]


def covariance(scales, jac):
    variance = [jnp.exp(2.0 * s) for s in scales]
    xx = sum(jac[0][j] * jac[0][j] * variance[j] for j in range(3)) + 0.3
    xy = sum(jac[0][j] * jac[1][j] * variance[j] for j in range(3))
    yy = sum(jac[1][j] * jac[1][j] * variance[j] for j in range(3)) + 0.3
    return variance, xx, xy, yy, xx * yy - xy * xy


def forward_kernel(
    fetched_ref,
    owner_ref,
    rank_ref,
    view_ref,
    length_ref,
    cams_ref,
    depth_ref,
    slab_ref,
    alpha_ref,
    weight_ref,
    shade_ref,
    entry_ref,
    found,
    rows,
    spread,
):
    fetched = side_by_side(fetched_ref[...].T)
    for b in range(TILES):
        named = onehot(owner_ref[b : b + 1, :], LANES).astype(BF16)
        found[...] = dot(fetched, jnp.concatenate([named, named, named], axis=0), NN)
        rank = rank_ref[b : b + 1, :]
        value = jnp.zeros((16, LANES), F32)
        for r in range(SLOTS):
            value = value + jnp.where(rank == r, found[r * PARAMS : r * PARAMS + 16, :], 0.0)
        entry_ref[b * 16 : (b + 1) * 16, :] = value
    entry = [entry_ref[pl.ds(p, TILES, stride=16), :] for p in range(PARAMS)]
    jac = camera_rows(view_ref, cams_ref)
    center_x = sum(jac[0][j] * entry[j] for j in range(3)) + jac[0][3] + 16.0
    center_y = sum(jac[1][j] * entry[j] for j in range(3)) + jac[1][3] + 16.0
    _, xx, xy, yy, det = covariance(entry[3:6], jac)
    place = depth_ref[0] * SLAB + iota((TILES, LANES), 1).astype(I32)
    length = per_tile([length_ref[b].astype(F32) for b in range(TILES)])
    live = jnp.where(place.astype(F32) < length, 1.0, 0.0)
    opacity = jax.nn.sigmoid(entry[6]) * live
    factors = [
        center_x,
        center_y,
        (-0.5 * LOG2E) * (yy / det),
        LOG2E * (xy / det),
        (-0.5 * LOG2E) * (xx / det),
        opacity,
        *entry[7:10],
    ]
    for p, factor in enumerate(factors):
        rows[p * TILES : (p + 1) * TILES, :] = factor
    rows[len(factors) * TILES :, :] = jnp.zeros((LANES - len(factors) * TILES, LANES), F32)
    turned = rows[...].T
    for p in range(9):
        for b in range(TILES):
            column = turned[:, p * TILES + b : p * TILES + b + 1]
            wide = jnp.broadcast_to(column, (SLAB, LANES))
            if p < 6:
                spread[p, b * SLAB : (b + 1) * SLAB, :] = wide
            else:
                shade_ref[p - 6, b * SLAB : (b + 1) * SLAB, :] = wide
    lane = iota((8, LANES), 1)
    pixel_x = (lane & 31).astype(F32) + 0.5
    pixel_y = (iota((8, LANES), 0) * 4 + (lane >> 5)).astype(F32) + 0.5

    def step(k, carry):
        out = []
        for b in range(TILES):
            trans, red, green, blue = carry[4 * b : 4 * b + 4]
            at = b * SLAB + k
            get = lambda ref, p: jnp.broadcast_to(ref[p, pl.ds(at, 1), :], (8, LANES))
            ex = pixel_x - get(spread, 0)
            ey = pixel_y - get(spread, 1)
            power = ex * (get(spread, 2) * ex + get(spread, 3) * ey) + get(spread, 4) * ey * ey
            alpha = get(spread, 5) * jnp.exp2(power)
            weight = alpha * trans
            alpha_ref[at] = alpha
            weight_ref[at] = weight
            out += [
                trans - weight,
                red + weight * get(shade_ref, 0),
                green + weight * get(shade_ref, 1),
                blue + weight * get(shade_ref, 2),
            ]
        return tuple(out)

    one, zero = jnp.ones((8, LANES), F32), jnp.zeros((8, LANES), F32)
    out = lax.fori_loop(0, SLAB, step, (one, zero, zero, zero) * TILES, unroll=4)
    for q in range(4 * TILES):
        slab_ref[q * 8 : (q + 1) * 8, :] = out[q]


def backward_kernel(
    slabs_ref,
    alpha_ref,
    weight_ref,
    shade_ref,
    entry_ref,
    owner_ref,
    rank_ref,
    view_ref,
    cams_ref,
    depth_ref,
    back_ref,
    target_ref,
    image_ref,
    outgoing_ref,
    slope,
    moment,
    grads,
    placed,
    picture,
):
    depth = depth_ref[0]
    back = [back_ref[c] for c in range(3)]
    seen, behind = [], []
    for c in range(3):
        for s in range(8):
            picture[pl.ds(c * TILES * 8 + s, TILES, stride=8), :] = target_ref[
                c, :, s * LANES : (s + 1) * LANES
            ]
    for b in range(TILES):
        part = lambda i, q: slabs_ref[i, (b * 4 + q) * 8 : (b * 4 + q + 1) * 8, :]
        trans = jnp.ones((8, LANES), F32)
        start = jnp.ones((8, LANES), F32)
        color = [jnp.zeros((8, LANES), F32)] * 3
        for i in range(DEPTHS):
            start = jnp.where(depth == i, trans, start)
            color = [color[c] + trans * part(i, 1 + c) for c in range(3)]
            trans = trans * part(i, 0)
        color = [color[c] + trans * back[c] for c in range(3)]
        miss = []
        for c in range(3):
            at = slice((c * TILES + b) * 8, (c * TILES + b + 1) * 8)
            miss.append(color[c] - picture[at, :])
            picture[at, :] = color[c]
        after = sum(back[c] * miss[c] for c in range(3))
        for i in range(DEPTHS - 1, 0, -1):
            joined = sum(part(i, 1 + c) * miss[c] for c in range(3)) + part(i, 0) * after
            after = jnp.where(i > depth, joined, after)
        seen.append([start * miss[c] for c in range(3)])
        behind.append(start * after)
    for c in range(3):
        for s in range(8):
            image_ref[c, :, s * LANES : (s + 1) * LANES] = picture[
                pl.ds(c * TILES * 8 + s, TILES, stride=8), :
            ]

    def step(n, carry):
        k = SLAB - 1 - n
        out = []
        for b in range(TILES):
            at = b * SLAB + k
            get = lambda p: jnp.broadcast_to(shade_ref[p, pl.ds(at, 1), :], (8, LANES))
            shade = sum(get(c) * seen[b][c] for c in range(3))
            gap = shade - carry[b]
            slope[at] = weight_ref[at] * gap
            out.append(carry[b] + alpha_ref[at] * gap)
        return tuple(out)

    lax.fori_loop(0, SLAB, step, tuple(behind), unroll=4)

    index = iota((16, LANES), 0)
    lane = iota((16, LANES), 1)
    across = (lane & 31) - 16
    sixteen = jnp.zeros((16, LANES), F32)
    for b in range(TILES):
        total = sixteen
        shades = sixteen
        for s in range(8):
            down = s * 4 + (lane >> 5) - 16
            powers = jnp.where(index == 0, 1, 0)
            for n, value in enumerate(
                (across, down, across * across, across * down, down * down), 1
            ):
                powers = jnp.where(index == n, value, powers)
            powers = powers.astype(F32).astype(BF16)
            field = side_by_side(slope[b * SLAB : (b + 1) * SLAB, s, :])
            total = total + dot(jnp.concatenate([powers] * 3, axis=1), field, NT)
            gaze = jnp.concatenate(
                [seen[b][c][s : s + 1, :] for c in range(3)] + [jnp.zeros((13, LANES), F32)],
                axis=0,
            )
            shades = shades + lax.dot_general(
                gaze,
                weight_ref[b * SLAB : (b + 1) * SLAB, s, :],
                NT,
                precision=lax.Precision.HIGHEST,
                preferred_element_type=F32,
            )
        moment[b * 32 : b * 32 + 16, :] = total
        moment[b * 32 + 16 : (b + 1) * 32, :] = shades
    entry = [entry_ref[pl.ds(p, TILES, stride=16), :] for p in range(PARAMS)]
    jac = camera_rows(view_ref, cams_ref)
    m0, mx, my, mxx, mxy, myy = (moment[pl.ds(n, TILES, stride=32), :] for n in range(6))
    variance, xx, xy, yy, det = covariance(entry[3:6], jac)
    cx = sum(jac[0][j] * entry[j] for j in range(3)) + jac[0][3] - 0.5
    cy = sum(jac[1][j] * entry[j] for j in range(3)) + jac[1][3] - 0.5
    sx = mx - cx * m0
    sy = my - cy * m0
    sxx = mxx - cx * (mx + sx)
    sxy = mxy - cx * my - cy * sx
    syy = myy - cy * (my + sy)
    inverse = 1.0 / det
    conic = (yy * inverse, -xy * inverse, xx * inverse)
    d_cx = conic[0] * sx + conic[1] * sy
    d_cy = conic[1] * sx + conic[2] * sy
    d_a, d_b, d_c = -0.5 * sxx, -sxy, -0.5 * syy
    d_det = -(d_a * conic[0] + d_b * conic[1] + d_c * conic[2]) * inverse
    d_xx = d_c * inverse + d_det * yy
    d_yy = d_a * inverse + d_det * xx
    d_xy = -d_b * inverse - 2.0 * xy * d_det
    result = [jac[0][j] * d_cx + jac[1][j] * d_cy for j in range(3)]
    result += [
        2.0
        * variance[j]
        * (
            jac[0][j] * jac[0][j] * d_xx
            + jac[0][j] * jac[1][j] * d_xy
            + jac[1][j] * jac[1][j] * d_yy
        )
        for j in range(3)
    ]
    result += [m0 * (1.0 - jax.nn.sigmoid(entry[6]))]
    result += [moment[pl.ds(16 + c, TILES, stride=32), :] for c in range(3)]
    for p, value in enumerate(result):
        grads[p * TILES : (p + 1) * TILES, :] = value
    placed[...] = jnp.zeros((LANES, LANES), F32)
    outgoing = jnp.zeros((LANES, LANES), F32)
    for b in range(TILES):
        mine = grads[pl.ds(b, PARAMS, stride=TILES), :]
        rank = rank_ref[b : b + 1, :]
        for r in range(SLOTS):
            placed[r * PARAMS : (r + 1) * PARAMS, :] = jnp.where(rank == r, mine, 0.0)
        named = onehot(owner_ref[b : b + 1, :], LANES).astype(BF16)
        named = jnp.concatenate([named, named, named], axis=1)
        outgoing = outgoing + dot(named, side_by_side(placed[...]), NT)
    outgoing_ref[...] = outgoing


def collect_kernel(asked_ref, incoming_ref, sums_ref, columns, turned):
    columns[...] = asked_ref[...].T
    turned[...] = incoming_ref[...].T
    total = jnp.zeros((BLOCKS * 16, LANES), F32)
    for r in range(SLOTS):
        row = columns[r : r + 1, :]
        pick = onehot(row & (LANES - 1), LANES).astype(BF16)
        block = row >> 7
        value = turned[r * PARAMS : r * PARAMS + 16, :]
        spread = jnp.concatenate(
            [jnp.where(block == a, value, 0.0) for a in range(BLOCKS)], axis=0
        )
        total = total + dot(
            side_by_side(spread), jnp.concatenate([pick, pick, pick], axis=1), NT
        )
    for a in range(BLOCKS):
        sums_ref[a * PARAMS : (a + 1) * PARAMS, :] = total[a * 16 : a * 16 + PARAMS]


def adam_kernel(sums_ref, params_ref, first_ref, second_ref, new_ref, new_first_ref, new_second_ref):
    for a in range(BLOCKS):
        at = slice(a * LANES, (a + 1) * LANES)
        gradient = sum(sums_ref[i, a * PARAMS : (a + 1) * PARAMS, :] for i in range(DEPTHS))
        first = 0.9 * first_ref[:, at] + 0.1 * gradient
        second = 0.999 * second_ref[:, at] + 0.001 * gradient * gradient
        step = first / (1.0 - 0.9**10) / (jnp.sqrt(second / (1.0 - 0.999**10)) + 1e-08)
        new_ref[:, at] = params_ref[:, at] - 0.05 * step
        new_first_ref[:, at] = first
        new_second_ref[:, at] = second


def call(kernel, outs, ins, scratch=()):
    return pl.pallas_call(
        kernel,
        out_shape=[jax.ShapeDtypeStruct(shape, dtype) for shape, dtype in outs],
        in_specs=ins,
        out_specs=[VMEM] * len(outs),
        scratch_shapes=[pltpu.VMEM(shape, dtype) for shape, dtype in scratch],
        compiler_params=pltpu.CompilerParams(vmem_limit_bytes=40 * 2**20),
    )


def exchanged(array):
    whole = lax.all_to_all(array.reshape(LANES, 1, LANES), "tile", 0, 0, tiled=True)
    return whole.reshape(LANES, LANES)


def body(
    positions,
    log_scales,
    opacity_logits,
    colors,
    first_moment,
    second_moment,
    cameras,
    background,
    target,
    tile_view,
    tile_length,
    list_owner,
    list_row,
):
    square = (LANES, LANES)
    owner = list_owner.reshape(TILES, SLAB)
    wanted = list_row.reshape(TILES, SLAB)
    depth = lax.axis_index("depth").astype(I32).reshape(1)
    cams = cameras.reshape(-1)
    params = jnp.concatenate([positions, log_scales, opacity_logits, colors], axis=0)
    request, rank = call(
        request_kernel, [(square, I32), ((TILES, SLAB), I32)], [VMEM, VMEM]
    )(owner, wanted)
    asked = exchanged(request)
    (reply,) = call(
        reply_kernel, [(square, F32)], [VMEM, VMEM], [(square, I32), (square, F32)]
    )(asked, params)
    fetched = exchanged(reply)
    field = (TILES * SLAB, 8, LANES)
    slab, alpha, weight, shade, entry = call(
        forward_kernel,
        [
            (square, F32),
            (field, F32),
            (field, F32),
            ((3, TILES * SLAB, LANES), F32),
            ((TILES * 16, LANES), F32),
        ],
        [VMEM] * 3 + [SMEM] * 4,
        [(square, F32), (square, F32), ((6, TILES * SLAB, LANES), F32)],
    )(fetched, owner, rank, tile_view, tile_length, cams, depth)
    slabs = lax.all_gather(slab[None], "depth", axis=0, tiled=True)
    image, outgoing = call(
        backward_kernel,
        [((3, TILES, 1024), F32), (square, F32)],
        [VMEM] * 7 + [SMEM] * 4 + [VMEM],
        [
            (field, F32),
            (square, F32),
            ((PARAMS * TILES, LANES), F32),
            (square, F32),
            ((3 * TILES * 8, LANES), F32),
        ],
    )(
        slabs,
        alpha,
        weight,
        shade,
        entry,
        owner,
        rank,
        tile_view,
        cams,
        depth,
        background,
        target.transpose(1, 0, 2),
    )
    incoming = exchanged(outgoing)
    (sums,) = call(
        collect_kernel,
        [((BLOCKS * PARAMS, LANES), F32)],
        [VMEM, VMEM],
        [(square, I32), (square, F32)],
    )(asked, incoming)
    sums = lax.all_gather(sums[None], "depth", axis=0, tiled=True)
    updated = call(adam_kernel, [(params.shape, F32)] * 3, [VMEM] * 4)(
        sums, params, first_moment, second_moment
    )
    return (image.transpose(1, 0, 2), *updated)


def solution(mesh):
    split = P(None, "tile")
    placed = (
        *[split] * 6,
        P(),
        P(),
        P("tile", None, None),
        P("tile"),
        P("tile"),
        P("depth", "tile", None, None),
        P("depth", "tile", None),
    )
    return jax.shard_map(
        body,
        mesh=mesh,
        in_specs=placed,
        out_specs=(P("tile", None, None), split, split, split),
        check_vma=False,
    )
```

```python
import math

import jax
import jax.numpy as jnp
from jax import lax
from jax.experimental import pallas as pl
from jax.experimental.pallas import tpu as pltpu
from jax.sharding import Mesh
from jax.sharding import PartitionSpec as P

LANES = 128
TILES = 4
SLAB = 128
DEPTHS = 4
SLOTS = 10
PARAMS = 10
BLOCKS = 16
LIVE, BACK, HERE, GOAL, FIXED = 32, 40, 64, 72, 168
PITCH = TILES * SLAB + 1
TILE = ("tile_z", "tile_y", "tile_x")
DEPTH = ("depth_x", "depth_core")
LOG2E = math.log2(math.e)
VMEM = pl.BlockSpec(memory_space=pltpu.VMEM)
SMEM = pl.BlockSpec(memory_space=pltpu.SMEM)
HBM = pl.BlockSpec(memory_space=pltpu.HBM)
F32 = jnp.float32
BF16 = jnp.bfloat16
I32 = jnp.int32
NT = (((1,), (1,)), ((), ()))
NN = (((1,), (0,)), ((), ()))


def iota(shape, dim):
    return lax.broadcasted_iota(I32, shape, dim)


def pieces(x):
    high = x.astype(BF16)
    rest = x - high.astype(F32)
    middle = rest.astype(BF16)
    low = (rest - middle.astype(F32)).astype(BF16)
    return high, middle, low


def side_by_side(x):
    return jnp.concatenate(pieces(x), axis=1)


def dot(a, b, dims):
    return lax.dot_general(a, b, dims, preferred_element_type=F32)


def onehot(index, rows):
    return jnp.where(iota((rows, LANES), 0) == index, 1.0, 0.0)


def request_kernel(owner_hbm, row_hbm, request_ref, rank_ref, owner_ref, row_ref, sems):
    copies = [
        pltpu.make_async_copy(owner_hbm, owner_ref, sems.at[0]),
        pltpu.make_async_copy(row_hbm, row_ref, sems.at[1]),
    ]
    for copy in copies:
        copy.start()
    for copy in copies:
        copy.wait()
    earlier = jnp.where(iota((SLAB, SLAB), 0) < iota((SLAB, SLAB), 1), 1.0, 0.0).astype(BF16)
    before = jnp.zeros((LANES, 1), F32)
    total = jnp.zeros((LANES, LANES), F32)
    for b in range(TILES):
        named = onehot(owner_ref[b : b + 1, :], LANES)
        named_16 = named.astype(BF16)
        count = dot(named_16, earlier, NN) + before
        before = before + jnp.sum(named, axis=1, keepdims=True)
        rank = jnp.sum(named * count, axis=0, keepdims=True).astype(I32)
        rank_ref[b : b + 1, :] = rank
        row = row_ref[b : b + 1, :]
        here = iota((LANES, SLAB), 0) == rank
        high = jnp.where(here, row >> 4, 0).astype(F32).astype(BF16)
        low = jnp.where(here, row & 15, 0).astype(F32).astype(BF16)
        total = total + 16.0 * dot(named_16, high, NT) + dot(named_16, low, NT)
    request_ref[...] = total.astype(I32)


def fixed_kernel(
    view_ref, length_ref, cams_ref, depth_ref, back_ref, target_ref, params_ref, fixed_ref, table_ref
):
    for i in range(2):
        for j in range(4):
            at = (i * 4 + j) * TILES
            fixed_ref[at : at + TILES, :] = per_tile([cams_ref[view_ref[b], i, j] for b in range(TILES)])
    place = depth_ref[0] * SLAB + iota((TILES, LANES), 1)
    length = per_tile([length_ref[b].astype(F32) for b in range(TILES)])
    fixed_ref[LIVE : LIVE + TILES, :] = jnp.where(place.astype(F32) < length, 1.0, 0.0)
    for c in range(3):
        fixed_ref[BACK + c * 8 : BACK + c * 8 + 8, :] = jnp.full((8, LANES), back_ref[c], F32)
    fixed_ref[HERE : HERE + 8, :] = jnp.full((8, LANES), depth_ref[0].astype(F32), F32)
    for c in range(3):
        for s in range(8):
            fixed_ref[pl.ds(GOAL + c * TILES * 8 + s, TILES, stride=8), :] = target_ref[
                c, :, s * LANES : (s + 1) * LANES
            ]
    for a in range(BLOCKS):
        block = jnp.concatenate(
            [params_ref[:, a * LANES : (a + 1) * LANES], jnp.zeros((16 - PARAMS, LANES), F32)], axis=0
        )
        table_ref[a * 16 : (a + 1) * 16, :] = side_by_side(block)


def reply_kernel(asked_ref, table_ref, reply_ref, columns, held):
    columns[...] = asked_ref[...].T
    table = table_ref[...]
    for r in range(SLOTS):
        row = columns[r : r + 1, :]
        pick = onehot(row & (LANES - 1), LANES).astype(BF16)
        found = dot(table, jnp.concatenate([pick, pick, pick], axis=0), NN)
        block = row >> 7
        value = jnp.zeros((16, LANES), F32)
        for a in range(BLOCKS):
            value = value + jnp.where(block == a, found[a * 16 : (a + 1) * 16], 0.0)
        held[r * PARAMS : r * PARAMS + 16, :] = value
    held[SLOTS * PARAMS :, :] = jnp.zeros((LANES - SLOTS * PARAMS, LANES), F32)
    reply_ref[...] = held[...].T


def per_tile(values):
    place = iota((TILES, LANES), 0)
    out = jnp.full((TILES, LANES), values[0], F32)
    for b in range(1, TILES):
        out = jnp.where(place == b, values[b], out)
    return out


def camera_rows(fixed_ref):
    rows = [fixed_ref[n * TILES : (n + 1) * TILES, :] for n in range(8)]
    return rows[:4], rows[4:]


def covariance(scales, jac):
    variance = [jnp.exp(2.0 * s) for s in scales]
    xx = sum(jac[0][j] * jac[0][j] * variance[j] for j in range(3)) + 0.3
    xy = sum(jac[0][j] * jac[1][j] * variance[j] for j in range(3))
    yy = sum(jac[1][j] * jac[1][j] * variance[j] for j in range(3)) + 0.3
    return variance, xx, xy, yy, xx * yy - xy * xy


def forward_kernel(
    fetched_ref,
    owner_ref,
    rank_ref,
    fixed_ref,
    slab_ref,
    alpha_ref,
    weight_ref,
    shade_ref,
    entry_ref,
    found,
    rows,
    spread,
):
    fetched = side_by_side(fetched_ref[...].T)
    for b in range(TILES):
        named = onehot(owner_ref[b : b + 1, :], LANES).astype(BF16)
        found[...] = dot(fetched, jnp.concatenate([named, named, named], axis=0), NN)
        rank = rank_ref[b : b + 1, :]
        value = jnp.zeros((16, LANES), F32)
        for r in range(SLOTS):
            value = value + jnp.where(rank == r, found[r * PARAMS : r * PARAMS + 16, :], 0.0)
        entry_ref[b * 16 : (b + 1) * 16, :] = value
    entry = [entry_ref[pl.ds(p, TILES, stride=16), :] for p in range(PARAMS)]
    jac = camera_rows(fixed_ref)
    center_x = sum(jac[0][j] * entry[j] for j in range(3)) + jac[0][3] + 16.0
    center_y = sum(jac[1][j] * entry[j] for j in range(3)) + jac[1][3] + 16.0
    _, xx, xy, yy, det = covariance(entry[3:6], jac)
    opacity = jax.nn.sigmoid(entry[6]) * fixed_ref[LIVE : LIVE + TILES, :]
    factors = [
        center_x,
        center_y,
        (-0.5 * LOG2E) * (yy / det),
        LOG2E * (xy / det),
        (-0.5 * LOG2E) * (xx / det),
        opacity,
        *entry[7:10],
    ]
    for p, factor in enumerate(factors):
        rows[p * TILES : (p + 1) * TILES, :] = factor
    rows[len(factors) * TILES :, :] = jnp.zeros((LANES - len(factors) * TILES, LANES), F32)
    turned = rows[...].T
    for p in range(9):
        for b in range(TILES):
            column = turned[:, p * TILES + b : p * TILES + b + 1]
            wide = jnp.broadcast_to(column, (SLAB, LANES))
            if p < 6:
                spread[p, b * SLAB : (b + 1) * SLAB, :] = wide
            else:
                shade_ref[p - 6, b * SLAB : (b + 1) * SLAB, :] = wide
    lane = iota((8, LANES), 1)
    pixel_x = (lane & 31).astype(F32) + 0.5
    pixel_y = (iota((8, LANES), 0) * 4 + (lane >> 5)).astype(F32) + 0.5

    def step(k, carry):
        out = []
        for b in range(TILES):
            trans, red, green, blue = carry[4 * b : 4 * b + 4]
            at = b * SLAB + k
            get = lambda ref, p: jnp.broadcast_to(ref[p, pl.ds(at, 1), :], (8, LANES))
            ex = pixel_x - get(spread, 0)
            ey = pixel_y - get(spread, 1)
            power = ex * (get(spread, 2) * ex + get(spread, 3) * ey) + get(spread, 4) * ey * ey
            alpha = get(spread, 5) * jnp.exp2(power)
            weight = alpha * trans
            alpha_ref[at] = alpha
            weight_ref[pl.ds(at, 8, stride=PITCH), :] = weight
            out += [
                trans - weight,
                red + weight * get(shade_ref, 0),
                green + weight * get(shade_ref, 1),
                blue + weight * get(shade_ref, 2),
            ]
        return tuple(out)

    one, zero = jnp.ones((8, LANES), F32), jnp.zeros((8, LANES), F32)
    out = lax.fori_loop(0, SLAB, step, (one, zero, zero, zero) * TILES, unroll=4)
    for q in range(4 * TILES):
        slab_ref[q * 8 : (q + 1) * 8, :] = out[q]


def backward_kernel(
    slabs_ref,
    alpha_ref,
    weight_ref,
    shade_ref,
    entry_ref,
    owner_ref,
    rank_ref,
    fixed_ref,
    image_ref,
    outgoing_ref,
    slope,
    moment,
    grads,
    placed,
    picture,
):
    depth = fixed_ref[HERE : HERE + 8, :]
    back = [fixed_ref[BACK + c * 8 : BACK + c * 8 + 8, :] for c in range(3)]
    seen, behind = [], []
    for b in range(TILES):
        part = lambda i, q: slabs_ref[i, (b * 4 + q) * 8 : (b * 4 + q + 1) * 8, :]
        trans = jnp.ones((8, LANES), F32)
        start = jnp.ones((8, LANES), F32)
        color = [jnp.zeros((8, LANES), F32)] * 3
        for i in range(DEPTHS):
            start = jnp.where(depth == i, trans, start)
            color = [color[c] + trans * part(i, 1 + c) for c in range(3)]
            trans = trans * part(i, 0)
        color = [color[c] + trans * back[c] for c in range(3)]
        miss = []
        for c in range(3):
            at = slice((c * TILES + b) * 8, (c * TILES + b + 1) * 8)
            miss.append(color[c] - fixed_ref[GOAL + at.start : GOAL + at.stop, :])
            picture[at, :] = color[c]
        after = sum(back[c] * miss[c] for c in range(3))
        for i in range(DEPTHS - 1, 0, -1):
            joined = sum(part(i, 1 + c) * miss[c] for c in range(3)) + part(i, 0) * after
            after = jnp.where(i > depth, joined, after)
        seen.append([start * miss[c] for c in range(3)])
        behind.append(start * after)
    for c in range(3):
        for s in range(8):
            image_ref[c, :, s * LANES : (s + 1) * LANES] = picture[
                pl.ds(c * TILES * 8 + s, TILES, stride=8), :
            ]

    def step(n, carry):
        k = SLAB - 1 - n
        out = []
        for b in range(TILES):
            at = b * SLAB + k
            get = lambda p: jnp.broadcast_to(shade_ref[p, pl.ds(at, 1), :], (8, LANES))
            shade = sum(get(c) * seen[b][c] for c in range(3))
            gap = shade - carry[b]
            rows = pl.ds(at, 8, stride=PITCH)
            slope[rows, :] = weight_ref[rows, :] * gap
            out.append(carry[b] + alpha_ref[at] * gap)
        return tuple(out)

    lax.fori_loop(0, SLAB, step, tuple(behind), unroll=4)

    index = iota((16, LANES), 0)
    lane = iota((16, LANES), 1)
    across = (lane & 31) - 16
    powers = []
    for s in range(8):
        down = s * 4 + (lane >> 5) - 16
        power = jnp.where(index == 0, 1, 0)
        for n, value in enumerate((across, down, across * across, across * down, down * down), 1):
            power = jnp.where(index == n, value, power)
        powers += [power.astype(F32).astype(BF16)] * 3
    powers = jnp.concatenate(powers, axis=1)
    for b in range(TILES):
        at = [slice(s * PITCH + b * SLAB, s * PITCH + (b + 1) * SLAB) for s in range(8)]
        field = jnp.concatenate([side_by_side(slope[at[s], :]) for s in range(8)], axis=1)
        moment[b * 32 : b * 32 + 16, :] = dot(powers, field, NT)
        gaze, weights = [], []
        for s in range(8):
            look = jnp.concatenate(
                [*pieces(jnp.concatenate([seen[b][c][s : s + 1, :] for c in range(3)], axis=0))][:2]
                + [jnp.zeros((10, LANES), BF16)],
                axis=0,
            )
            gaze += [look, look]
            weights += pieces(weight_ref[at[s], :])[:2]
        shades = dot(jnp.concatenate(gaze, axis=1), jnp.concatenate(weights, axis=1), NT)
        moment[b * 32 + 16 : (b + 1) * 32, :] = shades
    entry = [entry_ref[pl.ds(p, TILES, stride=16), :] for p in range(PARAMS)]
    jac = camera_rows(fixed_ref)
    m0, mx, my, mxx, mxy, myy = (moment[pl.ds(n, TILES, stride=32), :] for n in range(6))
    variance, xx, xy, yy, det = covariance(entry[3:6], jac)
    cx = sum(jac[0][j] * entry[j] for j in range(3)) + jac[0][3] - 0.5
    cy = sum(jac[1][j] * entry[j] for j in range(3)) + jac[1][3] - 0.5
    sx = mx - cx * m0
    sy = my - cy * m0
    sxx = mxx - cx * (mx + sx)
    sxy = mxy - cx * my - cy * sx
    syy = myy - cy * (my + sy)
    inverse = 1.0 / det
    conic = (yy * inverse, -xy * inverse, xx * inverse)
    d_cx = conic[0] * sx + conic[1] * sy
    d_cy = conic[1] * sx + conic[2] * sy
    d_a, d_b, d_c = -0.5 * sxx, -sxy, -0.5 * syy
    d_det = -(d_a * conic[0] + d_b * conic[1] + d_c * conic[2]) * inverse
    d_xx = d_c * inverse + d_det * yy
    d_yy = d_a * inverse + d_det * xx
    d_xy = -d_b * inverse - 2.0 * xy * d_det
    result = [jac[0][j] * d_cx + jac[1][j] * d_cy for j in range(3)]
    result += [
        2.0
        * variance[j]
        * (
            jac[0][j] * jac[0][j] * d_xx
            + jac[0][j] * jac[1][j] * d_xy
            + jac[1][j] * jac[1][j] * d_yy
        )
        for j in range(3)
    ]
    result += [m0 * (1.0 - jax.nn.sigmoid(entry[6]))]
    result += [
        moment[pl.ds(16 + c, TILES, stride=32), :] + moment[pl.ds(19 + c, TILES, stride=32), :]
        for c in range(3)
    ]
    for p, value in enumerate(result):
        grads[p * TILES : (p + 1) * TILES, :] = value
    placed[...] = jnp.zeros((LANES, LANES), F32)
    outgoing = jnp.zeros((LANES, LANES), F32)
    for b in range(TILES):
        mine = grads[pl.ds(b, PARAMS, stride=TILES), :]
        rank = rank_ref[b : b + 1, :]
        for r in range(SLOTS):
            placed[r * PARAMS : (r + 1) * PARAMS, :] = jnp.where(rank == r, mine, 0.0)
        named = onehot(owner_ref[b : b + 1, :], LANES).astype(BF16)
        named = jnp.concatenate([named, named, named], axis=1)
        outgoing = outgoing + dot(named, side_by_side(placed[...]), NT)
    outgoing_ref[...] = outgoing


def collect_kernel(asked_ref, incoming_ref, sums_ref, columns, turned):
    columns[...] = asked_ref[...].T
    turned[...] = incoming_ref[...].T
    total = jnp.zeros((BLOCKS * 16, LANES), F32)
    for r in range(SLOTS):
        row = columns[r : r + 1, :]
        pick = onehot(row & (LANES - 1), LANES).astype(BF16)
        block = row >> 7
        value = turned[r * PARAMS : r * PARAMS + 16, :]
        spread = jnp.concatenate(
            [jnp.where(block == a, value, 0.0) for a in range(BLOCKS)], axis=0
        )
        total = total + dot(
            side_by_side(spread), jnp.concatenate([pick, pick, pick], axis=1), NT
        )
    for a in range(BLOCKS):
        sums_ref[a * PARAMS : (a + 1) * PARAMS, :] = total[a * 16 : a * 16 + PARAMS]


def adam_kernel(sums_ref, params_ref, first_ref, second_ref, new_ref, new_first_ref, new_second_ref):
    for a in range(BLOCKS):
        at = slice(a * LANES, (a + 1) * LANES)
        gradient = sum(sums_ref[i, a * PARAMS : (a + 1) * PARAMS, :] for i in range(DEPTHS))
        first = 0.9 * first_ref[:, at] + 0.1 * gradient
        second = 0.999 * second_ref[:, at] + 0.001 * gradient * gradient
        step = first / (1.0 - 0.9**10) / (jnp.sqrt(second / (1.0 - 0.999**10)) + 1e-08)
        new_ref[:, at] = params_ref[:, at] - 0.05 * step
        new_first_ref[:, at] = first
        new_second_ref[:, at] = second


def call(kernel, outs, ins, scratch=()):
    return pl.pallas_call(
        kernel,
        out_shape=[jax.ShapeDtypeStruct(shape, dtype) for shape, dtype in outs],
        in_specs=ins,
        out_specs=[VMEM] * len(outs),
        scratch_shapes=list(scratch),
        compiler_params=pltpu.CompilerParams(vmem_limit_bytes=40 * 2**20),
    )


def exchanged(array):
    groups = [
        [zy * 4 + hi * 2 + (hi ^ g) for zy in range(LANES // 2) for hi in range(2)] for g in range(2)
    ]
    whole = lax.all_to_all(
        array.reshape(LANES, 1, LANES),
        (*TILE, DEPTH[0]),
        0,
        0,
        axis_index_groups=groups,
        tiled=True,
    )
    return whole.reshape(LANES, LANES)


def body(
    positions,
    log_scales,
    opacity_logits,
    colors,
    first_moment,
    second_moment,
    cameras,
    background,
    target,
    tile_view,
    tile_length,
    list_owner,
    list_row,
):
    square = (LANES, LANES)
    held = pltpu.VMEM(square, F32)
    asked_rows = pltpu.VMEM(square, I32)
    owner = list_owner.reshape(TILES, SLAB)
    wanted = list_row.reshape(TILES, SLAB)
    depth = lax.axis_index(DEPTH).astype(I32).reshape(1)
    params = jnp.concatenate([positions, log_scales, opacity_logits, colors], axis=0)
    few = ((TILES, SLAB), I32)
    request, rank, owner = call(
        request_kernel,
        [(square, I32), few, few],
        [HBM, HBM],
        [pltpu.VMEM(*few), pltpu.SemaphoreType.DMA((2,))],
    )(owner, wanted)
    asked = exchanged(request)
    fixed, table = call(
        fixed_kernel,
        [((FIXED, LANES), F32), ((BLOCKS * 16, 3 * LANES), BF16)],
        [SMEM] * 5 + [VMEM] * 2,
    )(
        tile_view,
        tile_length,
        cameras,
        depth,
        background,
        target.transpose(1, 0, 2),
        params,
    )
    (reply,) = call(reply_kernel, [(square, F32)], [VMEM, VMEM], [asked_rows, held])(asked, table)
    fetched = exchanged(reply)
    field = (TILES * SLAB, 8, LANES)
    tilted = (8 * PITCH, LANES)
    slab, alpha, weight, shade, entry = call(
        forward_kernel,
        [
            (square, F32),
            (field, F32),
            (tilted, F32),
            ((3, TILES * SLAB, LANES), F32),
            ((TILES * 16, LANES), F32),
        ],
        [VMEM] * 4,
        [held, held, pltpu.VMEM((6, TILES * SLAB, LANES), F32)],
    )(fetched, owner, rank, fixed)
    slabs = lax.all_gather(slab[None], DEPTH, axis=0, tiled=True)
    image, outgoing = call(
        backward_kernel,
        [((3, TILES, 1024), F32), (square, F32)],
        [VMEM] * 8,
        [
            pltpu.VMEM(tilted, F32),
            held,
            pltpu.VMEM((PARAMS * TILES, LANES), F32),
            held,
            pltpu.VMEM((3 * TILES * 8, LANES), F32),
        ],
    )(slabs, alpha, weight, shade, entry, owner, rank, fixed)
    incoming = exchanged(outgoing)
    (sums,) = call(
        collect_kernel,
        [((BLOCKS * PARAMS, LANES), F32)],
        [VMEM, VMEM],
        [asked_rows, held],
    )(asked, incoming)
    sums = lax.all_gather(sums[None], DEPTH, axis=0, tiled=True)
    updated = call(adam_kernel, [(params.shape, F32)] * 3, [VMEM] * 4)(
        sums, params, first_moment, second_moment
    )
    return (image.transpose(1, 0, 2), *updated)


def solution(mesh):
    torus = Mesh(mesh.devices.reshape(8, 8, 2, 2, 2), (*TILE, *DEPTH))
    split = P(None, TILE)
    placed = (
        *[split] * 6,
        P(),
        P(),
        P(TILE, None, None),
        P(TILE),
        P(TILE),
        P(DEPTH, TILE, None, None),
        P(DEPTH, TILE, None),
    )
    return jax.shard_map(
        body,
        mesh=torus,
        in_specs=placed,
        out_specs=(P(TILE, None, None), split, split, split),
        check_vma=False,
    )
```

```python
import math

import jax
import jax.numpy as jnp
from jax import lax
from jax.experimental import pallas as pl
from jax.experimental.pallas import tpu as pltpu
from jax.sharding import Mesh
from jax.sharding import PartitionSpec as P

LANES = 128
TILES = 4
SLAB = 128
DEPTHS = 4
SLOTS = 10
PARAMS = 10
BLOCKS = 16
GRANT_ALL = 60
LIVE, BACK, HERE, GOAL, FIXED = 32, 40, 64, 72, 168
PITCH = TILES * SLAB + 1
TILE = ("tile_z", "tile_y", "tile_x")
DEPTH = ("depth_x", "depth_core")
LOG2E = math.log2(math.e)
VMEM = pl.BlockSpec(memory_space=pltpu.VMEM)
SMEM = pl.BlockSpec(memory_space=pltpu.SMEM)
HBM = pl.BlockSpec(memory_space=pltpu.HBM)
F32 = jnp.float32
BF16 = jnp.bfloat16
I32 = jnp.int32
NT = (((1,), (1,)), ((), ()))
NN = (((1,), (0,)), ((), ()))


def iota(shape, dim):
    return lax.broadcasted_iota(I32, shape, dim)


def pieces(x):
    high = x.astype(BF16)
    rest = x - high.astype(F32)
    middle = rest.astype(BF16)
    low = (rest - middle.astype(F32)).astype(BF16)
    return high, middle, low


def side_by_side(x):
    return jnp.concatenate(pieces(x), axis=1)


def dot(a, b, dims):
    return lax.dot_general(a, b, dims, preferred_element_type=F32)


def onehot(index, rows):
    return jnp.where(iota((rows, LANES), 0) == index, 1.0, 0.0)


def request_kernel(owner_hbm, row_hbm, request_ref, rank_ref, owner_ref, row_ref, sems):
    copies = [
        pltpu.make_async_copy(owner_hbm, owner_ref, sems.at[0]),
        pltpu.make_async_copy(row_hbm, row_ref, sems.at[1]),
    ]
    for copy in copies:
        copy.start()
    for copy in copies:
        copy.wait()
    earlier = jnp.where(iota((SLAB, SLAB), 0) < iota((SLAB, SLAB), 1), 1.0, 0.0).astype(BF16)
    before = jnp.zeros((LANES, 1), F32)
    total = jnp.zeros((LANES, LANES), F32)
    for b in range(TILES):
        named = onehot(owner_ref[b : b + 1, :], LANES)
        named_16 = named.astype(BF16)
        count = dot(named_16, earlier, NN) + before
        before = before + jnp.sum(named, axis=1, keepdims=True)
        rank = jnp.sum(named * count, axis=0, keepdims=True).astype(I32)
        rank_ref[b : b + 1, :] = rank
        row = row_ref[b : b + 1, :]
        here = iota((LANES, SLAB), 0) == rank
        high = jnp.where(here, row >> 4, 0).astype(F32).astype(BF16)
        low = jnp.where(here, row & 15, 0).astype(F32).astype(BF16)
        total = total + 16.0 * dot(named_16, high, NT) + dot(named_16, low, NT)
    request_ref[...] = total.astype(I32)


def fixed_kernel(
    view_ref, length_ref, cams_ref, depth_ref, back_ref, target_ref, fixed_ref
):
    for i in range(2):
        for j in range(4):
            at = (i * 4 + j) * TILES
            fixed_ref[at : at + TILES, :] = per_tile([cams_ref[view_ref[b], i, j] for b in range(TILES)])
    place = depth_ref[0] * SLAB + iota((TILES, LANES), 1)
    length = per_tile([length_ref[b].astype(F32) for b in range(TILES)])
    fixed_ref[LIVE : LIVE + TILES, :] = jnp.where(place.astype(F32) < length, 1.0, 0.0)
    for c in range(3):
        fixed_ref[BACK + c * 8 : BACK + c * 8 + 8, :] = jnp.full((8, LANES), back_ref[c], F32)
    fixed_ref[HERE : HERE + 8, :] = jnp.full((8, LANES), depth_ref[0].astype(F32), F32)
    for c in range(3):
        for s in range(8):
            fixed_ref[pl.ds(GOAL + c * TILES * 8 + s, TILES, stride=8), :] = target_ref[
                c, :, s * LANES : (s + 1) * LANES
            ]

def table_kernel(side_ref, mine_ref, theirs_ref, table_ref):
    first = side_ref[0] == 0
    blank = jnp.zeros((16 - PARAMS, LANES), F32)
    for a in range(BLOCKS):
        mine = mine_ref[:, a * LANES : (a + 1) * LANES]
        theirs = theirs_ref[:, a * LANES : (a + 1) * LANES]
        for h in range(2):
            block = jnp.where(first, mine, theirs) if h == 0 else jnp.where(first, theirs, mine)
            table_ref[a * 16 : (a + 1) * 16, h * 384 : (h + 1) * 384] = side_by_side(
                jnp.concatenate([block, blank], axis=0)
            )


def reply_kernel(asked_ref, table_ref, reply_ref, columns, held):
    columns[...] = asked_ref[...].T
    table = table_ref[...]
    second = (iota((LANES, LANES), 1) & 1) == 1
    for r in range(SLOTS):
        row = columns[r : r + 1, :]
        pick = onehot(row & (LANES - 1), LANES)
        picks = [jnp.where(second, 0.0, pick).astype(BF16)] * 3
        picks += [jnp.where(second, pick, 0.0).astype(BF16)] * 3
        found = dot(table, jnp.concatenate(picks, axis=0), NN)
        block = row >> 7
        value = jnp.zeros((16, LANES), F32)
        for a in range(BLOCKS):
            value = value + jnp.where(block == a, found[a * 16 : (a + 1) * 16], 0.0)
        held[r * PARAMS : r * PARAMS + 16, :] = value
    held[SLOTS * PARAMS :, :] = jnp.zeros((LANES - SLOTS * PARAMS, LANES), F32)
    reply_ref[...] = held[...].T


def per_tile(values):
    place = iota((TILES, LANES), 0)
    out = jnp.full((TILES, LANES), values[0], F32)
    for b in range(1, TILES):
        out = jnp.where(place == b, values[b], out)
    return out


def camera_rows(fixed_ref):
    rows = [fixed_ref[n * TILES : (n + 1) * TILES, :] for n in range(8)]
    return rows[:4], rows[4:]


def covariance(scales, jac):
    variance = [jnp.exp(2.0 * s) for s in scales]
    xx = sum(jac[0][j] * jac[0][j] * variance[j] for j in range(3)) + 0.3
    xy = sum(jac[0][j] * jac[1][j] * variance[j] for j in range(3))
    yy = sum(jac[1][j] * jac[1][j] * variance[j] for j in range(3)) + 0.3
    return variance, xx, xy, yy, xx * yy - xy * xy


def forward_kernel(
    fetched_ref,
    owner_ref,
    rank_ref,
    fixed_ref,
    slab_ref,
    alpha_ref,
    weight_ref,
    shade_ref,
    entry_ref,
    found,
    rows,
    spread,
):
    fetched = side_by_side(fetched_ref[...].T)
    for b in range(TILES):
        named = onehot(owner_ref[b : b + 1, :], LANES).astype(BF16)
        found[...] = dot(fetched, jnp.concatenate([named, named, named], axis=0), NN)
        rank = rank_ref[b : b + 1, :]
        value = jnp.zeros((16, LANES), F32)
        for r in range(SLOTS):
            value = value + jnp.where(rank == r, found[r * PARAMS : r * PARAMS + 16, :], 0.0)
        entry_ref[b * 16 : (b + 1) * 16, :] = value
    entry = [entry_ref[pl.ds(p, TILES, stride=16), :] for p in range(PARAMS)]
    jac = camera_rows(fixed_ref)
    center_x = sum(jac[0][j] * entry[j] for j in range(3)) + jac[0][3] + 16.0
    center_y = sum(jac[1][j] * entry[j] for j in range(3)) + jac[1][3] + 16.0
    _, xx, xy, yy, det = covariance(entry[3:6], jac)
    opacity = jax.nn.sigmoid(entry[6]) * fixed_ref[LIVE : LIVE + TILES, :]
    factors = [
        center_x,
        center_y,
        (-0.5 * LOG2E) * (yy / det),
        LOG2E * (xy / det),
        (-0.5 * LOG2E) * (xx / det),
        opacity,
        *entry[7:10],
    ]
    for p, factor in enumerate(factors):
        rows[p * TILES : (p + 1) * TILES, :] = factor
    rows[len(factors) * TILES :, :] = jnp.zeros((LANES - len(factors) * TILES, LANES), F32)
    turned = rows[...].T
    for p in range(9):
        for b in range(TILES):
            column = turned[:, p * TILES + b : p * TILES + b + 1]
            wide = jnp.broadcast_to(column, (SLAB, LANES))
            if p < 6:
                spread[p, b * SLAB : (b + 1) * SLAB, :] = wide
            else:
                shade_ref[p - 6, b * SLAB : (b + 1) * SLAB, :] = wide
    lane = iota((8, LANES), 1)
    pixel_x = (lane & 31).astype(F32) + 0.5
    pixel_y = (iota((8, LANES), 0) * 4 + (lane >> 5)).astype(F32) + 0.5

    def step(k, carry):
        out = []
        for b in range(TILES):
            trans, red, green, blue = carry[4 * b : 4 * b + 4]
            at = b * SLAB + k
            get = lambda ref, p: jnp.broadcast_to(ref[p, pl.ds(at, 1), :], (8, LANES))
            ex = pixel_x - get(spread, 0)
            ey = pixel_y - get(spread, 1)
            power = ex * (get(spread, 2) * ex + get(spread, 3) * ey) + get(spread, 4) * ey * ey
            alpha = get(spread, 5) * jnp.exp2(power)
            weight = alpha * trans
            alpha_ref[at] = alpha
            weight_ref[pl.ds(at, 8, stride=PITCH), :] = weight
            out += [
                trans - weight,
                red + weight * get(shade_ref, 0),
                green + weight * get(shade_ref, 1),
                blue + weight * get(shade_ref, 2),
            ]
        return tuple(out)

    one, zero = jnp.ones((8, LANES), F32), jnp.zeros((8, LANES), F32)
    out = lax.fori_loop(0, SLAB, step, (one, zero, zero, zero) * TILES, unroll=4)
    for q in range(4 * TILES):
        slab_ref[q * 8 : (q + 1) * 8, :] = out[q]


def backward_kernel(
    slabs_ref,
    alpha_ref,
    weight_ref,
    shade_ref,
    entry_ref,
    owner_ref,
    rank_ref,
    row_ref,
    fixed_ref,
    image_ref,
    outgoing_ref,
    slope,
    moment,
    grads,
    placed,
    picture,
):
    depth = fixed_ref[HERE : HERE + 8, :]
    back = [fixed_ref[BACK + c * 8 : BACK + c * 8 + 8, :] for c in range(3)]
    seen, behind = [], []
    for b in range(TILES):
        part = lambda i, q: slabs_ref[i, (b * 4 + q) * 8 : (b * 4 + q + 1) * 8, :]
        trans = jnp.ones((8, LANES), F32)
        start = jnp.ones((8, LANES), F32)
        color = [jnp.zeros((8, LANES), F32)] * 3
        for i in range(DEPTHS):
            start = jnp.where(depth == i, trans, start)
            color = [color[c] + trans * part(i, 1 + c) for c in range(3)]
            trans = trans * part(i, 0)
        color = [color[c] + trans * back[c] for c in range(3)]
        miss = []
        for c in range(3):
            at = slice((c * TILES + b) * 8, (c * TILES + b + 1) * 8)
            miss.append(color[c] - fixed_ref[GOAL + at.start : GOAL + at.stop, :])
            picture[at, :] = color[c]
        after = sum(back[c] * miss[c] for c in range(3))
        for i in range(DEPTHS - 1, 0, -1):
            joined = sum(part(i, 1 + c) * miss[c] for c in range(3)) + part(i, 0) * after
            after = jnp.where(i > depth, joined, after)
        seen.append([start * miss[c] for c in range(3)])
        behind.append(start * after)
    for c in range(3):
        for s in range(8):
            image_ref[c, :, s * LANES : (s + 1) * LANES] = picture[
                pl.ds(c * TILES * 8 + s, TILES, stride=8), :
            ]

    def step(n, carry):
        k = SLAB - 1 - n
        out = []
        for b in range(TILES):
            at = b * SLAB + k
            get = lambda p: jnp.broadcast_to(shade_ref[p, pl.ds(at, 1), :], (8, LANES))
            shade = sum(get(c) * seen[b][c] for c in range(3))
            gap = shade - carry[b]
            rows = pl.ds(at, 8, stride=PITCH)
            slope[rows, :] = weight_ref[rows, :] * gap
            out.append(carry[b] + alpha_ref[at] * gap)
        return tuple(out)

    lax.fori_loop(0, SLAB, step, tuple(behind), unroll=4)

    index = iota((16, LANES), 0)
    lane = iota((16, LANES), 1)
    across = (lane & 31) - 16
    powers = []
    for s in range(8):
        down = s * 4 + (lane >> 5) - 16
        power = jnp.where(index == 0, 1, 0)
        for n, value in enumerate((across, down, across * across, across * down, down * down), 1):
            power = jnp.where(index == n, value, power)
        powers += [power.astype(F32).astype(BF16)] * 3
    powers = jnp.concatenate(powers, axis=1)
    for b in range(TILES):
        at = [slice(s * PITCH + b * SLAB, s * PITCH + (b + 1) * SLAB) for s in range(8)]
        field = jnp.concatenate([side_by_side(slope[at[s], :]) for s in range(8)], axis=1)
        moment[b * 32 : b * 32 + 16, :] = dot(powers, field, NT)
        gaze, weights = [], []
        for s in range(8):
            look = jnp.concatenate(
                [*pieces(jnp.concatenate([seen[b][c][s : s + 1, :] for c in range(3)], axis=0))][:2]
                + [jnp.zeros((10, LANES), BF16)],
                axis=0,
            )
            gaze += [look, look]
            weights += pieces(weight_ref[at[s], :])[:2]
        shades = dot(jnp.concatenate(gaze, axis=1), jnp.concatenate(weights, axis=1), NT)
        moment[b * 32 + 16 : (b + 1) * 32, :] = shades
    entry = [entry_ref[pl.ds(p, TILES, stride=16), :] for p in range(PARAMS)]
    jac = camera_rows(fixed_ref)
    m0, mx, my, mxx, mxy, myy = (moment[pl.ds(n, TILES, stride=32), :] for n in range(6))
    variance, xx, xy, yy, det = covariance(entry[3:6], jac)
    cx = sum(jac[0][j] * entry[j] for j in range(3)) + jac[0][3] - 0.5
    cy = sum(jac[1][j] * entry[j] for j in range(3)) + jac[1][3] - 0.5
    sx = mx - cx * m0
    sy = my - cy * m0
    sxx = mxx - cx * (mx + sx)
    sxy = mxy - cx * my - cy * sx
    syy = myy - cy * (my + sy)
    inverse = 1.0 / det
    conic = (yy * inverse, -xy * inverse, xx * inverse)
    d_cx = conic[0] * sx + conic[1] * sy
    d_cy = conic[1] * sx + conic[2] * sy
    d_a, d_b, d_c = -0.5 * sxx, -sxy, -0.5 * syy
    d_det = -(d_a * conic[0] + d_b * conic[1] + d_c * conic[2]) * inverse
    d_xx = d_c * inverse + d_det * yy
    d_yy = d_a * inverse + d_det * xx
    d_xy = -d_b * inverse - 2.0 * xy * d_det
    result = [jac[0][j] * d_cx + jac[1][j] * d_cy for j in range(3)]
    result += [
        2.0
        * variance[j]
        * (
            jac[0][j] * jac[0][j] * d_xx
            + jac[0][j] * jac[1][j] * d_xy
            + jac[1][j] * jac[1][j] * d_yy
        )
        for j in range(3)
    ]
    result += [m0 * (1.0 - jax.nn.sigmoid(entry[6]))]
    result += [
        moment[pl.ds(16 + c, TILES, stride=32), :] + moment[pl.ds(19 + c, TILES, stride=32), :]
        for c in range(3)
    ]
    for p, value in enumerate(result):
        grads[p * TILES : (p + 1) * TILES, :] = value
    placed[...] = jnp.zeros((LANES, LANES), F32)
    outgoing = jnp.zeros((LANES, LANES), F32)
    for b in range(TILES):
        mine = grads[pl.ds(b, PARAMS, stride=TILES), :]
        rank = rank_ref[b : b + 1, :]
        for r in range(SLOTS):
            placed[r * PARAMS : (r + 1) * PARAMS, :] = jnp.where(rank == r, mine, 0.0)
        here = iota((16, LANES), 0) == rank
        row = jnp.where(here, row_ref[b : b + 1, :].astype(F32), 0.0)
        placed[SLOTS * PARAMS : SLOTS * PARAMS + 16, :] = row
        named = onehot(owner_ref[b : b + 1, :], LANES).astype(BF16)
        named = jnp.concatenate([named, named, named], axis=1)
        outgoing = outgoing + dot(named, side_by_side(placed[...]), NT)
    outgoing_ref[...] = outgoing


def collect_kernel(incoming_ref, sums_ref, turned):
    turned[...] = incoming_ref[...].T
    total = jnp.zeros((BLOCKS * 16, LANES), F32)
    for r in range(SLOTS):
        row = turned[SLOTS * PARAMS + r : SLOTS * PARAMS + r + 1, :].astype(I32)
        pick = onehot(row & (LANES - 1), LANES).astype(BF16)
        block = row >> 7
        value = turned[r * PARAMS : r * PARAMS + 16, :]
        spread = jnp.concatenate(
            [jnp.where(block == a, value, 0.0) for a in range(BLOCKS)], axis=0
        )
        total = total + dot(
            side_by_side(spread), jnp.concatenate([pick, pick, pick], axis=1), NT
        )
    for a in range(BLOCKS):
        sums_ref[a * PARAMS : (a + 1) * PARAMS, :] = total[a * 16 : a * 16 + PARAMS]


def adam_kernel(sums_ref, params_ref, first_ref, second_ref, new_ref, new_first_ref, new_second_ref):
    for a in range(BLOCKS):
        at = slice(a * LANES, (a + 1) * LANES)
        gradient = sum(sums_ref[i, a * PARAMS : (a + 1) * PARAMS, :] for i in range(DEPTHS))
        first = 0.9 * first_ref[:, at] + 0.1 * gradient
        second = 0.999 * second_ref[:, at] + 0.001 * gradient * gradient
        step = first / (1.0 - 0.9**10) / (jnp.sqrt(second / (1.0 - 0.999**10)) + 1e-08)
        new_ref[:, at] = params_ref[:, at] - 0.05 * step
        new_first_ref[:, at] = first
        new_second_ref[:, at] = second


def call(kernel, outs, ins, scratch=(), grant=40):
    return pl.pallas_call(
        kernel,
        out_shape=[jax.ShapeDtypeStruct(shape, dtype) for shape, dtype in outs],
        in_specs=ins,
        out_specs=[VMEM] * len(outs),
        scratch_shapes=list(scratch),
        compiler_params=pltpu.CompilerParams(vmem_limit_bytes=grant * 2**20),
    )


def exchanged_in_plane(array):
    pairs = array.reshape(LANES // 2, 2, LANES)
    return lax.all_to_all(pairs, TILE[:2], 0, 0, tiled=True).reshape(LANES, LANES)


def exchanged(array):
    groups = [
        [zy * 4 + hi * 2 + (hi ^ g) for zy in range(LANES // 2) for hi in range(2)] for g in range(2)
    ]
    whole = lax.all_to_all(
        array.reshape(LANES, 1, LANES),
        (*TILE, DEPTH[0]),
        0,
        0,
        axis_index_groups=groups,
        tiled=True,
    )
    return whole.reshape(LANES, LANES)


def body(
    positions,
    log_scales,
    opacity_logits,
    colors,
    first_moment,
    second_moment,
    cameras,
    background,
    target,
    tile_view,
    tile_length,
    list_owner,
    list_row,
):
    square = (LANES, LANES)
    held = pltpu.VMEM(square, F32)
    asked_rows = pltpu.VMEM(square, I32)
    owner = list_owner.reshape(TILES, SLAB)
    wanted = list_row.reshape(TILES, SLAB)
    depth = lax.axis_index(DEPTH).astype(I32).reshape(1)
    params = jnp.concatenate([positions, log_scales, opacity_logits, colors], axis=0)
    few = ((TILES, SLAB), I32)
    request, rank, owner, wanted = call(
        request_kernel,
        [(square, I32), few, few, few],
        [HBM, HBM],
        [pltpu.SemaphoreType.DMA((2,))],
        GRANT_ALL,
    )(owner, wanted)
    asked = exchanged_in_plane(request)
    theirs = lax.ppermute(params, (TILE[2], DEPTH[0]), [(0, 3), (3, 0), (1, 2), (2, 1)])
    (fixed,) = call(fixed_kernel, [((FIXED, LANES), F32)], [SMEM] * 5 + [VMEM])(
        tile_view, tile_length, cameras, depth, background, target.transpose(1, 0, 2)
    )
    side = lax.axis_index(TILE[2]).astype(I32).reshape(1)
    (table,) = call(
        table_kernel, [((BLOCKS * 16, 6 * LANES), BF16)], [SMEM, VMEM, VMEM]
    )(side, params, theirs)
    (reply,) = call(reply_kernel, [(square, F32)], [VMEM, VMEM], [asked_rows, held])(asked, table)
    fetched = exchanged_in_plane(reply)
    field = (TILES * SLAB, 8, LANES)
    tilted = (8 * PITCH, LANES)
    slab, alpha, weight, shade, entry = call(
        forward_kernel,
        [
            (square, F32),
            (field, F32),
            (tilted, F32),
            ((3, TILES * SLAB, LANES), F32),
            ((TILES * 16, LANES), F32),
        ],
        [VMEM] * 4,
        [held, held, pltpu.VMEM((6, TILES * SLAB, LANES), F32)],
    )(fetched, owner, rank, fixed)
    slabs = lax.all_gather(slab[None], DEPTH, axis=0, tiled=True)
    image, outgoing = call(
        backward_kernel,
        [((3, TILES, 1024), F32), (square, F32)],
        [VMEM] * 9,
        [
            pltpu.VMEM(tilted, F32),
            held,
            pltpu.VMEM((PARAMS * TILES, LANES), F32),
            held,
            pltpu.VMEM((3 * TILES * 8, LANES), F32),
        ],
    )(slabs, alpha, weight, shade, entry, owner, rank, wanted, fixed)
    incoming = exchanged(outgoing)
    (sums,) = call(
        collect_kernel,
        [((BLOCKS * PARAMS, LANES), F32)],
        [VMEM],
        [held],
    )(incoming)
    sums = lax.all_gather(sums[None], DEPTH, axis=0, tiled=True)
    updated = call(adam_kernel, [(params.shape, F32)] * 3, [VMEM] * 4)(
        sums, params, first_moment, second_moment
    )
    return (image.transpose(1, 0, 2), *updated)


def solution(mesh):
    torus = Mesh(mesh.devices.reshape(8, 8, 2, 2, 2), (*TILE, *DEPTH))
    split = P(None, TILE)
    placed = (
        *[split] * 6,
        P(),
        P(),
        P(TILE, None, None),
        P(TILE),
        P(TILE),
        P(DEPTH, TILE, None, None),
        P(DEPTH, TILE, None),
    )
    return jax.shard_map(
        body,
        mesh=torus,
        in_specs=placed,
        out_specs=(P(TILE, None, None), split, split, split),
        check_vma=False,
    )
```

```python
import math

import jax
import jax.numpy as jnp
from jax import lax
from jax.experimental import pallas as pl
from jax.experimental.pallas import tpu as pltpu
from jax.sharding import Mesh
from jax.sharding import PartitionSpec as P

LANES = 128
TILES = 4
SLAB = 128
DEPTHS = 4
SLOTS = 10
PARAMS = 10
BLOCKS = 16
GRANT_ALL = 60
LIVE, BACK, HERE, GOAL, OWNER, FIXED = 32, 40, 64, 72, 168, 184
RANK, ROW = OWNER + TILES, OWNER + 2 * TILES
PITCH = TILES * SLAB + 1
TILE = ("tile_z", "tile_y", "tile_x")
DEPTH = ("depth_x", "depth_core")
LOG2E = math.log2(math.e)
VMEM = pl.BlockSpec(memory_space=pltpu.VMEM)
SMEM = pl.BlockSpec(memory_space=pltpu.SMEM)
HBM = pl.BlockSpec(memory_space=pltpu.HBM)
F32 = jnp.float32
BF16 = jnp.bfloat16
I32 = jnp.int32
NT = (((1,), (1,)), ((), ()))
NN = (((1,), (0,)), ((), ()))


def iota(shape, dim):
    return lax.broadcasted_iota(I32, shape, dim)


def pieces(x):
    high = x.astype(BF16)
    rest = x - high.astype(F32)
    middle = rest.astype(BF16)
    low = (rest - middle.astype(F32)).astype(BF16)
    return high, middle, low


def side_by_side(x):
    return jnp.concatenate(pieces(x), axis=1)


def dot(a, b, dims):
    return lax.dot_general(a, b, dims, preferred_element_type=F32)


def onehot(index, rows):
    return jnp.where(iota((rows, LANES), 0) == index, 1.0, 0.0)


def request_kernel(
    owner_hbm,
    row_hbm,
    position_hbm,
    scale_hbm,
    opacity_hbm,
    color_hbm,
    request_ref,
    list_ref,
    params_ref,
    owner_ref,
    row_ref,
    position,
    scale,
    opacity,
    color,
    sems,
):
    sources = (owner_hbm, row_hbm, position_hbm, scale_hbm, opacity_hbm, color_hbm)
    held = (owner_ref, row_ref, position, scale, opacity, color)
    copies = [
        pltpu.make_async_copy(source, there, sems.at[n])
        for n, (source, there) in enumerate(zip(sources, held))
    ]
    for copy in copies:
        copy.start()
    for copy in copies[:2]:
        copy.wait()
    earlier = jnp.where(iota((SLAB, SLAB), 0) < iota((SLAB, SLAB), 1), 1.0, 0.0).astype(BF16)
    before = jnp.zeros((LANES, 1), F32)
    total = jnp.zeros((LANES // 2, LANES), F32)
    for b in range(TILES):
        owner = owner_ref[b : b + 1, :]
        row = row_ref[b : b + 1, :]
        named = onehot(owner, LANES)
        count = dot(named.astype(BF16), earlier, NN) + before
        before = before + jnp.sum(named, axis=1, keepdims=True)
        rank = jnp.sum(named * count, axis=0, keepdims=True).astype(I32)
        here = iota((LANES, SLAB), 0) == (owner & 1) * 16 + rank
        high = jnp.where(here, row >> 4, 0).astype(F32).astype(BF16)
        low = jnp.where(here, row & 15, 0).astype(F32).astype(BF16)
        place = onehot(owner >> 1, LANES // 2).astype(BF16)
        total = total + 16.0 * dot(place, high, NT) + dot(place, low, NT)
        list_ref[b : b + 1, :] = owner
        list_ref[TILES + b : TILES + b + 1, :] = rank
        list_ref[2 * TILES + b : 2 * TILES + b + 1, :] = row
    list_ref[3 * TILES :, :] = jnp.zeros((TILES, LANES), I32)
    request_ref[...] = total.astype(I32)
    for copy in copies[2:]:
        copy.wait()
    for a in range(BLOCKS):
        at = slice(a * LANES, (a + 1) * LANES)
        params_ref[a * PARAMS : a * PARAMS + 3, :] = position[:, at]
        params_ref[a * PARAMS + 3 : a * PARAMS + 6, :] = scale[:, at]
        params_ref[a * PARAMS + 6 : a * PARAMS + 7, :] = opacity[:, at]
        params_ref[a * PARAMS + 7 : a * PARAMS + 10, :] = color[:, at]


def fixed_kernel(scalar_ref, target_ref, list_ref, fixed_ref):
    for i in range(2):
        for j in range(4):
            at = (i * 4 + j) * TILES
            fixed_ref[at : at + TILES, :] = per_tile(
                [scalar_ref[scalar_ref[b].astype(I32) * 8 + i * 4 + j + 12] for b in range(TILES)]
            )
    depth = scalar_ref[11]
    place = depth * SLAB + iota((TILES, LANES), 1).astype(F32)
    length = per_tile([scalar_ref[4 + b] for b in range(TILES)])
    fixed_ref[LIVE : LIVE + TILES, :] = jnp.where(place < length, 1.0, 0.0)
    for c in range(3):
        fixed_ref[BACK + c * 8 : BACK + c * 8 + 8, :] = jnp.full((8, LANES), scalar_ref[8 + c], F32)
    fixed_ref[HERE : HERE + 8, :] = jnp.full((8, LANES), depth, F32)
    for c in range(3):
        for s in range(8):
            fixed_ref[pl.ds(GOAL + c * TILES * 8 + s, TILES, stride=8), :] = target_ref[
                c, :, s * LANES : (s + 1) * LANES
            ]
    fixed_ref[OWNER : OWNER + 16, :] = list_ref[...].astype(F32)


def table_kernel(side_ref, mine_ref, theirs_ref, table_ref):
    first = side_ref[0] == 0
    blank = jnp.zeros((16 - PARAMS, LANES), F32)
    for a in range(BLOCKS):
        mine = mine_ref[a * PARAMS : (a + 1) * PARAMS, :]
        theirs = theirs_ref[a * PARAMS : (a + 1) * PARAMS, :]
        for h in range(2):
            block = jnp.where(first, mine, theirs) if h == 0 else jnp.where(first, theirs, mine)
            at = h * BLOCKS * 16 + a * 16
            table_ref[at : at + 16, :] = side_by_side(jnp.concatenate([block, blank], axis=0))


def reply_kernel(asked_ref, table_ref, reply_ref, columns, held):
    half = LANES // 2
    columns[...] = asked_ref[...].T
    for h in range(2):
        slots = columns[h * 16 : h * 16 + 16, :]
        rows = jnp.concatenate([slots[:5], slots[5:10]], axis=1)
        table = table_ref[h * BLOCKS * 16 : (h + 1) * BLOCKS * 16, :]
        for q in range(5):
            row = rows[q : q + 1, :]
            pick = onehot(row & (LANES - 1), LANES).astype(BF16)
            found = dot(table, jnp.concatenate([pick, pick, pick], axis=0), NN)
            block = row >> 7
            value = jnp.zeros((16, LANES), F32)
            for a in range(BLOCKS):
                value = value + jnp.where(block == a, found[a * 16 : (a + 1) * 16], 0.0)
            held[q * PARAMS : q * PARAMS + 16, :] = value
        held[5 * PARAMS :, :] = jnp.zeros((LANES - 5 * PARAMS, LANES), F32)
        turned = held[...].T
        reply_ref[:, h, :] = turned[:half] + pltpu.roll(turned[half:], 5 * PARAMS, 1)


def per_tile(values):
    place = iota((TILES, LANES), 0)
    out = jnp.full((TILES, LANES), values[0], F32)
    for b in range(1, TILES):
        out = jnp.where(place == b, values[b], out)
    return out


def camera_rows(fixed_ref):
    rows = [fixed_ref[n * TILES : (n + 1) * TILES, :] for n in range(8)]
    return rows[:4], rows[4:]


def listed(fixed_ref, at, b):
    return fixed_ref[at + b : at + b + 1, :].astype(I32)


def covariance(scales, jac):
    variance = [jnp.exp(2.0 * s) for s in scales]
    xx = sum(jac[0][j] * jac[0][j] * variance[j] for j in range(3)) + 0.3
    xy = sum(jac[0][j] * jac[1][j] * variance[j] for j in range(3))
    yy = sum(jac[1][j] * jac[1][j] * variance[j] for j in range(3)) + 0.3
    return variance, xx, xy, yy, xx * yy - xy * xy


def forward_kernel(
    fetched_ref,
    fixed_ref,
    slab_ref,
    alpha_ref,
    weight_ref,
    shade_ref,
    entry_ref,
    found,
    rows,
    spread,
):
    fetched = side_by_side(fetched_ref[...].T)
    for b in range(TILES):
        named = onehot(listed(fixed_ref, OWNER, b), LANES).astype(BF16)
        found[...] = dot(fetched, jnp.concatenate([named, named, named], axis=0), NN)
        rank = listed(fixed_ref, RANK, b)
        value = jnp.zeros((16, LANES), F32)
        for r in range(SLOTS):
            value = value + jnp.where(rank == r, found[r * PARAMS : r * PARAMS + 16, :], 0.0)
        entry_ref[b * 16 : (b + 1) * 16, :] = value
    entry = [entry_ref[pl.ds(p, TILES, stride=16), :] for p in range(PARAMS)]
    jac = camera_rows(fixed_ref)
    center_x = sum(jac[0][j] * entry[j] for j in range(3)) + jac[0][3] + 16.0
    center_y = sum(jac[1][j] * entry[j] for j in range(3)) + jac[1][3] + 16.0
    _, xx, xy, yy, det = covariance(entry[3:6], jac)
    opacity = jax.nn.sigmoid(entry[6]) * fixed_ref[LIVE : LIVE + TILES, :]
    factors = [
        center_x,
        center_y,
        (-0.5 * LOG2E) * (yy / det),
        LOG2E * (xy / det),
        (-0.5 * LOG2E) * (xx / det),
        opacity,
        *entry[7:10],
    ]
    for p, factor in enumerate(factors):
        rows[p * TILES : (p + 1) * TILES, :] = factor
    rows[len(factors) * TILES :, :] = jnp.zeros((LANES - len(factors) * TILES, LANES), F32)
    turned = rows[...].T
    for p in range(9):
        for b in range(TILES):
            column = turned[:, p * TILES + b : p * TILES + b + 1]
            wide = jnp.broadcast_to(column, (SLAB, LANES))
            if p < 6:
                spread[p, b * SLAB : (b + 1) * SLAB, :] = wide
            else:
                shade_ref[p - 6, b * SLAB : (b + 1) * SLAB, :] = wide
    lane = iota((8, LANES), 1)
    pixel_x = (lane & 31).astype(F32) + 0.5
    pixel_y = (iota((8, LANES), 0) * 4 + (lane >> 5)).astype(F32) + 0.5

    def step(k, carry):
        out = []
        for b in range(TILES):
            trans, red, green, blue = carry[4 * b : 4 * b + 4]
            at = b * SLAB + k
            get = lambda ref, p: jnp.broadcast_to(ref[p, pl.ds(at, 1), :], (8, LANES))
            ex = pixel_x - get(spread, 0)
            ey = pixel_y - get(spread, 1)
            power = ex * (get(spread, 2) * ex + get(spread, 3) * ey) + get(spread, 4) * ey * ey
            alpha = get(spread, 5) * jnp.exp2(power)
            weight = alpha * trans
            alpha_ref[at] = alpha
            weight_ref[pl.ds(at, 8, stride=PITCH), :] = weight
            out += [
                trans - weight,
                red + weight * get(shade_ref, 0),
                green + weight * get(shade_ref, 1),
                blue + weight * get(shade_ref, 2),
            ]
        return tuple(out)

    one, zero = jnp.ones((8, LANES), F32), jnp.zeros((8, LANES), F32)
    out = lax.fori_loop(0, SLAB, step, (one, zero, zero, zero) * TILES, unroll=4)
    for q in range(4 * TILES):
        slab_ref[q * 8 : (q + 1) * 8, :] = out[q]


def backward_kernel(
    slabs_ref,
    alpha_ref,
    weight_ref,
    shade_ref,
    entry_ref,
    fixed_ref,
    image_ref,
    outgoing_ref,
    slope,
    moment,
    grads,
    placed,
    picture,
):
    depth = fixed_ref[HERE : HERE + 8, :]
    back = [fixed_ref[BACK + c * 8 : BACK + c * 8 + 8, :] for c in range(3)]
    seen, behind = [], []
    for b in range(TILES):
        part = lambda i, q: slabs_ref[i, (b * 4 + q) * 8 : (b * 4 + q + 1) * 8, :]
        trans = jnp.ones((8, LANES), F32)
        start = jnp.ones((8, LANES), F32)
        color = [jnp.zeros((8, LANES), F32)] * 3
        for i in range(DEPTHS):
            start = jnp.where(depth == i, trans, start)
            color = [color[c] + trans * part(i, 1 + c) for c in range(3)]
            trans = trans * part(i, 0)
        color = [color[c] + trans * back[c] for c in range(3)]
        miss = []
        for c in range(3):
            at = slice((c * TILES + b) * 8, (c * TILES + b + 1) * 8)
            miss.append(color[c] - fixed_ref[GOAL + at.start : GOAL + at.stop, :])
            picture[at, :] = color[c]
        after = sum(back[c] * miss[c] for c in range(3))
        for i in range(DEPTHS - 1, 0, -1):
            joined = sum(part(i, 1 + c) * miss[c] for c in range(3)) + part(i, 0) * after
            after = jnp.where(i > depth, joined, after)
        seen.append([start * miss[c] for c in range(3)])
        behind.append(start * after)
    for c in range(3):
        for s in range(8):
            image_ref[c, :, s * LANES : (s + 1) * LANES] = picture[
                pl.ds(c * TILES * 8 + s, TILES, stride=8), :
            ]

    def step(n, carry):
        k = SLAB - 1 - n
        out = []
        for b in range(TILES):
            at = b * SLAB + k
            get = lambda p: jnp.broadcast_to(shade_ref[p, pl.ds(at, 1), :], (8, LANES))
            shade = sum(get(c) * seen[b][c] for c in range(3))
            gap = shade - carry[b]
            rows = pl.ds(at, 8, stride=PITCH)
            slope[rows, :] = weight_ref[rows, :] * gap
            out.append(carry[b] + alpha_ref[at] * gap)
        return tuple(out)

    lax.fori_loop(0, SLAB, step, tuple(behind), unroll=4)

    index = iota((16, LANES), 0)
    lane = iota((16, LANES), 1)
    across = (lane & 31) - 16
    powers = []
    for s in range(8):
        down = s * 4 + (lane >> 5) - 16
        power = jnp.where(index == 0, 1, 0)
        for n, value in enumerate((across, down, across * across, across * down, down * down), 1):
            power = jnp.where(index == n, value, power)
        powers += [power.astype(F32).astype(BF16)] * 3
    powers = jnp.concatenate(powers, axis=1)
    for b in range(TILES):
        at = [slice(s * PITCH + b * SLAB, s * PITCH + (b + 1) * SLAB) for s in range(8)]
        field = jnp.concatenate([side_by_side(slope[at[s], :]) for s in range(8)], axis=1)
        moment[b * 32 : b * 32 + 16, :] = dot(powers, field, NT)
        gaze, weights = [], []
        for s in range(8):
            look = jnp.concatenate(
                [*pieces(jnp.concatenate([seen[b][c][s : s + 1, :] for c in range(3)], axis=0))][:2]
                + [jnp.zeros((10, LANES), BF16)],
                axis=0,
            )
            gaze += [look, look]
            weights += pieces(weight_ref[at[s], :])[:2]
        shades = dot(jnp.concatenate(gaze, axis=1), jnp.concatenate(weights, axis=1), NT)
        moment[b * 32 + 16 : (b + 1) * 32, :] = shades
    entry = [entry_ref[pl.ds(p, TILES, stride=16), :] for p in range(PARAMS)]
    jac = camera_rows(fixed_ref)
    m0, mx, my, mxx, mxy, myy = (moment[pl.ds(n, TILES, stride=32), :] for n in range(6))
    variance, xx, xy, yy, det = covariance(entry[3:6], jac)
    cx = sum(jac[0][j] * entry[j] for j in range(3)) + jac[0][3] - 0.5
    cy = sum(jac[1][j] * entry[j] for j in range(3)) + jac[1][3] - 0.5
    sx = mx - cx * m0
    sy = my - cy * m0
    sxx = mxx - cx * (mx + sx)
    sxy = mxy - cx * my - cy * sx
    syy = myy - cy * (my + sy)
    inverse = 1.0 / det
    conic = (yy * inverse, -xy * inverse, xx * inverse)
    d_cx = conic[0] * sx + conic[1] * sy
    d_cy = conic[1] * sx + conic[2] * sy
    d_a, d_b, d_c = -0.5 * sxx, -sxy, -0.5 * syy
    d_det = -(d_a * conic[0] + d_b * conic[1] + d_c * conic[2]) * inverse
    d_xx = d_c * inverse + d_det * yy
    d_yy = d_a * inverse + d_det * xx
    d_xy = -d_b * inverse - 2.0 * xy * d_det
    result = [jac[0][j] * d_cx + jac[1][j] * d_cy for j in range(3)]
    result += [
        2.0
        * variance[j]
        * (
            jac[0][j] * jac[0][j] * d_xx
            + jac[0][j] * jac[1][j] * d_xy
            + jac[1][j] * jac[1][j] * d_yy
        )
        for j in range(3)
    ]
    result += [m0 * (1.0 - jax.nn.sigmoid(entry[6]))]
    result += [
        moment[pl.ds(16 + c, TILES, stride=32), :] + moment[pl.ds(19 + c, TILES, stride=32), :]
        for c in range(3)
    ]
    for p, value in enumerate(result):
        grads[p * TILES : (p + 1) * TILES, :] = value
    placed[...] = jnp.zeros((LANES, LANES), F32)
    outgoing = jnp.zeros((LANES, LANES), F32)
    for b in range(TILES):
        mine = grads[pl.ds(b, PARAMS, stride=TILES), :]
        rank = listed(fixed_ref, RANK, b)
        for r in range(SLOTS):
            placed[r * PARAMS : (r + 1) * PARAMS, :] = jnp.where(rank == r, mine, 0.0)
        here = iota((16, LANES), 0) == rank
        row = jnp.where(here, fixed_ref[ROW + b : ROW + b + 1, :], 0.0)
        placed[SLOTS * PARAMS : SLOTS * PARAMS + 16, :] = row
        named = onehot(listed(fixed_ref, OWNER, b), LANES).astype(BF16)
        named = jnp.concatenate([named, named, named], axis=1)
        outgoing = outgoing + dot(named, side_by_side(placed[...]), NT)
    outgoing_ref[...] = outgoing


def collect_kernel(incoming_ref, sums_ref, turned):
    turned[...] = incoming_ref[...].T
    total = jnp.zeros((BLOCKS * 16, LANES), F32)
    for r in range(SLOTS):
        row = turned[SLOTS * PARAMS + r : SLOTS * PARAMS + r + 1, :].astype(I32)
        pick = onehot(row & (LANES - 1), LANES).astype(BF16)
        block = row >> 7
        value = turned[r * PARAMS : r * PARAMS + 16, :]
        spread = jnp.concatenate(
            [jnp.where(block == a, value, 0.0) for a in range(BLOCKS)], axis=0
        )
        total = total + dot(
            side_by_side(spread), jnp.concatenate([pick, pick, pick], axis=1), NT
        )
    for a in range(BLOCKS):
        sums_ref[a * PARAMS : (a + 1) * PARAMS, :] = total[a * 16 : a * 16 + PARAMS]


def adam_kernel(sums_ref, params_ref, first_ref, second_ref, new_ref, new_first_ref, new_second_ref):
    for a in range(BLOCKS):
        at = slice(a * LANES, (a + 1) * LANES)
        gradient = sum(sums_ref[i, a * PARAMS : (a + 1) * PARAMS, :] for i in range(DEPTHS))
        first = 0.9 * first_ref[:, at] + 0.1 * gradient
        second = 0.999 * second_ref[:, at] + 0.001 * gradient * gradient
        step = first / (1.0 - 0.9**10) / (jnp.sqrt(second / (1.0 - 0.999**10)) + 1e-08)
        new_ref[:, at] = params_ref[a * PARAMS : (a + 1) * PARAMS, :] - 0.05 * step
        new_first_ref[:, at] = first
        new_second_ref[:, at] = second


def call(kernel, outs, ins, scratch=(), grant=40):
    return pl.pallas_call(
        kernel,
        out_shape=[jax.ShapeDtypeStruct(shape, dtype) for shape, dtype in outs],
        in_specs=ins,
        out_specs=[VMEM] * len(outs),
        scratch_shapes=list(scratch),
        compiler_params=pltpu.CompilerParams(vmem_limit_bytes=grant * 2**20),
    )


def exchanged_in_plane(array):
    return lax.all_to_all(array, TILE[:2], 0, 0, tiled=True)


def exchanged(array):
    groups = [
        [zy * 4 + hi * 2 + (hi ^ g) for zy in range(LANES // 2) for hi in range(2)] for g in range(2)
    ]
    whole = lax.all_to_all(
        array.reshape(LANES, 1, LANES),
        (*TILE, DEPTH[0]),
        0,
        0,
        axis_index_groups=groups,
        tiled=True,
    )
    return whole.reshape(LANES, LANES)


def body(
    positions,
    log_scales,
    opacity_logits,
    colors,
    first_moment,
    second_moment,
    cameras,
    background,
    target,
    tile_view,
    tile_length,
    list_owner,
    list_row,
):
    square = (LANES, LANES)
    held = pltpu.VMEM(square, F32)
    plane = LANES // 2
    flat = (BLOCKS * PARAMS, LANES)
    lists = (TILES, SLAB)
    sources = (
        list_owner.reshape(lists),
        list_row.reshape(lists),
        positions,
        log_scales,
        opacity_logits,
        colors,
    )
    request, listing, params = call(
        request_kernel,
        [((plane, LANES), I32), ((16, LANES), I32), (flat, F32)],
        [HBM] * 6,
        [pltpu.VMEM(a.shape, a.dtype) for a in sources] + [pltpu.SemaphoreType.DMA((6,))],
        GRANT_ALL,
    )(*sources)
    asked = exchanged_in_plane(request.reshape(plane, 1, LANES)).reshape(plane, LANES)
    theirs = lax.ppermute(params, (TILE[2], DEPTH[0]), [(0, 3), (3, 0), (1, 2), (2, 1)])
    side = lax.axis_index(TILE[2]).astype(I32).reshape(1)
    (table,) = call(
        table_kernel, [((2 * BLOCKS * 16, 3 * LANES), BF16)], [SMEM, VMEM, VMEM]
    )(side, params, theirs)
    (reply,) = call(
        reply_kernel,
        [((plane, 2, LANES), F32)],
        [VMEM, VMEM],
        [pltpu.VMEM((LANES, plane), I32), held],
    )(asked, table)
    fetched = exchanged_in_plane(reply).reshape(square)
    depth = lax.axis_index(DEPTH).astype(F32).reshape(1)
    scalars = jnp.concatenate(
        [tile_view.astype(F32), tile_length.astype(F32), background, depth, cameras.reshape(-1)]
    )
    (fixed,) = call(fixed_kernel, [((FIXED, LANES), F32)], [SMEM, VMEM, VMEM])(
        scalars, target.transpose(1, 0, 2), listing
    )
    field = (TILES * SLAB, 8, LANES)
    tilted = (8 * PITCH, LANES)
    slab, alpha, weight, shade, entry = call(
        forward_kernel,
        [
            (square, F32),
            (field, F32),
            (tilted, F32),
            ((3, TILES * SLAB, LANES), F32),
            ((TILES * 16, LANES), F32),
        ],
        [VMEM] * 2,
        [held, held, pltpu.VMEM((6, TILES * SLAB, LANES), F32)],
    )(fetched, fixed)
    slabs = lax.all_gather(slab[None], DEPTH, axis=0, tiled=True)
    image, outgoing = call(
        backward_kernel,
        [((3, TILES, 1024), F32), (square, F32)],
        [VMEM] * 6,
        [
            pltpu.VMEM(tilted, F32),
            held,
            pltpu.VMEM((PARAMS * TILES, LANES), F32),
            held,
            pltpu.VMEM((3 * TILES * 8, LANES), F32),
        ],
    )(slabs, alpha, weight, shade, entry, fixed)
    incoming = exchanged(outgoing)
    (sums,) = call(
        collect_kernel,
        [((BLOCKS * PARAMS, LANES), F32)],
        [VMEM],
        [held],
    )(incoming)
    sums = lax.all_gather(sums[None], DEPTH, axis=0, tiled=True)
    updated = call(adam_kernel, [(first_moment.shape, F32)] * 3, [VMEM] * 4)(
        sums, params, first_moment, second_moment
    )
    return (image.transpose(1, 0, 2), *updated)


def solution(mesh):
    torus = Mesh(mesh.devices.reshape(8, 8, 2, 2, 2), (*TILE, *DEPTH))
    split = P(None, TILE)
    placed = (
        *[split] * 6,
        P(),
        P(),
        P(TILE, None, None),
        P(TILE),
        P(TILE),
        P(DEPTH, TILE, None, None),
        P(DEPTH, TILE, None),
    )
    return jax.shard_map(
        body,
        mesh=torus,
        in_specs=placed,
        out_specs=(P(TILE, None, None), split, split, split),
        check_vma=False,
    )
```

```python
import math

import jax
import jax.numpy as jnp
from jax import lax
from jax.experimental import pallas as pl
from jax.experimental.pallas import tpu as pltpu
from jax.sharding import Mesh
from jax.sharding import PartitionSpec as P

LANES = 128
TILES = 4
SLAB = 128
DEPTHS = 4
SLOTS = 10
PARAMS = 10
BLOCKS = 16
GRANT_ALL = 60
LIVE, BACK, HERE, GOAL, OWNER, FIXED = 32, 40, 64, 72, 168, 184
RANK, ROW = OWNER + TILES, OWNER + 2 * TILES
PITCH = TILES * SLAB + 1
TILE = ("tile_z", "tile_y", "tile_x")
DEPTH = ("depth_x", "depth_core")
LOG2E = math.log2(math.e)
VMEM = pl.BlockSpec(memory_space=pltpu.VMEM)
SMEM = pl.BlockSpec(memory_space=pltpu.SMEM)
HBM = pl.BlockSpec(memory_space=pltpu.HBM)
F32 = jnp.float32
BF16 = jnp.bfloat16
I32 = jnp.int32
NT = (((1,), (1,)), ((), ()))
NN = (((1,), (0,)), ((), ()))


def iota(shape, dim):
    return lax.broadcasted_iota(I32, shape, dim)


def pieces(x):
    high = x.astype(BF16)
    rest = x - high.astype(F32)
    middle = rest.astype(BF16)
    low = (rest - middle.astype(F32)).astype(BF16)
    return high, middle, low


def side_by_side(x):
    return jnp.concatenate(pieces(x), axis=1)


def dot(a, b, dims):
    return lax.dot_general(a, b, dims, preferred_element_type=F32)


def onehot(index, rows):
    return jnp.where(iota((rows, LANES), 0) == index, 1.0, 0.0)


def fetch(sources, held, sems):
    copies = [
        pltpu.make_async_copy(source, there, sems.at[n])
        for n, (source, there) in enumerate(zip(sources, held))
    ]
    for copy in copies:
        copy.start()
    for copy in copies:
        copy.wait()


def request_kernel(owner_hbm, row_hbm, request_ref, list_ref, owner_ref, row_ref, sems):
    fetch((owner_hbm, row_hbm), (owner_ref, row_ref), sems)
    earlier = jnp.where(iota((SLAB, SLAB), 0) < iota((SLAB, SLAB), 1), 1.0, 0.0).astype(BF16)
    before = jnp.zeros((LANES, 1), F32)
    total = jnp.zeros((LANES // 2, LANES), F32)
    for b in range(TILES):
        owner = owner_ref[b : b + 1, :]
        row = row_ref[b : b + 1, :]
        named = onehot(owner, LANES)
        count = dot(named.astype(BF16), earlier, NN) + before
        before = before + jnp.sum(named, axis=1, keepdims=True)
        rank = jnp.sum(named * count, axis=0, keepdims=True).astype(I32)
        here = iota((LANES, SLAB), 0) == (owner & 1) * 16 + rank
        high = jnp.where(here, row >> 4, 0).astype(F32).astype(BF16)
        low = jnp.where(here, row & 15, 0).astype(F32).astype(BF16)
        place = onehot(owner >> 1, LANES // 2).astype(BF16)
        total = total + 16.0 * dot(place, high, NT) + dot(place, low, NT)
        list_ref[b : b + 1, :] = owner
        list_ref[TILES + b : TILES + b + 1, :] = rank
        list_ref[2 * TILES + b : 2 * TILES + b + 1, :] = row
    list_ref[3 * TILES :, :] = jnp.zeros((TILES, LANES), I32)
    request_ref[:, 0, :] = total.astype(I32)
    request_ref[:, 1, :] = jnp.zeros((LANES // 2, LANES), I32)


def layout_kernel(
    list_hbm,
    position_hbm,
    scale_hbm,
    opacity_hbm,
    color_hbm,
    params_ref,
    position,
    scale,
    opacity,
    color,
    sems,
):
    fetch(
        (position_hbm, scale_hbm, opacity_hbm, color_hbm), (position, scale, opacity, color), sems
    )
    for a in range(BLOCKS):
        at = slice(a * LANES, (a + 1) * LANES)
        params_ref[a * PARAMS : a * PARAMS + 3, :] = position[:, at]
        params_ref[a * PARAMS + 3 : a * PARAMS + 6, :] = scale[:, at]
        params_ref[a * PARAMS + 6 : a * PARAMS + 7, :] = opacity[:, at]
        params_ref[a * PARAMS + 7 : a * PARAMS + 10, :] = color[:, at]


def fixed_kernel(scalar_ref, target_ref, list_ref, fixed_ref):
    for i in range(2):
        for j in range(4):
            at = (i * 4 + j) * TILES
            fixed_ref[at : at + TILES, :] = per_tile(
                [scalar_ref[scalar_ref[b].astype(I32) * 8 + i * 4 + j + 12] for b in range(TILES)]
            )
    depth = scalar_ref[11]
    place = depth * SLAB + iota((TILES, LANES), 1).astype(F32)
    length = per_tile([scalar_ref[4 + b] for b in range(TILES)])
    fixed_ref[LIVE : LIVE + TILES, :] = jnp.where(place < length, 1.0, 0.0)
    for c in range(3):
        fixed_ref[BACK + c * 8 : BACK + c * 8 + 8, :] = jnp.full((8, LANES), scalar_ref[8 + c], F32)
    fixed_ref[HERE : HERE + 8, :] = jnp.full((8, LANES), depth, F32)
    for c in range(3):
        for s in range(8):
            fixed_ref[pl.ds(GOAL + c * TILES * 8 + s, TILES, stride=8), :] = target_ref[
                c, :, s * LANES : (s + 1) * LANES
            ]
    fixed_ref[OWNER : OWNER + 16, :] = list_ref[...].astype(F32)


def table_kernel(side_ref, mine_ref, theirs_ref, table_ref):
    first = side_ref[0] == 0
    blank = jnp.zeros((16 - PARAMS, LANES), F32)
    for a in range(BLOCKS):
        mine = mine_ref[a * PARAMS : (a + 1) * PARAMS, :]
        theirs = theirs_ref[a * PARAMS : (a + 1) * PARAMS, :]
        for h in range(2):
            block = jnp.where(first, mine, theirs) if h == 0 else jnp.where(first, theirs, mine)
            at = h * BLOCKS * 16 + a * 16
            table_ref[at : at + 16, :] = side_by_side(jnp.concatenate([block, blank], axis=0))


def reply_kernel(asked_ref, table_ref, reply_ref, columns, held):
    half = LANES // 2
    columns[...] = asked_ref[:, 0, :].T
    for h in range(2):
        slots = columns[h * 16 : h * 16 + 16, :]
        rows = jnp.concatenate([slots[:5], slots[5:10]], axis=1)
        table = table_ref[h * BLOCKS * 16 : (h + 1) * BLOCKS * 16, :]
        for q in range(5):
            row = rows[q : q + 1, :]
            pick = onehot(row & (LANES - 1), LANES).astype(BF16)
            found = dot(table, jnp.concatenate([pick, pick, pick], axis=0), NN)
            block = row >> 7
            value = jnp.zeros((16, LANES), F32)
            for a in range(BLOCKS):
                value = value + jnp.where(block == a, found[a * 16 : (a + 1) * 16], 0.0)
            held[q * PARAMS : q * PARAMS + 16, :] = value
        held[5 * PARAMS :, :] = jnp.zeros((LANES - 5 * PARAMS, LANES), F32)
        turned = held[...].T
        reply_ref[:, h, :] = turned[:half] + pltpu.roll(turned[half:], 5 * PARAMS, 1)


def per_tile(values):
    place = iota((TILES, LANES), 0)
    out = jnp.full((TILES, LANES), values[0], F32)
    for b in range(1, TILES):
        out = jnp.where(place == b, values[b], out)
    return out


def camera_rows(fixed_ref):
    rows = [fixed_ref[n * TILES : (n + 1) * TILES, :] for n in range(8)]
    return rows[:4], rows[4:]


def listed(fixed_ref, at, b):
    return fixed_ref[at + b : at + b + 1, :].astype(I32)


def covariance(scales, jac):
    variance = [jnp.exp(2.0 * s) for s in scales]
    xx = sum(jac[0][j] * jac[0][j] * variance[j] for j in range(3)) + 0.3
    xy = sum(jac[0][j] * jac[1][j] * variance[j] for j in range(3))
    yy = sum(jac[1][j] * jac[1][j] * variance[j] for j in range(3)) + 0.3
    return variance, xx, xy, yy, xx * yy - xy * xy


def forward_kernel(
    fetched_ref,
    fixed_ref,
    slab_ref,
    alpha_ref,
    weight_ref,
    shade_ref,
    entry_ref,
    found,
    rows,
    spread,
):
    fetched = side_by_side(fetched_ref[...].T)
    for b in range(TILES):
        named = onehot(listed(fixed_ref, OWNER, b), LANES).astype(BF16)
        found[...] = dot(fetched, jnp.concatenate([named, named, named], axis=0), NN)
        rank = listed(fixed_ref, RANK, b)
        value = jnp.zeros((16, LANES), F32)
        for r in range(SLOTS):
            value = value + jnp.where(rank == r, found[r * PARAMS : r * PARAMS + 16, :], 0.0)
        entry_ref[b * 16 : (b + 1) * 16, :] = value
    entry = [entry_ref[pl.ds(p, TILES, stride=16), :] for p in range(PARAMS)]
    jac = camera_rows(fixed_ref)
    center_x = sum(jac[0][j] * entry[j] for j in range(3)) + jac[0][3] + 16.0
    center_y = sum(jac[1][j] * entry[j] for j in range(3)) + jac[1][3] + 16.0
    _, xx, xy, yy, det = covariance(entry[3:6], jac)
    opacity = jax.nn.sigmoid(entry[6]) * fixed_ref[LIVE : LIVE + TILES, :]
    factors = [
        center_x,
        center_y,
        (-0.5 * LOG2E) * (yy / det),
        LOG2E * (xy / det),
        (-0.5 * LOG2E) * (xx / det),
        opacity,
        *entry[7:10],
    ]
    for p, factor in enumerate(factors):
        rows[p * TILES : (p + 1) * TILES, :] = factor
    rows[len(factors) * TILES :, :] = jnp.zeros((LANES - len(factors) * TILES, LANES), F32)
    turned = rows[...].T
    for p in range(9):
        for b in range(TILES):
            column = turned[:, p * TILES + b : p * TILES + b + 1]
            wide = jnp.broadcast_to(column, (SLAB, LANES))
            if p < 6:
                spread[p, b * SLAB : (b + 1) * SLAB, :] = wide
            else:
                shade_ref[p - 6, b * SLAB : (b + 1) * SLAB, :] = wide
    lane = iota((8, LANES), 1)
    pixel_x = (lane & 31).astype(F32) + 0.5
    pixel_y = (iota((8, LANES), 0) * 4 + (lane >> 5)).astype(F32) + 0.5

    def step(k, carry):
        out = []
        for b in range(TILES):
            trans, red, green, blue = carry[4 * b : 4 * b + 4]
            at = b * SLAB + k
            get = lambda ref, p: jnp.broadcast_to(ref[p, pl.ds(at, 1), :], (8, LANES))
            ex = pixel_x - get(spread, 0)
            ey = pixel_y - get(spread, 1)
            power = ex * (get(spread, 2) * ex + get(spread, 3) * ey) + get(spread, 4) * ey * ey
            alpha = get(spread, 5) * jnp.exp2(power)
            weight = alpha * trans
            alpha_ref[at] = alpha
            weight_ref[pl.ds(at, 8, stride=PITCH), :] = weight
            out += [
                trans - weight,
                red + weight * get(shade_ref, 0),
                green + weight * get(shade_ref, 1),
                blue + weight * get(shade_ref, 2),
            ]
        return tuple(out)

    one, zero = jnp.ones((8, LANES), F32), jnp.zeros((8, LANES), F32)
    out = lax.fori_loop(0, SLAB, step, (one, zero, zero, zero) * TILES, unroll=4)
    for q in range(4 * TILES):
        slab_ref[q * 8 : (q + 1) * 8, :] = out[q]


def backward_kernel(
    slabs_ref,
    alpha_ref,
    weight_ref,
    shade_ref,
    entry_ref,
    fixed_ref,
    image_ref,
    outgoing_ref,
    slope,
    moment,
    grads,
    placed,
    picture,
):
    depth = fixed_ref[HERE : HERE + 8, :]
    back = [fixed_ref[BACK + c * 8 : BACK + c * 8 + 8, :] for c in range(3)]
    seen, behind = [], []
    for b in range(TILES):
        part = lambda i, q: slabs_ref[i, (b * 4 + q) * 8 : (b * 4 + q + 1) * 8, :]
        trans = jnp.ones((8, LANES), F32)
        start = jnp.ones((8, LANES), F32)
        color = [jnp.zeros((8, LANES), F32)] * 3
        for i in range(DEPTHS):
            start = jnp.where(depth == i, trans, start)
            color = [color[c] + trans * part(i, 1 + c) for c in range(3)]
            trans = trans * part(i, 0)
        color = [color[c] + trans * back[c] for c in range(3)]
        miss = []
        for c in range(3):
            at = slice((c * TILES + b) * 8, (c * TILES + b + 1) * 8)
            miss.append(color[c] - fixed_ref[GOAL + at.start : GOAL + at.stop, :])
            picture[at, :] = color[c]
        after = sum(back[c] * miss[c] for c in range(3))
        for i in range(DEPTHS - 1, 0, -1):
            joined = sum(part(i, 1 + c) * miss[c] for c in range(3)) + part(i, 0) * after
            after = jnp.where(i > depth, joined, after)
        seen.append([start * miss[c] for c in range(3)])
        behind.append(start * after)
    for c in range(3):
        for s in range(8):
            image_ref[c, :, s * LANES : (s + 1) * LANES] = picture[
                pl.ds(c * TILES * 8 + s, TILES, stride=8), :
            ]

    def step(n, carry):
        k = SLAB - 1 - n
        out = []
        for b in range(TILES):
            at = b * SLAB + k
            get = lambda p: jnp.broadcast_to(shade_ref[p, pl.ds(at, 1), :], (8, LANES))
            shade = sum(get(c) * seen[b][c] for c in range(3))
            gap = shade - carry[b]
            rows = pl.ds(at, 8, stride=PITCH)
            slope[rows, :] = weight_ref[rows, :] * gap
            out.append(carry[b] + alpha_ref[at] * gap)
        return tuple(out)

    lax.fori_loop(0, SLAB, step, tuple(behind), unroll=4)

    index = iota((16, LANES), 0)
    lane = iota((16, LANES), 1)
    across = (lane & 31) - 16
    powers = []
    for s in range(8):
        down = s * 4 + (lane >> 5) - 16
        power = jnp.where(index == 0, 1, 0)
        for n, value in enumerate((across, down, across * across, across * down, down * down), 1):
            power = jnp.where(index == n, value, power)
        powers += [power.astype(F32).astype(BF16)] * 3
    powers = jnp.concatenate(powers, axis=1)
    for b in range(TILES):
        at = [slice(s * PITCH + b * SLAB, s * PITCH + (b + 1) * SLAB) for s in range(8)]
        field = jnp.concatenate([side_by_side(slope[at[s], :]) for s in range(8)], axis=1)
        moment[b * 32 : b * 32 + 16, :] = dot(powers, field, NT)
        gaze, weights = [], []
        for s in range(8):
            look = jnp.concatenate(
                [*pieces(jnp.concatenate([seen[b][c][s : s + 1, :] for c in range(3)], axis=0))][:2]
                + [jnp.zeros((10, LANES), BF16)],
                axis=0,
            )
            gaze += [look, look]
            weights += pieces(weight_ref[at[s], :])[:2]
        shades = dot(jnp.concatenate(gaze, axis=1), jnp.concatenate(weights, axis=1), NT)
        moment[b * 32 + 16 : (b + 1) * 32, :] = shades
    entry = [entry_ref[pl.ds(p, TILES, stride=16), :] for p in range(PARAMS)]
    jac = camera_rows(fixed_ref)
    m0, mx, my, mxx, mxy, myy = (moment[pl.ds(n, TILES, stride=32), :] for n in range(6))
    variance, xx, xy, yy, det = covariance(entry[3:6], jac)
    cx = sum(jac[0][j] * entry[j] for j in range(3)) + jac[0][3] - 0.5
    cy = sum(jac[1][j] * entry[j] for j in range(3)) + jac[1][3] - 0.5
    sx = mx - cx * m0
    sy = my - cy * m0
    sxx = mxx - cx * (mx + sx)
    sxy = mxy - cx * my - cy * sx
    syy = myy - cy * (my + sy)
    inverse = 1.0 / det
    conic = (yy * inverse, -xy * inverse, xx * inverse)
    d_cx = conic[0] * sx + conic[1] * sy
    d_cy = conic[1] * sx + conic[2] * sy
    d_a, d_b, d_c = -0.5 * sxx, -sxy, -0.5 * syy
    d_det = -(d_a * conic[0] + d_b * conic[1] + d_c * conic[2]) * inverse
    d_xx = d_c * inverse + d_det * yy
    d_yy = d_a * inverse + d_det * xx
    d_xy = -d_b * inverse - 2.0 * xy * d_det
    result = [jac[0][j] * d_cx + jac[1][j] * d_cy for j in range(3)]
    result += [
        2.0
        * variance[j]
        * (
            jac[0][j] * jac[0][j] * d_xx
            + jac[0][j] * jac[1][j] * d_xy
            + jac[1][j] * jac[1][j] * d_yy
        )
        for j in range(3)
    ]
    result += [m0 * (1.0 - jax.nn.sigmoid(entry[6]))]
    result += [
        moment[pl.ds(16 + c, TILES, stride=32), :] + moment[pl.ds(19 + c, TILES, stride=32), :]
        for c in range(3)
    ]
    for p, value in enumerate(result):
        grads[p * TILES : (p + 1) * TILES, :] = value
    placed[...] = jnp.zeros((LANES, LANES), F32)
    outgoing = jnp.zeros((LANES, LANES), F32)
    for b in range(TILES):
        mine = grads[pl.ds(b, PARAMS, stride=TILES), :]
        rank = listed(fixed_ref, RANK, b)
        for r in range(SLOTS):
            placed[r * PARAMS : (r + 1) * PARAMS, :] = jnp.where(rank == r, mine, 0.0)
        here = iota((16, LANES), 0) == rank
        row = jnp.where(here, fixed_ref[ROW + b : ROW + b + 1, :], 0.0)
        placed[SLOTS * PARAMS : SLOTS * PARAMS + 16, :] = row
        named = onehot(listed(fixed_ref, OWNER, b), LANES).astype(BF16)
        named = jnp.concatenate([named, named, named], axis=1)
        outgoing = outgoing + dot(named, side_by_side(placed[...]), NT)
    outgoing_ref[...] = outgoing


def collect_kernel(incoming_ref, sums_ref, turned):
    turned[...] = incoming_ref[...].T
    total = jnp.zeros((BLOCKS * 16, LANES), F32)
    for r in range(SLOTS):
        row = turned[SLOTS * PARAMS + r : SLOTS * PARAMS + r + 1, :].astype(I32)
        pick = onehot(row & (LANES - 1), LANES).astype(BF16)
        block = row >> 7
        value = turned[r * PARAMS : r * PARAMS + 16, :]
        spread = jnp.concatenate(
            [jnp.where(block == a, value, 0.0) for a in range(BLOCKS)], axis=0
        )
        total = total + dot(
            side_by_side(spread), jnp.concatenate([pick, pick, pick], axis=1), NT
        )
    for a in range(BLOCKS):
        sums_ref[a * PARAMS : (a + 1) * PARAMS, :] = total[a * 16 : a * 16 + PARAMS]


def adam_kernel(sums_ref, params_ref, first_ref, second_ref, new_ref, new_first_ref, new_second_ref):
    for a in range(BLOCKS):
        at = slice(a * LANES, (a + 1) * LANES)
        gradient = sum(sums_ref[i, a * PARAMS : (a + 1) * PARAMS, :] for i in range(DEPTHS))
        first = 0.9 * first_ref[:, at] + 0.1 * gradient
        second = 0.999 * second_ref[:, at] + 0.001 * gradient * gradient
        step = first / (1.0 - 0.9**10) / (jnp.sqrt(second / (1.0 - 0.999**10)) + 1e-08)
        new_ref[:, at] = params_ref[a * PARAMS : (a + 1) * PARAMS, :] - 0.05 * step
        new_first_ref[:, at] = first
        new_second_ref[:, at] = second


def call(kernel, outs, ins, scratch=(), grant=40):
    return pl.pallas_call(
        kernel,
        out_shape=[jax.ShapeDtypeStruct(shape, dtype) for shape, dtype in outs],
        in_specs=ins,
        out_specs=[VMEM] * len(outs),
        scratch_shapes=list(scratch),
        compiler_params=pltpu.CompilerParams(vmem_limit_bytes=grant * 2**20),
    )


def exchanged_in_plane(array):
    return lax.all_to_all(array, TILE[:2], 0, 0, tiled=True)


def exchanged(array):
    groups = [
        [zy * 4 + hi * 2 + (hi ^ g) for zy in range(LANES // 2) for hi in range(2)] for g in range(2)
    ]
    whole = lax.all_to_all(
        array.reshape(LANES, 1, LANES),
        (*TILE, DEPTH[0]),
        0,
        0,
        axis_index_groups=groups,
        tiled=True,
    )
    return whole.reshape(LANES, LANES)


def body(
    positions,
    log_scales,
    opacity_logits,
    colors,
    first_moment,
    second_moment,
    cameras,
    background,
    target,
    tile_view,
    tile_length,
    list_owner,
    list_row,
):
    square = (LANES, LANES)
    held = pltpu.VMEM(square, F32)
    plane = LANES // 2
    flat = (BLOCKS * PARAMS, LANES)
    lists = (TILES, SLAB)
    named = (list_owner.reshape(lists), list_row.reshape(lists))
    request, listing = call(
        request_kernel,
        [((plane, 2, LANES), I32), ((16, LANES), I32)],
        [HBM] * 2,
        [pltpu.VMEM(lists, I32)] * 2 + [pltpu.SemaphoreType.DMA((2,))],
        GRANT_ALL,
    )(*named)
    asked = exchanged_in_plane(request)
    groups = (positions, log_scales, opacity_logits, colors)
    (params,) = call(
        layout_kernel,
        [(flat, F32)],
        [HBM] * 5,
        [pltpu.VMEM(a.shape, F32) for a in groups] + [pltpu.SemaphoreType.DMA((4,))],
        GRANT_ALL,
    )(listing, *groups)
    theirs = lax.ppermute(params, (TILE[2], DEPTH[0]), [(0, 3), (3, 0), (1, 2), (2, 1)])
    side = lax.axis_index(TILE[2]).astype(I32).reshape(1)
    (table,) = call(
        table_kernel, [((2 * BLOCKS * 16, 3 * LANES), BF16)], [SMEM, VMEM, VMEM]
    )(side, params, theirs)
    (reply,) = call(
        reply_kernel,
        [((plane, 2, LANES), F32)],
        [VMEM, VMEM],
        [pltpu.VMEM((LANES, plane), I32), held],
    )(asked, table)
    fetched = exchanged_in_plane(reply).reshape(square)
    depth = lax.axis_index(DEPTH).astype(F32).reshape(1)
    scalars = jnp.concatenate(
        [tile_view.astype(F32), tile_length.astype(F32), background, depth, cameras.reshape(-1)]
    )
    (fixed,) = call(fixed_kernel, [((FIXED, LANES), F32)], [SMEM, VMEM, VMEM])(
        scalars, target.transpose(1, 0, 2), listing
    )
    field = (TILES * SLAB, 8, LANES)
    tilted = (8 * PITCH, LANES)
    slab, alpha, weight, shade, entry = call(
        forward_kernel,
        [
            (square, F32),
            (field, F32),
            (tilted, F32),
            ((3, TILES * SLAB, LANES), F32),
            ((TILES * 16, LANES), F32),
        ],
        [VMEM] * 2,
        [held, held, pltpu.VMEM((6, TILES * SLAB, LANES), F32)],
    )(fetched, fixed)
    slabs = lax.all_gather(slab[None], DEPTH, axis=0, tiled=True)
    image, outgoing = call(
        backward_kernel,
        [((3, TILES, 1024), F32), (square, F32)],
        [VMEM] * 6,
        [
            pltpu.VMEM(tilted, F32),
            held,
            pltpu.VMEM((PARAMS * TILES, LANES), F32),
            held,
            pltpu.VMEM((3 * TILES * 8, LANES), F32),
        ],
    )(slabs, alpha, weight, shade, entry, fixed)
    incoming = exchanged(outgoing)
    (sums,) = call(
        collect_kernel,
        [((BLOCKS * PARAMS, LANES), F32)],
        [VMEM],
        [held],
    )(incoming)
    sums = lax.all_gather(sums[None], DEPTH, axis=0, tiled=True)
    updated = call(adam_kernel, [(first_moment.shape, F32)] * 3, [VMEM] * 4)(
        sums, params, first_moment, second_moment
    )
    return (image.transpose(1, 0, 2), *updated)


def solution(mesh):
    torus = Mesh(mesh.devices.reshape(8, 8, 2, 2, 2), (*TILE, *DEPTH))
    split = P(None, TILE)
    placed = (
        *[split] * 6,
        P(),
        P(),
        P(TILE, None, None),
        P(TILE),
        P(TILE),
        P(DEPTH, TILE, None, None),
        P(DEPTH, TILE, None),
    )
    return jax.shard_map(
        body,
        mesh=torus,
        in_specs=placed,
        out_specs=(P(TILE, None, None), split, split, split),
        check_vma=False,
    )
```

```python
import math

import jax
import jax.numpy as jnp
from jax import lax
from jax.experimental import pallas as pl
from jax.experimental.pallas import tpu as pltpu
from jax.sharding import Mesh
from jax.sharding import PartitionSpec as P

LANES = 128
TILES = 4
SLAB = 128
DEPTHS = 4
SLOTS = 10
PARAMS = 10
BLOCKS = 16
GRANT_ALL = 60
LIVE, BACK, HERE, GOAL, OWNER, FIXED = 32, 40, 64, 72, 168, 184
RANK, ROW = OWNER + TILES, OWNER + 2 * TILES
PITCH = TILES * SLAB + 1
TILE = ("tile_z", "tile_y", "tile_x")
DEPTH = ("depth_x", "depth_core")
LOG2E = math.log2(math.e)
VMEM = pl.BlockSpec(memory_space=pltpu.VMEM)
SMEM = pl.BlockSpec(memory_space=pltpu.SMEM)
HBM = pl.BlockSpec(memory_space=pltpu.HBM)
F32 = jnp.float32
BF16 = jnp.bfloat16
I32 = jnp.int32
NT = (((1,), (1,)), ((), ()))
NN = (((1,), (0,)), ((), ()))


def iota(shape, dim):
    return lax.broadcasted_iota(I32, shape, dim)


def pieces(x):
    high = x.astype(BF16)
    rest = x - high.astype(F32)
    middle = rest.astype(BF16)
    low = (rest - middle.astype(F32)).astype(BF16)
    return high, middle, low


def side_by_side(x):
    return jnp.concatenate(pieces(x), axis=1)


def dot(a, b, dims):
    return lax.dot_general(a, b, dims, preferred_element_type=F32)


def onehot(index, rows):
    return jnp.where(iota((rows, LANES), 0) == index, 1.0, 0.0)


def request_kernel(
    owner_hbm,
    row_hbm,
    position_hbm,
    scale_hbm,
    opacity_hbm,
    color_hbm,
    request_hbm,
    list_hbm,
    params_hbm,
    owner_ref,
    row_ref,
    position,
    scale,
    opacity,
    color,
    request_ref,
    list_ref,
    params_ref,
    sems,
):
    sources = (owner_hbm, row_hbm, position_hbm, scale_hbm, opacity_hbm, color_hbm)
    held = (owner_ref, row_ref, position, scale, opacity, color)
    copies = [
        pltpu.make_async_copy(source, there, sems.at[n])
        for n, (source, there) in enumerate(zip(sources, held))
    ]
    for copy in copies:
        copy.start()
    for copy in copies[2:]:
        copy.wait()
    for a in range(BLOCKS):
        at = slice(a * LANES, (a + 1) * LANES)
        params_ref[a * PARAMS : a * PARAMS + 3, :] = position[:, at]
        params_ref[a * PARAMS + 3 : a * PARAMS + 6, :] = scale[:, at]
        params_ref[a * PARAMS + 6 : a * PARAMS + 7, :] = opacity[:, at]
        params_ref[a * PARAMS + 7 : a * PARAMS + 10, :] = color[:, at]
    results = [
        pltpu.make_async_copy(params_ref, params_hbm, sems.at[6]),
        pltpu.make_async_copy(request_ref, request_hbm, sems.at[7]),
        pltpu.make_async_copy(list_ref, list_hbm, sems.at[8]),
    ]
    results[0].start()
    for copy in copies[:2]:
        copy.wait()
    earlier = jnp.where(iota((SLAB, SLAB), 0) < iota((SLAB, SLAB), 1), 1.0, 0.0).astype(BF16)
    before = jnp.zeros((LANES, 1), F32)
    total = jnp.zeros((LANES // 2, LANES), F32)
    for b in range(TILES):
        owner = owner_ref[b : b + 1, :]
        row = row_ref[b : b + 1, :]
        named = onehot(owner, LANES)
        count = dot(named.astype(BF16), earlier, NN) + before
        before = before + jnp.sum(named, axis=1, keepdims=True)
        rank = jnp.sum(named * count, axis=0, keepdims=True).astype(I32)
        here = iota((LANES, SLAB), 0) == (owner & 1) * 16 + rank
        high = jnp.where(here, row >> 4, 0).astype(F32).astype(BF16)
        low = jnp.where(here, row & 15, 0).astype(F32).astype(BF16)
        place = onehot(owner >> 1, LANES // 2).astype(BF16)
        total = total + 16.0 * dot(place, high, NT) + dot(place, low, NT)
        list_ref[b : b + 1, :] = owner
        list_ref[TILES + b : TILES + b + 1, :] = rank
        list_ref[2 * TILES + b : 2 * TILES + b + 1, :] = row
    list_ref[3 * TILES :, :] = jnp.zeros((TILES, LANES), I32)
    request_ref[...] = total.astype(I32)
    for result in results[1:]:
        result.start()
    for result in results:
        result.wait()


def fixed_kernel(scalar_ref, target_ref, list_ref, fixed_ref):
    for i in range(2):
        for j in range(4):
            at = (i * 4 + j) * TILES
            fixed_ref[at : at + TILES, :] = per_tile(
                [scalar_ref[scalar_ref[b].astype(I32) * 8 + i * 4 + j + 12] for b in range(TILES)]
            )
    depth = scalar_ref[11]
    place = depth * SLAB + iota((TILES, LANES), 1).astype(F32)
    length = per_tile([scalar_ref[4 + b] for b in range(TILES)])
    fixed_ref[LIVE : LIVE + TILES, :] = jnp.where(place < length, 1.0, 0.0)
    for c in range(3):
        fixed_ref[BACK + c * 8 : BACK + c * 8 + 8, :] = jnp.full((8, LANES), scalar_ref[8 + c], F32)
    fixed_ref[HERE : HERE + 8, :] = jnp.full((8, LANES), depth, F32)
    for c in range(3):
        for s in range(8):
            fixed_ref[pl.ds(GOAL + c * TILES * 8 + s, TILES, stride=8), :] = target_ref[
                c, :, s * LANES : (s + 1) * LANES
            ]
    fixed_ref[OWNER : OWNER + 16, :] = list_ref[...].astype(F32)


def table_kernel(side_ref, mine_ref, theirs_ref, table_ref):
    first = side_ref[0] == 0
    blank = jnp.zeros((16 - PARAMS, LANES), F32)
    for a in range(BLOCKS):
        mine = mine_ref[a * PARAMS : (a + 1) * PARAMS, :]
        theirs = theirs_ref[a * PARAMS : (a + 1) * PARAMS, :]
        for h in range(2):
            block = jnp.where(first, mine, theirs) if h == 0 else jnp.where(first, theirs, mine)
            at = h * BLOCKS * 16 + a * 16
            table_ref[at : at + 16, :] = side_by_side(jnp.concatenate([block, blank], axis=0))


def reply_kernel(asked_ref, table_ref, reply_ref, columns, held):
    half = LANES // 2
    columns[...] = asked_ref[...].T
    for h in range(2):
        slots = columns[h * 16 : h * 16 + 16, :]
        rows = jnp.concatenate([slots[:5], slots[5:10]], axis=1)
        table = table_ref[h * BLOCKS * 16 : (h + 1) * BLOCKS * 16, :]
        for q in range(5):
            row = rows[q : q + 1, :]
            pick = onehot(row & (LANES - 1), LANES).astype(BF16)
            found = dot(table, jnp.concatenate([pick, pick, pick], axis=0), NN)
            block = row >> 7
            value = jnp.zeros((16, LANES), F32)
            for a in range(BLOCKS):
                value = value + jnp.where(block == a, found[a * 16 : (a + 1) * 16], 0.0)
            held[q * PARAMS : q * PARAMS + 16, :] = value
        held[5 * PARAMS :, :] = jnp.zeros((LANES - 5 * PARAMS, LANES), F32)
        turned = held[...].T
        reply_ref[:, h, :] = turned[:half] + pltpu.roll(turned[half:], 5 * PARAMS, 1)


def per_tile(values):
    place = iota((TILES, LANES), 0)
    out = jnp.full((TILES, LANES), values[0], F32)
    for b in range(1, TILES):
        out = jnp.where(place == b, values[b], out)
    return out


def camera_rows(fixed_ref):
    rows = [fixed_ref[n * TILES : (n + 1) * TILES, :] for n in range(8)]
    return rows[:4], rows[4:]


def listed(fixed_ref, at, b):
    return fixed_ref[at + b : at + b + 1, :].astype(I32)


def covariance(scales, jac):
    variance = [jnp.exp(2.0 * s) for s in scales]
    xx = sum(jac[0][j] * jac[0][j] * variance[j] for j in range(3)) + 0.3
    xy = sum(jac[0][j] * jac[1][j] * variance[j] for j in range(3))
    yy = sum(jac[1][j] * jac[1][j] * variance[j] for j in range(3)) + 0.3
    return variance, xx, xy, yy, xx * yy - xy * xy


def forward_kernel(
    fetched_ref,
    fixed_ref,
    slab_ref,
    alpha_ref,
    weight_ref,
    shade_ref,
    entry_ref,
    found,
    rows,
    spread,
):
    fetched = side_by_side(fetched_ref[...].T)
    for b in range(TILES):
        named = onehot(listed(fixed_ref, OWNER, b), LANES).astype(BF16)
        found[...] = dot(fetched, jnp.concatenate([named, named, named], axis=0), NN)
        rank = listed(fixed_ref, RANK, b)
        value = jnp.zeros((16, LANES), F32)
        for r in range(SLOTS):
            value = value + jnp.where(rank == r, found[r * PARAMS : r * PARAMS + 16, :], 0.0)
        entry_ref[b * 16 : (b + 1) * 16, :] = value
    entry = [entry_ref[pl.ds(p, TILES, stride=16), :] for p in range(PARAMS)]
    jac = camera_rows(fixed_ref)
    center_x = sum(jac[0][j] * entry[j] for j in range(3)) + jac[0][3] + 16.0
    center_y = sum(jac[1][j] * entry[j] for j in range(3)) + jac[1][3] + 16.0
    _, xx, xy, yy, det = covariance(entry[3:6], jac)
    opacity = jax.nn.sigmoid(entry[6]) * fixed_ref[LIVE : LIVE + TILES, :]
    factors = [
        center_x,
        center_y,
        (-0.5 * LOG2E) * (yy / det),
        LOG2E * (xy / det),
        (-0.5 * LOG2E) * (xx / det),
        opacity,
        *entry[7:10],
    ]
    for p, factor in enumerate(factors):
        rows[p * TILES : (p + 1) * TILES, :] = factor
    rows[len(factors) * TILES :, :] = jnp.zeros((LANES - len(factors) * TILES, LANES), F32)
    turned = rows[...].T
    for p in range(9):
        for b in range(TILES):
            column = turned[:, p * TILES + b : p * TILES + b + 1]
            wide = jnp.broadcast_to(column, (SLAB, LANES))
            if p < 6:
                spread[p, b * SLAB : (b + 1) * SLAB, :] = wide
            else:
                shade_ref[p - 6, b * SLAB : (b + 1) * SLAB, :] = wide
    lane = iota((8, LANES), 1)
    pixel_x = (lane & 31).astype(F32) + 0.5
    pixel_y = (iota((8, LANES), 0) * 4 + (lane >> 5)).astype(F32) + 0.5

    def step(k, carry):
        out = []
        for b in range(TILES):
            trans, red, green, blue = carry[4 * b : 4 * b + 4]
            at = b * SLAB + k
            get = lambda ref, p: ref[p, pl.ds(at, 8, stride=0), :]
            ex = pixel_x - get(spread, 0)
            ey = pixel_y - get(spread, 1)
            power = ex * (get(spread, 2) * ex + get(spread, 3) * ey) + get(spread, 4) * ey * ey
            alpha = get(spread, 5) * jnp.exp2(power)
            weight = alpha * trans
            alpha_ref[at] = alpha
            weight_ref[pl.ds(at, 8, stride=PITCH), :] = weight
            out += [
                trans - weight,
                red + weight * get(shade_ref, 0),
                green + weight * get(shade_ref, 1),
                blue + weight * get(shade_ref, 2),
            ]
        return tuple(out)

    one, zero = jnp.ones((8, LANES), F32), jnp.zeros((8, LANES), F32)
    out = lax.fori_loop(0, SLAB, step, (one, zero, zero, zero) * TILES, unroll=32)
    for q in range(4 * TILES):
        slab_ref[q * 8 : (q + 1) * 8, :] = out[q]


def row_sums(rows):
    a = rows[0]
    b = a + rows[1]
    c = b + rows[2]
    d = c + rows[3]
    e = rows[7]
    f = e + rows[6]
    g = f + rows[5]
    return d + g + rows[4], e + f + g - (a + b + c + d), 7.0 * a + 5.0 * (b + e) + 3.0 * (c + f) + (d + g)


def backward_kernel(
    slabs_ref,
    alpha_ref,
    weight_ref,
    shade_ref,
    entry_ref,
    fixed_ref,
    image_hbm,
    outgoing_ref,
    slope,
    moment,
    grads,
    placed,
    picture,
    image_ref,
    sem,
):
    depth = fixed_ref[HERE : HERE + 8, :]
    back = [fixed_ref[BACK + c * 8 : BACK + c * 8 + 8, :] for c in range(3)]
    seen, behind = [], []
    for b in range(TILES):
        part = lambda i, q: slabs_ref[i, (b * 4 + q) * 8 : (b * 4 + q + 1) * 8, :]
        trans = jnp.ones((8, LANES), F32)
        start = jnp.ones((8, LANES), F32)
        color = [jnp.zeros((8, LANES), F32)] * 3
        for i in range(DEPTHS):
            start = jnp.where(depth == i, trans, start)
            color = [color[c] + trans * part(i, 1 + c) for c in range(3)]
            trans = trans * part(i, 0)
        color = [color[c] + trans * back[c] for c in range(3)]
        miss = []
        for c in range(3):
            at = slice((c * TILES + b) * 8, (c * TILES + b + 1) * 8)
            miss.append(color[c] - fixed_ref[GOAL + at.start : GOAL + at.stop, :])
            picture[at, :] = color[c]
        after = sum(back[c] * miss[c] for c in range(3))
        for i in range(DEPTHS - 1, 0, -1):
            joined = sum(part(i, 1 + c) * miss[c] for c in range(3)) + part(i, 0) * after
            after = jnp.where(i > depth, joined, after)
        seen.append([start * miss[c] for c in range(3)])
        behind.append(start * after)
    for c in range(3):
        for s in range(8):
            image_ref[c, :, s * LANES : (s + 1) * LANES] = picture[
                pl.ds(c * TILES * 8 + s, TILES, stride=8), :
            ]
    shown = pltpu.make_async_copy(image_ref, image_hbm, sem)
    shown.start()

    def step(n, carry):
        k = SLAB - 1 - n
        out = []
        for b in range(TILES):
            at = b * SLAB + k
            get = lambda p: shade_ref[p, pl.ds(at, 8, stride=0), :]
            shade = sum(get(c) * seen[b][c] for c in range(3))
            gap = shade - carry[b]
            rows = pl.ds(at, 8, stride=PITCH)
            slope[rows, :] = weight_ref[rows, :] * gap
            out.append(carry[b] + alpha_ref[at] * gap)
        return tuple(out)

    lax.fori_loop(0, SLAB, step, tuple(behind), unroll=8)

    index = iota((16, LANES), 0)
    lane = iota((16, LANES), 1)
    across, down = (lane & 31) - 16, lane >> 5
    powers = []
    for rows in (
        (1, across, down, across * across, across * down, down * down),
        (0, 0, 4, 0, 4 * across, 8 * down),
        (0, 0, 0, 0, 0, 16),
    ):
        power = jnp.zeros((16, LANES), I32)
        for n, value in enumerate(rows):
            power = jnp.where(index == n, value, power)
        powers += [power.astype(F32).astype(BF16)] * 3
    powers = jnp.concatenate(powers, axis=1)
    for b in range(TILES):
        at = [slice(s * PITCH + b * SLAB, s * PITCH + (b + 1) * SLAB) for s in range(8)]
        field = jnp.concatenate(
            [side_by_side(part) for part in row_sums([slope[at[s], :] for s in range(8)])], axis=1
        )
        moment[b * 32 : b * 32 + 16, :] = dot(powers, field, NT)
        gaze, weights = [], []
        for s in range(8):
            look = jnp.concatenate(
                [*pieces(jnp.concatenate([seen[b][c][s : s + 1, :] for c in range(3)], axis=0))][:2]
                + [jnp.zeros((10, LANES), BF16)],
                axis=0,
            )
            gaze += [look, look]
            weights += pieces(weight_ref[at[s], :])[:2]
        shades = dot(jnp.concatenate(gaze, axis=1), jnp.concatenate(weights, axis=1), NT)
        moment[b * 32 + 16 : (b + 1) * 32, :] = shades
    entry = [entry_ref[pl.ds(p, TILES, stride=16), :] for p in range(PARAMS)]
    jac = camera_rows(fixed_ref)
    m0, mx, my, mxx, mxy, myy = (moment[pl.ds(n, TILES, stride=32), :] for n in range(6))
    variance, xx, xy, yy, det = covariance(entry[3:6], jac)
    cx = sum(jac[0][j] * entry[j] for j in range(3)) + jac[0][3] - 0.5
    cy = sum(jac[1][j] * entry[j] for j in range(3)) + jac[1][3] - 0.5
    sx = mx - cx * m0
    sy = my - cy * m0
    sxx = mxx - cx * (mx + sx)
    sxy = mxy - cx * my - cy * sx
    syy = myy - cy * (my + sy)
    inverse = 1.0 / det
    conic = (yy * inverse, -xy * inverse, xx * inverse)
    d_cx = conic[0] * sx + conic[1] * sy
    d_cy = conic[1] * sx + conic[2] * sy
    d_a, d_b, d_c = -0.5 * sxx, -sxy, -0.5 * syy
    d_det = -(d_a * conic[0] + d_b * conic[1] + d_c * conic[2]) * inverse
    d_xx = d_c * inverse + d_det * yy
    d_yy = d_a * inverse + d_det * xx
    d_xy = -d_b * inverse - 2.0 * xy * d_det
    result = [jac[0][j] * d_cx + jac[1][j] * d_cy for j in range(3)]
    result += [
        2.0
        * variance[j]
        * (
            jac[0][j] * jac[0][j] * d_xx
            + jac[0][j] * jac[1][j] * d_xy
            + jac[1][j] * jac[1][j] * d_yy
        )
        for j in range(3)
    ]
    result += [m0 * (1.0 - jax.nn.sigmoid(entry[6]))]
    result += [
        moment[pl.ds(16 + c, TILES, stride=32), :] + moment[pl.ds(19 + c, TILES, stride=32), :]
        for c in range(3)
    ]
    for p, value in enumerate(result):
        grads[p * TILES : (p + 1) * TILES, :] = value
    placed[...] = jnp.zeros((LANES, LANES), F32)
    outgoing = jnp.zeros((LANES, LANES), F32)
    for b in range(TILES):
        mine = grads[pl.ds(b, PARAMS, stride=TILES), :]
        rank = listed(fixed_ref, RANK, b)
        for r in range(SLOTS):
            placed[r * PARAMS : (r + 1) * PARAMS, :] = jnp.where(rank == r, mine, 0.0)
        here = iota((16, LANES), 0) == rank
        row = jnp.where(here, fixed_ref[ROW + b : ROW + b + 1, :], 0.0)
        placed[SLOTS * PARAMS : SLOTS * PARAMS + 16, :] = row
        named = onehot(listed(fixed_ref, OWNER, b), LANES).astype(BF16)
        named = jnp.concatenate([named, named, named], axis=1)
        outgoing = outgoing + dot(named, side_by_side(placed[...]), NT)
    outgoing_ref[...] = outgoing
    shown.wait()


def collect_kernel(incoming_ref, sums_ref, turned):
    turned[...] = incoming_ref[...].T
    total = jnp.zeros((BLOCKS * 16, LANES), F32)
    for r in range(SLOTS):
        row = turned[SLOTS * PARAMS + r : SLOTS * PARAMS + r + 1, :].astype(I32)
        pick = onehot(row & (LANES - 1), LANES).astype(BF16)
        block = row >> 7
        value = turned[r * PARAMS : r * PARAMS + 16, :]
        spread = jnp.concatenate(
            [jnp.where(block == a, value, 0.0) for a in range(BLOCKS)], axis=0
        )
        total = total + dot(
            side_by_side(spread), jnp.concatenate([pick, pick, pick], axis=1), NT
        )
    for a in range(BLOCKS):
        sums_ref[a * PARAMS : (a + 1) * PARAMS, :] = total[a * 16 : a * 16 + PARAMS]


def adam_kernel(sums_ref, params_ref, first_ref, second_ref, new_ref, new_first_ref, new_second_ref):
    for a in range(BLOCKS):
        at = slice(a * LANES, (a + 1) * LANES)
        gradient = sum(sums_ref[i, a * PARAMS : (a + 1) * PARAMS, :] for i in range(DEPTHS))
        first = 0.9 * first_ref[:, at] + 0.1 * gradient
        second = 0.999 * second_ref[:, at] + 0.001 * gradient * gradient
        step = first / (1.0 - 0.9**10) / (jnp.sqrt(second / (1.0 - 0.999**10)) + 1e-08)
        new_ref[:, at] = params_ref[a * PARAMS : (a + 1) * PARAMS, :] - 0.05 * step
        new_first_ref[:, at] = first
        new_second_ref[:, at] = second


def call(kernel, outs, ins, scratch=(), grant=40, to=None):
    return pl.pallas_call(
        kernel,
        out_shape=[jax.ShapeDtypeStruct(shape, dtype) for shape, dtype in outs],
        in_specs=ins,
        out_specs=to or [VMEM] * len(outs),
        scratch_shapes=list(scratch),
        compiler_params=pltpu.CompilerParams(vmem_limit_bytes=grant * 2**20),
    )


def exchanged_in_plane(array):
    return lax.all_to_all(array, TILE[:2], 0, 0, tiled=True)


def exchanged(array):
    groups = [
        [zy * 4 + hi * 2 + (hi ^ g) for zy in range(LANES // 2) for hi in range(2)] for g in range(2)
    ]
    whole = lax.all_to_all(
        array.reshape(LANES, 1, LANES),
        (*TILE, DEPTH[0]),
        0,
        0,
        axis_index_groups=groups,
        tiled=True,
    )
    return whole.reshape(LANES, LANES)


def body(
    positions,
    log_scales,
    opacity_logits,
    colors,
    first_moment,
    second_moment,
    cameras,
    background,
    target,
    tile_view,
    tile_length,
    list_owner,
    list_row,
):
    square = (LANES, LANES)
    held = pltpu.VMEM(square, F32)
    plane = LANES // 2
    flat = (BLOCKS * PARAMS, LANES)
    lists = (TILES, SLAB)
    sources = (
        list_owner.reshape(lists),
        list_row.reshape(lists),
        positions,
        log_scales,
        opacity_logits,
        colors,
    )
    results = [((plane, LANES), I32), ((16, LANES), I32), (flat, F32)]
    request, listing, params = call(
        request_kernel,
        results,
        [HBM] * 6,
        [pltpu.VMEM(a.shape, a.dtype) for a in sources]
        + [pltpu.VMEM(*result) for result in results]
        + [pltpu.SemaphoreType.DMA((9,))],
        GRANT_ALL,
        [HBM] * 3,
    )(*sources)
    asked = exchanged_in_plane(request.reshape(plane, 1, LANES)).reshape(plane, LANES)
    theirs = lax.ppermute(params, (TILE[2], DEPTH[0]), [(0, 3), (3, 0), (1, 2), (2, 1)])
    side = lax.axis_index(TILE[2]).astype(I32).reshape(1)
    (table,) = call(
        table_kernel, [((2 * BLOCKS * 16, 3 * LANES), BF16)], [SMEM, VMEM, VMEM]
    )(side, params, theirs)
    (reply,) = call(
        reply_kernel,
        [((plane, 2, LANES), F32)],
        [VMEM, VMEM],
        [pltpu.VMEM((LANES, plane), I32), held],
    )(asked, table)
    fetched = exchanged_in_plane(reply).reshape(square)
    depth = lax.axis_index(DEPTH).astype(F32).reshape(1)
    scalars = jnp.concatenate(
        [tile_view.astype(F32), tile_length.astype(F32), background, depth, cameras.reshape(-1)]
    )
    (fixed,) = call(fixed_kernel, [((FIXED, LANES), F32)], [SMEM, VMEM, VMEM])(
        scalars, target.transpose(1, 0, 2), listing
    )
    field = (TILES * SLAB, 8, LANES)
    tilted = (8 * PITCH, LANES)
    slab, alpha, weight, shade, entry = call(
        forward_kernel,
        [
            (square, F32),
            (field, F32),
            (tilted, F32),
            ((3, TILES * SLAB + 8, LANES), F32),
            ((TILES * 16, LANES), F32),
        ],
        [VMEM] * 2,
        [held, held, pltpu.VMEM((6, TILES * SLAB + 8, LANES), F32)],
    )(fetched, fixed)
    slabs = lax.all_gather(slab[None], DEPTH, axis=0, tiled=True)
    image, outgoing = call(
        backward_kernel,
        [((3, TILES, 1024), F32), (square, F32)],
        [VMEM] * 6,
        [
            pltpu.VMEM(tilted, F32),
            held,
            pltpu.VMEM((PARAMS * TILES, LANES), F32),
            held,
            pltpu.VMEM((3 * TILES * 8, LANES), F32),
            pltpu.VMEM((3, TILES, 1024), F32),
            pltpu.SemaphoreType.DMA(()),
        ],
        to=[HBM, VMEM],
    )(slabs, alpha, weight, shade, entry, fixed)
    incoming = exchanged(outgoing)
    (sums,) = call(
        collect_kernel,
        [((BLOCKS * PARAMS, LANES), F32)],
        [VMEM],
        [held],
    )(incoming)
    sums = lax.all_gather(sums[None], DEPTH, axis=0, tiled=True)
    updated = call(adam_kernel, [(first_moment.shape, F32)] * 3, [VMEM] * 4)(
        sums, params, first_moment, second_moment
    )
    return (image.transpose(1, 0, 2), *updated)


def solution(mesh):
    torus = Mesh(mesh.devices.reshape(8, 8, 2, 2, 2), (*TILE, *DEPTH))
    split = P(None, TILE)
    placed = (
        *[split] * 6,
        P(),
        P(),
        P(TILE, None, None),
        P(TILE),
        P(TILE),
        P(DEPTH, TILE, None, None),
        P(DEPTH, TILE, None),
    )
    return jax.shard_map(
        body,
        mesh=torus,
        in_specs=placed,
        out_specs=(P(TILE, None, None), split, split, split),
        check_vma=False,
    )
```

```python
import math

import jax
import jax.numpy as jnp
from jax import lax
from jax.experimental import pallas as pl
from jax.experimental.pallas import tpu as pltpu
from jax.sharding import Mesh
from jax.sharding import PartitionSpec as P

LANES = 128
TILES = 4
SLAB = 128
DEPTHS = 4
SLOTS = 10
PARAMS = 10
BLOCKS = 16
GRANT_ALL = 60
LIVE, BACK, HERE, GOAL, OWNER, FIXED = 32, 40, 64, 72, 168, 184
RANK, ROW = OWNER + TILES, OWNER + 2 * TILES
PITCH = TILES * SLAB + 1
TILE = ("tile_z", "tile_y", "tile_x")
DEPTH = ("depth_x", "depth_core")
LOG2E = math.log2(math.e)
VMEM = pl.BlockSpec(memory_space=pltpu.VMEM)
SMEM = pl.BlockSpec(memory_space=pltpu.SMEM)
HBM = pl.BlockSpec(memory_space=pltpu.HBM)
F32 = jnp.float32
BF16 = jnp.bfloat16
I32 = jnp.int32
NT = (((1,), (1,)), ((), ()))
NN = (((1,), (0,)), ((), ()))


def iota(shape, dim):
    return lax.broadcasted_iota(I32, shape, dim)


def pieces(x):
    high = x.astype(BF16)
    rest = x - high.astype(F32)
    middle = rest.astype(BF16)
    low = (rest - middle.astype(F32)).astype(BF16)
    return high, middle, low


def side_by_side(x):
    return jnp.concatenate(pieces(x), axis=1)


def dot(a, b, dims):
    return lax.dot_general(a, b, dims, preferred_element_type=F32)


def onehot(index, rows):
    return jnp.where(iota((rows, LANES), 0) == index, 1.0, 0.0)


def request_kernel(
    owner_hbm,
    row_hbm,
    position_hbm,
    scale_hbm,
    opacity_hbm,
    color_hbm,
    request_ref,
    list_ref,
    params_ref,
    owner_ref,
    row_ref,
    position,
    scale,
    opacity,
    color,
    sems,
):
    sources = (owner_hbm, row_hbm, position_hbm, scale_hbm, opacity_hbm, color_hbm)
    held = (owner_ref, row_ref, position, scale, opacity, color)
    copies = [
        pltpu.make_async_copy(source, there, sems.at[n])
        for n, (source, there) in enumerate(zip(sources, held))
    ]
    for copy in copies:
        copy.start()
    for copy in copies[:2]:
        copy.wait()
    earlier = jnp.where(iota((SLAB, SLAB), 0) < iota((SLAB, SLAB), 1), 1.0, 0.0).astype(BF16)
    before = jnp.zeros((LANES, 1), F32)
    total = jnp.zeros((LANES // 2, LANES), F32)
    for b in range(TILES):
        owner = owner_ref[b : b + 1, :]
        row = row_ref[b : b + 1, :]
        named = onehot(owner, LANES)
        count = dot(named.astype(BF16), earlier, NN) + before
        before = before + jnp.sum(named, axis=1, keepdims=True)
        rank = jnp.sum(named * count, axis=0, keepdims=True).astype(I32)
        here = iota((LANES, SLAB), 0) == (owner & 1) * 16 + rank
        high = jnp.where(here, row >> 4, 0).astype(F32).astype(BF16)
        low = jnp.where(here, row & 15, 0).astype(F32).astype(BF16)
        place = onehot(owner >> 1, LANES // 2).astype(BF16)
        total = total + 16.0 * dot(place, high, NT) + dot(place, low, NT)
        list_ref[b : b + 1, :] = owner
        list_ref[TILES + b : TILES + b + 1, :] = rank
        list_ref[2 * TILES + b : 2 * TILES + b + 1, :] = row
    list_ref[3 * TILES :, :] = jnp.zeros((TILES, LANES), I32)
    request_ref[...] = total.astype(I32)
    for copy in copies[2:]:
        copy.wait()
    for a in range(BLOCKS):
        at = slice(a * LANES, (a + 1) * LANES)
        params_ref[a * PARAMS : a * PARAMS + 3, :] = position[:, at]
        params_ref[a * PARAMS + 3 : a * PARAMS + 6, :] = scale[:, at]
        params_ref[a * PARAMS + 6 : a * PARAMS + 7, :] = opacity[:, at]
        params_ref[a * PARAMS + 7 : a * PARAMS + 10, :] = color[:, at]


def fixed_kernel(
    depth_ref,
    view_hbm,
    length_hbm,
    cams_hbm,
    back_hbm,
    target_hbm,
    list_hbm,
    fixed_ref,
    view_ref,
    length_ref,
    cams_ref,
    back_ref,
    target_ref,
    list_ref,
    sems,
):
    sources = (view_hbm, length_hbm, cams_hbm, back_hbm, target_hbm, list_hbm)
    held = (view_ref, length_ref, cams_ref, back_ref, target_ref, list_ref)
    copies = [
        pltpu.make_async_copy(source, there, sems.at[n])
        for n, (source, there) in enumerate(zip(sources, held))
    ]
    for copy in copies:
        copy.start()
    for copy in copies:
        copy.wait()
    for i in range(2):
        for j in range(4):
            at = (i * 4 + j) * TILES
            fixed_ref[at : at + TILES, :] = per_tile([cams_ref[view_ref[b], i, j] for b in range(TILES)])
    place = depth_ref[0] * SLAB + iota((TILES, LANES), 1)
    length = per_tile([length_ref[b].astype(F32) for b in range(TILES)])
    fixed_ref[LIVE : LIVE + TILES, :] = jnp.where(place.astype(F32) < length, 1.0, 0.0)
    for c in range(3):
        fixed_ref[BACK + c * 8 : BACK + c * 8 + 8, :] = jnp.full((8, LANES), back_ref[c], F32)
    fixed_ref[HERE : HERE + 8, :] = jnp.full((8, LANES), depth_ref[0].astype(F32), F32)
    for c in range(3):
        for s in range(8):
            fixed_ref[pl.ds(GOAL + c * TILES * 8 + s, TILES, stride=8), :] = target_ref[
                c, :, s * LANES : (s + 1) * LANES
            ]
    fixed_ref[OWNER : OWNER + 16, :] = list_ref[...].astype(F32)


def table_kernel(side_ref, mine_ref, theirs_ref, loose_ref, table_ref, fixed_ref):
    fixed_ref[...] = loose_ref[...]
    first = side_ref[0] == 0
    blank = jnp.zeros((16 - PARAMS, LANES), F32)
    for a in range(BLOCKS):
        mine = mine_ref[a * PARAMS : (a + 1) * PARAMS, :]
        theirs = theirs_ref[a * PARAMS : (a + 1) * PARAMS, :]
        for h in range(2):
            block = jnp.where(first, mine, theirs) if h == 0 else jnp.where(first, theirs, mine)
            at = h * BLOCKS * 16 + a * 16
            table_ref[at : at + 16, :] = side_by_side(jnp.concatenate([block, blank], axis=0))


def reply_kernel(asked_ref, table_ref, reply_ref, columns, held):
    half = LANES // 2
    columns[...] = asked_ref[...].T
    for h in range(2):
        slots = columns[h * 16 : h * 16 + 16, :]
        rows = jnp.concatenate([slots[:5], slots[5:10]], axis=1)
        table = table_ref[h * BLOCKS * 16 : (h + 1) * BLOCKS * 16, :]
        for q in range(5):
            row = rows[q : q + 1, :]
            pick = onehot(row & (LANES - 1), LANES).astype(BF16)
            found = dot(table, jnp.concatenate([pick, pick, pick], axis=0), NN)
            block = row >> 7
            value = jnp.zeros((16, LANES), F32)
            for a in range(BLOCKS):
                value = value + jnp.where(block == a, found[a * 16 : (a + 1) * 16], 0.0)
            held[q * PARAMS : q * PARAMS + 16, :] = value
        held[5 * PARAMS :, :] = jnp.zeros((LANES - 5 * PARAMS, LANES), F32)
        turned = held[...].T
        reply_ref[:, h, :] = turned[:half] + pltpu.roll(turned[half:], 5 * PARAMS, 1)


def per_tile(values):
    place = iota((TILES, LANES), 0)
    out = jnp.full((TILES, LANES), values[0], F32)
    for b in range(1, TILES):
        out = jnp.where(place == b, values[b], out)
    return out


def camera_rows(fixed_ref):
    rows = [fixed_ref[n * TILES : (n + 1) * TILES, :] for n in range(8)]
    return rows[:4], rows[4:]


def listed(fixed_ref, at, b):
    return fixed_ref[at + b : at + b + 1, :].astype(I32)


def covariance(scales, jac):
    variance = [jnp.exp(2.0 * s) for s in scales]
    xx = sum(jac[0][j] * jac[0][j] * variance[j] for j in range(3)) + 0.3
    xy = sum(jac[0][j] * jac[1][j] * variance[j] for j in range(3))
    yy = sum(jac[1][j] * jac[1][j] * variance[j] for j in range(3)) + 0.3
    return variance, xx, xy, yy, xx * yy - xy * xy


def forward_kernel(
    fetched_ref,
    fixed_ref,
    slab_ref,
    alpha_ref,
    weight_ref,
    shade_ref,
    entry_ref,
    found,
    rows,
    spread,
):
    fetched = side_by_side(fetched_ref[...].T)
    for b in range(TILES):
        named = onehot(listed(fixed_ref, OWNER, b), LANES).astype(BF16)
        found[...] = dot(fetched, jnp.concatenate([named, named, named], axis=0), NN)
        rank = listed(fixed_ref, RANK, b)
        value = jnp.zeros((16, LANES), F32)
        for r in range(SLOTS):
            value = value + jnp.where(rank == r, found[r * PARAMS : r * PARAMS + 16, :], 0.0)
        entry_ref[b * 16 : (b + 1) * 16, :] = value
    entry = [entry_ref[pl.ds(p, TILES, stride=16), :] for p in range(PARAMS)]
    jac = camera_rows(fixed_ref)
    center_x = sum(jac[0][j] * entry[j] for j in range(3)) + jac[0][3] + 16.0
    center_y = sum(jac[1][j] * entry[j] for j in range(3)) + jac[1][3] + 16.0
    _, xx, xy, yy, det = covariance(entry[3:6], jac)
    opacity = jax.nn.sigmoid(entry[6]) * fixed_ref[LIVE : LIVE + TILES, :]
    factors = [
        center_x,
        center_y,
        (-0.5 * LOG2E) * (yy / det),
        LOG2E * (xy / det),
        (-0.5 * LOG2E) * (xx / det),
        opacity,
        *entry[7:10],
    ]
    for p, factor in enumerate(factors):
        rows[p * TILES : (p + 1) * TILES, :] = factor
    rows[len(factors) * TILES :, :] = jnp.zeros((LANES - len(factors) * TILES, LANES), F32)
    turned = rows[...].T
    for p in range(9):
        for b in range(TILES):
            column = turned[:, p * TILES + b : p * TILES + b + 1]
            wide = jnp.broadcast_to(column, (SLAB, LANES))
            if p < 6:
                spread[p, b * SLAB : (b + 1) * SLAB, :] = wide
            else:
                shade_ref[p - 6, b * SLAB : (b + 1) * SLAB, :] = wide
    lane = iota((8, LANES), 1)
    pixel_x = (lane & 31).astype(F32) + 0.5
    pixel_y = (iota((8, LANES), 0) * 4 + (lane >> 5)).astype(F32) + 0.5

    def step(k, carry):
        out = []
        for b in range(TILES):
            trans, red, green, blue = carry[4 * b : 4 * b + 4]
            at = b * SLAB + k
            get = lambda ref, p: ref[p, pl.ds(at, 8, stride=0), :]
            ex = pixel_x - get(spread, 0)
            ey = pixel_y - get(spread, 1)
            power = ex * (get(spread, 2) * ex + get(spread, 3) * ey) + get(spread, 4) * ey * ey
            alpha = get(spread, 5) * jnp.exp2(power)
            weight = alpha * trans
            alpha_ref[at] = alpha
            weight_ref[pl.ds(at, 8, stride=PITCH), :] = weight
            out += [
                trans - weight,
                red + weight * get(shade_ref, 0),
                green + weight * get(shade_ref, 1),
                blue + weight * get(shade_ref, 2),
            ]
        return tuple(out)

    one, zero = jnp.ones((8, LANES), F32), jnp.zeros((8, LANES), F32)
    out = lax.fori_loop(0, SLAB, step, (one, zero, zero, zero) * TILES, unroll=32)
    for q in range(4 * TILES):
        slab_ref[q * 8 : (q + 1) * 8, :] = out[q]


def row_sums(rows):
    a = rows[0]
    b = a + rows[1]
    c = b + rows[2]
    d = c + rows[3]
    e = rows[7]
    f = e + rows[6]
    g = f + rows[5]
    return d + g + rows[4], e + f + g - (a + b + c + d), 7.0 * a + 5.0 * (b + e) + 3.0 * (c + f) + (d + g)


def backward_kernel(
    slabs_ref,
    alpha_ref,
    weight_ref,
    shade_ref,
    entry_ref,
    fixed_ref,
    image_hbm,
    outgoing_ref,
    slope,
    moment,
    grads,
    placed,
    picture,
    image_ref,
    sem,
):
    depth = fixed_ref[HERE : HERE + 8, :]
    back = [fixed_ref[BACK + c * 8 : BACK + c * 8 + 8, :] for c in range(3)]
    seen, behind = [], []
    for b in range(TILES):
        part = lambda i, q: slabs_ref[i, (b * 4 + q) * 8 : (b * 4 + q + 1) * 8, :]
        trans = jnp.ones((8, LANES), F32)
        start = jnp.ones((8, LANES), F32)
        color = [jnp.zeros((8, LANES), F32)] * 3
        for i in range(DEPTHS):
            start = jnp.where(depth == i, trans, start)
            color = [color[c] + trans * part(i, 1 + c) for c in range(3)]
            trans = trans * part(i, 0)
        color = [color[c] + trans * back[c] for c in range(3)]
        miss = []
        for c in range(3):
            at = slice((c * TILES + b) * 8, (c * TILES + b + 1) * 8)
            miss.append(color[c] - fixed_ref[GOAL + at.start : GOAL + at.stop, :])
            picture[at, :] = color[c]
        after = sum(back[c] * miss[c] for c in range(3))
        for i in range(DEPTHS - 1, 0, -1):
            joined = sum(part(i, 1 + c) * miss[c] for c in range(3)) + part(i, 0) * after
            after = jnp.where(i > depth, joined, after)
        seen.append([start * miss[c] for c in range(3)])
        behind.append(start * after)
    for c in range(3):
        for s in range(8):
            image_ref[c, :, s * LANES : (s + 1) * LANES] = picture[
                pl.ds(c * TILES * 8 + s, TILES, stride=8), :
            ]
    shown = pltpu.make_async_copy(image_ref, image_hbm, sem)
    shown.start()

    def step(n, carry):
        k = SLAB - 1 - n
        out = []
        for b in range(TILES):
            at = b * SLAB + k
            get = lambda p: shade_ref[p, pl.ds(at, 8, stride=0), :]
            shade = sum(get(c) * seen[b][c] for c in range(3))
            gap = shade - carry[b]
            rows = pl.ds(at, 8, stride=PITCH)
            slope[rows, :] = weight_ref[rows, :] * gap
            out.append(carry[b] + alpha_ref[at] * gap)
        return tuple(out)

    lax.fori_loop(0, SLAB, step, tuple(behind), unroll=8)

    index = iota((16, LANES), 0)
    lane = iota((16, LANES), 1)
    across, down = (lane & 31) - 16, lane >> 5
    powers = []
    for rows in (
        (1, across, down, across * across, across * down, down * down),
        (0, 0, 4, 0, 4 * across, 8 * down),
        (0, 0, 0, 0, 0, 16),
    ):
        power = jnp.zeros((16, LANES), I32)
        for n, value in enumerate(rows):
            power = jnp.where(index == n, value, power)
        powers += [power.astype(F32).astype(BF16)] * 3
    powers = jnp.concatenate(powers, axis=1)
    for b in range(TILES):
        at = [slice(s * PITCH + b * SLAB, s * PITCH + (b + 1) * SLAB) for s in range(8)]
        field = jnp.concatenate(
            [side_by_side(part) for part in row_sums([slope[at[s], :] for s in range(8)])], axis=1
        )
        moment[b * 32 : b * 32 + 16, :] = dot(powers, field, NT)
        gaze, weights = [], []
        for s in range(8):
            look = jnp.concatenate(
                [*pieces(jnp.concatenate([seen[b][c][s : s + 1, :] for c in range(3)], axis=0))][:2]
                + [jnp.zeros((10, LANES), BF16)],
                axis=0,
            )
            gaze += [look, look]
            weights += pieces(weight_ref[at[s], :])[:2]
        shades = dot(jnp.concatenate(gaze, axis=1), jnp.concatenate(weights, axis=1), NT)
        moment[b * 32 + 16 : (b + 1) * 32, :] = shades
    entry = [entry_ref[pl.ds(p, TILES, stride=16), :] for p in range(PARAMS)]
    jac = camera_rows(fixed_ref)
    m0, mx, my, mxx, mxy, myy = (moment[pl.ds(n, TILES, stride=32), :] for n in range(6))
    variance, xx, xy, yy, det = covariance(entry[3:6], jac)
    cx = sum(jac[0][j] * entry[j] for j in range(3)) + jac[0][3] - 0.5
    cy = sum(jac[1][j] * entry[j] for j in range(3)) + jac[1][3] - 0.5
    sx = mx - cx * m0
    sy = my - cy * m0
    sxx = mxx - cx * (mx + sx)
    sxy = mxy - cx * my - cy * sx
    syy = myy - cy * (my + sy)
    inverse = 1.0 / det
    conic = (yy * inverse, -xy * inverse, xx * inverse)
    d_cx = conic[0] * sx + conic[1] * sy
    d_cy = conic[1] * sx + conic[2] * sy
    d_a, d_b, d_c = -0.5 * sxx, -sxy, -0.5 * syy
    d_det = -(d_a * conic[0] + d_b * conic[1] + d_c * conic[2]) * inverse
    d_xx = d_c * inverse + d_det * yy
    d_yy = d_a * inverse + d_det * xx
    d_xy = -d_b * inverse - 2.0 * xy * d_det
    result = [jac[0][j] * d_cx + jac[1][j] * d_cy for j in range(3)]
    result += [
        2.0
        * variance[j]
        * (
            jac[0][j] * jac[0][j] * d_xx
            + jac[0][j] * jac[1][j] * d_xy
            + jac[1][j] * jac[1][j] * d_yy
        )
        for j in range(3)
    ]
    result += [m0 * (1.0 - jax.nn.sigmoid(entry[6]))]
    result += [
        moment[pl.ds(16 + c, TILES, stride=32), :] + moment[pl.ds(19 + c, TILES, stride=32), :]
        for c in range(3)
    ]
    for p, value in enumerate(result):
        grads[p * TILES : (p + 1) * TILES, :] = value
    placed[...] = jnp.zeros((LANES, LANES), F32)
    outgoing = jnp.zeros((LANES, LANES), F32)
    for b in range(TILES):
        mine = grads[pl.ds(b, PARAMS, stride=TILES), :]
        rank = listed(fixed_ref, RANK, b)
        for r in range(SLOTS):
            placed[r * PARAMS : (r + 1) * PARAMS, :] = jnp.where(rank == r, mine, 0.0)
        here = iota((16, LANES), 0) == rank
        row = jnp.where(here, fixed_ref[ROW + b : ROW + b + 1, :], 0.0)
        placed[SLOTS * PARAMS : SLOTS * PARAMS + 16, :] = row
        named = onehot(listed(fixed_ref, OWNER, b), LANES).astype(BF16)
        named = jnp.concatenate([named, named, named], axis=1)
        outgoing = outgoing + dot(named, side_by_side(placed[...]), NT)
    outgoing_ref[...] = outgoing
    shown.wait()


def collect_kernel(incoming_ref, sums_ref, turned):
    turned[...] = incoming_ref[...].T
    total = jnp.zeros((BLOCKS * 16, LANES), F32)
    for r in range(SLOTS):
        row = turned[SLOTS * PARAMS + r : SLOTS * PARAMS + r + 1, :].astype(I32)
        pick = onehot(row & (LANES - 1), LANES).astype(BF16)
        block = row >> 7
        value = turned[r * PARAMS : r * PARAMS + 16, :]
        spread = jnp.concatenate(
            [jnp.where(block == a, value, 0.0) for a in range(BLOCKS)], axis=0
        )
        total = total + dot(
            side_by_side(spread), jnp.concatenate([pick, pick, pick], axis=1), NT
        )
    for a in range(BLOCKS):
        sums_ref[a * PARAMS : (a + 1) * PARAMS, :] = total[a * 16 : a * 16 + PARAMS]


def adam_kernel(sums_ref, params_ref, first_ref, second_ref, new_ref, new_first_ref, new_second_ref):
    for a in range(BLOCKS):
        at = slice(a * LANES, (a + 1) * LANES)
        gradient = sum(sums_ref[i, a * PARAMS : (a + 1) * PARAMS, :] for i in range(DEPTHS))
        first = 0.9 * first_ref[:, at] + 0.1 * gradient
        second = 0.999 * second_ref[:, at] + 0.001 * gradient * gradient
        step = first / (1.0 - 0.9**10) / (jnp.sqrt(second / (1.0 - 0.999**10)) + 1e-08)
        new_ref[:, at] = params_ref[a * PARAMS : (a + 1) * PARAMS, :] - 0.05 * step
        new_first_ref[:, at] = first
        new_second_ref[:, at] = second


def call(kernel, outs, ins, scratch=(), grant=40, to=None):
    return pl.pallas_call(
        kernel,
        out_shape=[jax.ShapeDtypeStruct(shape, dtype) for shape, dtype in outs],
        in_specs=ins,
        out_specs=to or [VMEM] * len(outs),
        scratch_shapes=list(scratch),
        compiler_params=pltpu.CompilerParams(vmem_limit_bytes=grant * 2**20),
    )


def exchanged_in_plane(array):
    return lax.all_to_all(array, TILE[:2], 0, 0, tiled=True)


def exchanged(array):
    groups = [
        [zy * 4 + hi * 2 + (hi ^ g) for zy in range(LANES // 2) for hi in range(2)] for g in range(2)
    ]
    whole = lax.all_to_all(
        array.reshape(LANES, 1, LANES),
        (*TILE, DEPTH[0]),
        0,
        0,
        axis_index_groups=groups,
        tiled=True,
    )
    return whole.reshape(LANES, LANES)


def body(
    positions,
    log_scales,
    opacity_logits,
    colors,
    first_moment,
    second_moment,
    cameras,
    background,
    target,
    tile_view,
    tile_length,
    list_owner,
    list_row,
):
    square = (LANES, LANES)
    held = pltpu.VMEM(square, F32)
    plane = LANES // 2
    flat = (BLOCKS * PARAMS, LANES)
    lists = (TILES, SLAB)
    sources = (
        list_owner.reshape(lists),
        list_row.reshape(lists),
        positions,
        log_scales,
        opacity_logits,
        colors,
    )
    results = [((plane, LANES), I32), ((16, LANES), I32), (flat, F32)]
    request, listing, params = call(
        request_kernel,
        results,
        [HBM] * 6,
        [pltpu.VMEM(a.shape, a.dtype) for a in sources] + [pltpu.SemaphoreType.DMA((6,))],
        GRANT_ALL,
    )(*sources)
    asked = exchanged_in_plane(request.reshape(plane, 1, LANES)).reshape(plane, LANES)
    theirs = lax.ppermute(params, (TILE[2], DEPTH[0]), [(0, 3), (3, 0), (1, 2), (2, 1)])
    depth = lax.axis_index(DEPTH).astype(I32).reshape(1)
    loose = (
        tile_view,
        tile_length,
        cameras,
        background,
        target.transpose(1, 0, 2),
        listing,
    )
    (fixed,) = call(
        fixed_kernel,
        [((FIXED, LANES), F32)],
        [SMEM] + [HBM] * 6,
        [pltpu.SMEM(a.shape, a.dtype) for a in loose[:4]]
        + [pltpu.VMEM(a.shape, a.dtype) for a in loose[4:]]
        + [pltpu.SemaphoreType.DMA((6,))],
        GRANT_ALL,
    )(depth, *loose)
    side = lax.axis_index(TILE[2]).astype(I32).reshape(1)
    table, fixed = call(
        table_kernel,
        [((2 * BLOCKS * 16, 3 * LANES), BF16), ((FIXED, LANES), F32)],
        [SMEM, VMEM, VMEM, VMEM],
    )(side, params, theirs, fixed)
    (reply,) = call(
        reply_kernel,
        [((plane, 2, LANES), F32)],
        [VMEM, VMEM],
        [pltpu.VMEM((LANES, plane), I32), held],
    )(asked, table)
    fetched = exchanged_in_plane(reply).reshape(square)
    field = (TILES * SLAB, 8, LANES)
    tilted = (8 * PITCH, LANES)
    slab, alpha, weight, shade, entry = call(
        forward_kernel,
        [
            (square, F32),
            (field, F32),
            (tilted, F32),
            ((3, TILES * SLAB + 8, LANES), F32),
            ((TILES * 16, LANES), F32),
        ],
        [VMEM] * 2,
        [held, held, pltpu.VMEM((6, TILES * SLAB + 8, LANES), F32)],
    )(fetched, fixed)
    slabs = lax.all_gather(slab[None], DEPTH, axis=0, tiled=True)
    image, outgoing = call(
        backward_kernel,
        [((3, TILES, 1024), F32), (square, F32)],
        [VMEM] * 6,
        [
            pltpu.VMEM(tilted, F32),
            held,
            pltpu.VMEM((PARAMS * TILES, LANES), F32),
            held,
            pltpu.VMEM((3 * TILES * 8, LANES), F32),
            pltpu.VMEM((3, TILES, 1024), F32),
            pltpu.SemaphoreType.DMA(()),
        ],
        to=[HBM, VMEM],
    )(slabs, alpha, weight, shade, entry, fixed)
    incoming = exchanged(outgoing)
    (sums,) = call(
        collect_kernel,
        [((BLOCKS * PARAMS, LANES), F32)],
        [VMEM],
        [held],
    )(incoming)
    sums = lax.all_gather(sums[None], DEPTH, axis=0, tiled=True)
    updated = call(adam_kernel, [(first_moment.shape, F32)] * 3, [VMEM] * 4)(
        sums, params, first_moment, second_moment
    )
    return (image.transpose(1, 0, 2), *updated)


def solution(mesh):
    torus = Mesh(mesh.devices.reshape(8, 8, 2, 2, 2), (*TILE, *DEPTH))
    split = P(None, TILE)
    placed = (
        *[split] * 6,
        P(),
        P(),
        P(TILE, None, None),
        P(TILE),
        P(TILE),
        P(DEPTH, TILE, None, None),
        P(DEPTH, TILE, None),
    )
    return jax.shard_map(
        body,
        mesh=torus,
        in_specs=placed,
        out_specs=(P(TILE, None, None), split, split, split),
        check_vma=False,
    )
```

```python
import math

import jax
import jax.numpy as jnp
from jax import lax
from jax.experimental import pallas as pl
from jax.experimental.pallas import tpu as pltpu
from jax.sharding import Mesh
from jax.sharding import PartitionSpec as P

LANES = 128
TILES = 4
SLAB = 128
DEPTHS = 4
SLOTS = 10
PARAMS = 10
BLOCKS = 16
GRANT_ALL = 60
LIVE, BACK, HERE, GOAL, OWNER, FIXED = 32, 40, 64, 72, 168, 184
RANK, ROW = OWNER + TILES, OWNER + 2 * TILES
PITCH = TILES * SLAB + 1
TILE = ("tile_z", "tile_y", "tile_x")
DEPTH = ("depth_x", "depth_core")
LOG2E = math.log2(math.e)
VMEM = pl.BlockSpec(memory_space=pltpu.VMEM)
SMEM = pl.BlockSpec(memory_space=pltpu.SMEM)
HBM = pl.BlockSpec(memory_space=pltpu.HBM)
F32 = jnp.float32
BF16 = jnp.bfloat16
I32 = jnp.int32
NT = (((1,), (1,)), ((), ()))
NN = (((1,), (0,)), ((), ()))


def iota(shape, dim):
    return lax.broadcasted_iota(I32, shape, dim)


def pieces(x):
    high = x.astype(BF16)
    rest = x - high.astype(F32)
    middle = rest.astype(BF16)
    low = (rest - middle.astype(F32)).astype(BF16)
    return high, middle, low


def side_by_side(x):
    return jnp.concatenate(pieces(x), axis=1)


def dot(a, b, dims):
    return lax.dot_general(a, b, dims, preferred_element_type=F32)


def onehot(index, rows):
    return jnp.where(iota((rows, LANES), 0) == index, 1.0, 0.0)


def request_kernel(
    owner_hbm,
    row_hbm,
    position_hbm,
    scale_hbm,
    opacity_hbm,
    color_hbm,
    request_ref,
    list_ref,
    params_ref,
    owner_ref,
    row_ref,
    position,
    scale,
    opacity,
    color,
    sems,
):
    sources = (owner_hbm, row_hbm, position_hbm, scale_hbm, opacity_hbm, color_hbm)
    held = (owner_ref, row_ref, position, scale, opacity, color)
    copies = [
        pltpu.make_async_copy(source, there, sems.at[n])
        for n, (source, there) in enumerate(zip(sources, held))
    ]
    for copy in copies:
        copy.start()
    for copy in copies[:2]:
        copy.wait()
    earlier = jnp.where(iota((SLAB, SLAB), 0) < iota((SLAB, SLAB), 1), 1.0, 0.0).astype(BF16)
    before = jnp.zeros((LANES, 1), F32)
    total = jnp.zeros((LANES // 2, LANES), F32)
    for b in range(TILES):
        owner = owner_ref[b : b + 1, :]
        row = row_ref[b : b + 1, :]
        named = onehot(owner, LANES)
        count = dot(named.astype(BF16), earlier, NN) + before
        before = before + jnp.sum(named, axis=1, keepdims=True)
        rank = jnp.sum(named * count, axis=0, keepdims=True).astype(I32)
        here = iota((LANES, SLAB), 0) == (owner & 1) * 16 + rank
        high = jnp.where(here, row >> 4, 0).astype(F32).astype(BF16)
        low = jnp.where(here, row & 15, 0).astype(F32).astype(BF16)
        place = onehot(owner >> 1, LANES // 2).astype(BF16)
        total = total + 16.0 * dot(place, high, NT) + dot(place, low, NT)
        list_ref[b : b + 1, :] = owner
        list_ref[TILES + b : TILES + b + 1, :] = rank
        list_ref[2 * TILES + b : 2 * TILES + b + 1, :] = row
    list_ref[3 * TILES :, :] = jnp.zeros((TILES, LANES), I32)
    request_ref[...] = total.astype(I32)
    for copy in copies[2:]:
        copy.wait()
    for a in range(BLOCKS):
        at = slice(a * LANES, (a + 1) * LANES)
        params_ref[a * PARAMS : a * PARAMS + 3, :] = position[:, at]
        params_ref[a * PARAMS + 3 : a * PARAMS + 6, :] = scale[:, at]
        params_ref[a * PARAMS + 6 : a * PARAMS + 7, :] = opacity[:, at]
        params_ref[a * PARAMS + 7 : a * PARAMS + 10, :] = color[:, at]


def fixed_kernel(
    depth_ref,
    view_hbm,
    length_hbm,
    cams_hbm,
    back_hbm,
    target_hbm,
    list_hbm,
    fixed_ref,
    view_ref,
    length_ref,
    cams_ref,
    back_ref,
    target_ref,
    list_ref,
    sems,
):
    sources = (view_hbm, length_hbm, cams_hbm, back_hbm, target_hbm, list_hbm)
    held = (view_ref, length_ref, cams_ref, back_ref, target_ref, list_ref)
    copies = [
        pltpu.make_async_copy(source, there, sems.at[n])
        for n, (source, there) in enumerate(zip(sources, held))
    ]
    for copy in copies:
        copy.start()
    for copy in copies:
        copy.wait()
    for i in range(2):
        for j in range(4):
            at = (i * 4 + j) * TILES
            fixed_ref[at : at + TILES, :] = per_tile([cams_ref[view_ref[b], i, j] for b in range(TILES)])
    place = depth_ref[0] * SLAB + iota((TILES, LANES), 1)
    length = per_tile([length_ref[b].astype(F32) for b in range(TILES)])
    fixed_ref[LIVE : LIVE + TILES, :] = jnp.where(place.astype(F32) < length, 1.0, 0.0)
    for c in range(3):
        fixed_ref[BACK + c * 8 : BACK + c * 8 + 8, :] = jnp.full((8, LANES), back_ref[c], F32)
    fixed_ref[HERE : HERE + 8, :] = jnp.full((8, LANES), depth_ref[0].astype(F32), F32)
    for c in range(3):
        for s in range(8):
            fixed_ref[pl.ds(GOAL + c * TILES * 8 + s, TILES, stride=8), :] = target_ref[
                c, :, s * LANES : (s + 1) * LANES
            ]
    fixed_ref[OWNER : OWNER + 16, :] = list_ref[...].astype(F32)


def monomials(shape, rows):
    index, pixel = iota(shape, 0), iota(shape, 1)
    x, y = (pixel & 31) - 16, (pixel >> 5) - 16
    out = jnp.zeros(shape, I32)
    for k in range(3 * rows):
        out = jnp.where(index == k, (1, x, y, x * x, x * y, y * y)[k % rows], out)
    return out.astype(F32).astype(BF16)


def table_kernel(side_ref, mine_ref, theirs_ref, loose_ref, table_ref, fixed_ref, powers_ref):
    fixed_ref[...] = loose_ref[...]
    powers_ref[...] = monomials((32, 1024), 6)
    first = side_ref[0] == 0
    blank = jnp.zeros((16 - PARAMS, LANES), F32)
    for a in range(BLOCKS):
        mine = mine_ref[a * PARAMS : (a + 1) * PARAMS, :]
        theirs = theirs_ref[a * PARAMS : (a + 1) * PARAMS, :]
        for h in range(2):
            block = jnp.where(first, mine, theirs) if h == 0 else jnp.where(first, theirs, mine)
            at = h * BLOCKS * 16 + a * 16
            table_ref[at : at + 16, :] = side_by_side(jnp.concatenate([block, blank], axis=0))


def reply_kernel(asked_ref, table_ref, reply_ref, columns, held):
    half = LANES // 2
    columns[...] = asked_ref[...].T
    for h in range(2):
        slots = columns[h * 16 : h * 16 + 16, :]
        rows = jnp.concatenate([slots[:5], slots[5:10]], axis=1)
        table = table_ref[h * BLOCKS * 16 : (h + 1) * BLOCKS * 16, :]
        for q in range(5):
            row = rows[q : q + 1, :]
            pick = onehot(row & (LANES - 1), LANES).astype(BF16)
            found = dot(table, jnp.concatenate([pick, pick, pick], axis=0), NN)
            block = row >> 7
            value = jnp.zeros((16, LANES), F32)
            for a in range(BLOCKS):
                value = value + jnp.where(block == a, found[a * 16 : (a + 1) * 16], 0.0)
            held[q * PARAMS : q * PARAMS + 16, :] = value
        held[5 * PARAMS :, :] = jnp.zeros((LANES - 5 * PARAMS, LANES), F32)
        turned = held[...].T
        reply_ref[:, h, :] = turned[:half] + pltpu.roll(turned[half:], 5 * PARAMS, 1)


def per_tile(values):
    place = iota((TILES, LANES), 0)
    out = jnp.full((TILES, LANES), values[0], F32)
    for b in range(1, TILES):
        out = jnp.where(place == b, values[b], out)
    return out


def camera_rows(fixed_ref):
    rows = [fixed_ref[n * TILES : (n + 1) * TILES, :] for n in range(8)]
    return rows[:4], rows[4:]


def listed(fixed_ref, at, b):
    return fixed_ref[at + b : at + b + 1, :].astype(I32)


def covariance(scales, jac):
    variance = [jnp.exp(2.0 * s) for s in scales]
    xx = sum(jac[0][j] * jac[0][j] * variance[j] for j in range(3)) + 0.3
    xy = sum(jac[0][j] * jac[1][j] * variance[j] for j in range(3))
    yy = sum(jac[1][j] * jac[1][j] * variance[j] for j in range(3)) + 0.3
    return variance, xx, xy, yy, xx * yy - xy * xy


def forward_kernel(
    fetched_ref,
    fixed_ref,
    powers_ref,
    slab_ref,
    alpha_ref,
    weight_ref,
    shade_ref,
    entry_ref,
    found,
    rows,
):
    fetched = side_by_side(fetched_ref[...].T)
    for b in range(TILES):
        named = onehot(listed(fixed_ref, OWNER, b), LANES).astype(BF16)
        found[...] = dot(fetched, jnp.concatenate([named, named, named], axis=0), NN)
        rank = listed(fixed_ref, RANK, b)
        value = jnp.zeros((16, LANES), F32)
        for r in range(SLOTS):
            value = value + jnp.where(rank == r, found[r * PARAMS : r * PARAMS + 16, :], 0.0)
        entry_ref[b * 16 : (b + 1) * 16, :] = value
    entry = [entry_ref[pl.ds(p, TILES, stride=16), :] for p in range(PARAMS)]
    jac = camera_rows(fixed_ref)
    cx = sum(jac[0][j] * entry[j] for j in range(3)) + jac[0][3] - 0.5
    cy = sum(jac[1][j] * entry[j] for j in range(3)) + jac[1][3] - 0.5
    _, xx, xy, yy, det = covariance(entry[3:6], jac)
    qa = (-0.5 * LOG2E) * (yy / det)
    qb = LOG2E * (xy / det)
    qc = (-0.5 * LOG2E) * (xx / det)
    live = fixed_ref[LIVE : LIVE + TILES, :]
    height = LOG2E * jnp.log(jax.nn.sigmoid(entry[6])) - 1e5 * (1.0 - live)
    factors = [
        cx * (qa * cx + qb * cy) + qc * cy * cy + height,
        -(2.0 * qa * cx + qb * cy),
        -(2.0 * qc * cy + qb * cx),
        qa,
        qb,
        qc,
    ]
    rows[...] = jnp.zeros((LANES, LANES), F32)
    for k, factor in enumerate(factors):
        for n, piece in enumerate(pieces(factor)):
            rows[pl.ds(n * 6 + k, TILES, stride=32), :] = piece.astype(F32)
    for c in range(3):
        rows[pl.ds(18 + c, TILES, stride=32), :] = entry[7 + c]
    turned = rows[...].T
    powers = powers_ref[...]
    for b in range(TILES):
        blank = [jnp.zeros((32, 1024), BF16)] * TILES
        blank[b] = powers
        alpha = jnp.exp2(dot(turned.astype(BF16), jnp.concatenate(blank, axis=0), NN))
        for s in range(8):
            at = s * PITCH + b * SLAB
            alpha_ref[at : at + SLAB, :] = alpha[:, s * LANES : (s + 1) * LANES]
        for c in range(3):
            column = turned[:, b * 32 + 18 + c : b * 32 + 19 + c]
            shade_ref[c, b * SLAB : (b + 1) * SLAB, :] = jnp.broadcast_to(column, (SLAB, LANES))

    def step(k, carry):
        out = []
        for b in range(TILES):
            trans, red, green, blue = carry[4 * b : 4 * b + 4]
            at = b * SLAB + k
            spots = pl.ds(at, 8, stride=PITCH)
            get = lambda p: shade_ref[p, pl.ds(at, 8, stride=0), :]
            weight = alpha_ref[spots, :] * trans
            weight_ref[spots, :] = weight
            out += [
                trans - weight,
                red + weight * get(0),
                green + weight * get(1),
                blue + weight * get(2),
            ]
        return tuple(out)

    one, zero = jnp.ones((8, LANES), F32), jnp.zeros((8, LANES), F32)
    out = lax.fori_loop(0, SLAB, step, (one, zero, zero, zero) * TILES, unroll=32)
    for q in range(4 * TILES):
        slab_ref[q * 8 : (q + 1) * 8, :] = out[q]


def row_sums(rows):
    a = rows[0]
    b = a + rows[1]
    c = b + rows[2]
    d = c + rows[3]
    e = rows[7]
    f = e + rows[6]
    g = f + rows[5]
    return d + g + rows[4], e + f + g - (a + b + c + d), 7.0 * a + 5.0 * (b + e) + 3.0 * (c + f) + (d + g)


def backward_kernel(
    slabs_ref,
    alpha_ref,
    weight_ref,
    shade_ref,
    entry_ref,
    fixed_ref,
    image_hbm,
    outgoing_ref,
    slope,
    moment,
    grads,
    placed,
    picture,
    image_ref,
    sem,
):
    depth = fixed_ref[HERE : HERE + 8, :]
    back = [fixed_ref[BACK + c * 8 : BACK + c * 8 + 8, :] for c in range(3)]
    seen, behind = [], []
    for b in range(TILES):
        part = lambda i, q: slabs_ref[i, (b * 4 + q) * 8 : (b * 4 + q + 1) * 8, :]
        trans = jnp.ones((8, LANES), F32)
        start = jnp.ones((8, LANES), F32)
        color = [jnp.zeros((8, LANES), F32)] * 3
        for i in range(DEPTHS):
            start = jnp.where(depth == i, trans, start)
            color = [color[c] + trans * part(i, 1 + c) for c in range(3)]
            trans = trans * part(i, 0)
        color = [color[c] + trans * back[c] for c in range(3)]
        miss = []
        for c in range(3):
            at = slice((c * TILES + b) * 8, (c * TILES + b + 1) * 8)
            miss.append(color[c] - fixed_ref[GOAL + at.start : GOAL + at.stop, :])
            picture[at, :] = color[c]
        after = sum(back[c] * miss[c] for c in range(3))
        for i in range(DEPTHS - 1, 0, -1):
            joined = sum(part(i, 1 + c) * miss[c] for c in range(3)) + part(i, 0) * after
            after = jnp.where(i > depth, joined, after)
        seen.append([start * miss[c] for c in range(3)])
        behind.append(start * after)
    for c in range(3):
        for s in range(8):
            image_ref[c, :, s * LANES : (s + 1) * LANES] = picture[
                pl.ds(c * TILES * 8 + s, TILES, stride=8), :
            ]
    shown = pltpu.make_async_copy(image_ref, image_hbm, sem)
    shown.start()

    def step(n, carry):
        k = SLAB - 1 - n
        out = []
        for b in range(TILES):
            at = b * SLAB + k
            get = lambda p: shade_ref[p, pl.ds(at, 8, stride=0), :]
            shade = sum(get(c) * seen[b][c] for c in range(3))
            gap = shade - carry[b]
            rows = pl.ds(at, 8, stride=PITCH)
            slope[rows, :] = weight_ref[rows, :] * gap
            out.append(carry[b] + alpha_ref[rows, :] * gap)
        return tuple(out)

    lax.fori_loop(0, SLAB, step, tuple(behind), unroll=8)

    index = iota((16, LANES), 0)
    lane = iota((16, LANES), 1)
    across, down = (lane & 31) - 16, lane >> 5
    powers = []
    for rows in (
        (1, across, down, across * across, across * down, down * down),
        (0, 0, 4, 0, 4 * across, 8 * down),
        (0, 0, 0, 0, 0, 16),
    ):
        power = jnp.zeros((16, LANES), I32)
        for n, value in enumerate(rows):
            power = jnp.where(index == n, value, power)
        powers += [power.astype(F32).astype(BF16)] * 3
    powers = jnp.concatenate(powers, axis=1)
    for b in range(TILES):
        at = [slice(s * PITCH + b * SLAB, s * PITCH + (b + 1) * SLAB) for s in range(8)]
        field = jnp.concatenate(
            [side_by_side(part) for part in row_sums([slope[at[s], :] for s in range(8)])], axis=1
        )
        moment[b * 32 : b * 32 + 16, :] = dot(powers, field, NT)
        gaze, weights = [], []
        for s in range(8):
            look = jnp.concatenate(
                [*pieces(jnp.concatenate([seen[b][c][s : s + 1, :] for c in range(3)], axis=0))][:2]
                + [jnp.zeros((10, LANES), BF16)],
                axis=0,
            )
            gaze += [look, look]
            weights += pieces(weight_ref[at[s], :])[:2]
        shades = dot(jnp.concatenate(gaze, axis=1), jnp.concatenate(weights, axis=1), NT)
        moment[b * 32 + 16 : (b + 1) * 32, :] = shades
    entry = [entry_ref[pl.ds(p, TILES, stride=16), :] for p in range(PARAMS)]
    jac = camera_rows(fixed_ref)
    m0, mx, my, mxx, mxy, myy = (moment[pl.ds(n, TILES, stride=32), :] for n in range(6))
    variance, xx, xy, yy, det = covariance(entry[3:6], jac)
    cx = sum(jac[0][j] * entry[j] for j in range(3)) + jac[0][3] - 0.5
    cy = sum(jac[1][j] * entry[j] for j in range(3)) + jac[1][3] - 0.5
    sx = mx - cx * m0
    sy = my - cy * m0
    sxx = mxx - cx * (mx + sx)
    sxy = mxy - cx * my - cy * sx
    syy = myy - cy * (my + sy)
    inverse = 1.0 / det
    conic = (yy * inverse, -xy * inverse, xx * inverse)
    d_cx = conic[0] * sx + conic[1] * sy
    d_cy = conic[1] * sx + conic[2] * sy
    d_a, d_b, d_c = -0.5 * sxx, -sxy, -0.5 * syy
    d_det = -(d_a * conic[0] + d_b * conic[1] + d_c * conic[2]) * inverse
    d_xx = d_c * inverse + d_det * yy
    d_yy = d_a * inverse + d_det * xx
    d_xy = -d_b * inverse - 2.0 * xy * d_det
    result = [jac[0][j] * d_cx + jac[1][j] * d_cy for j in range(3)]
    result += [
        2.0
        * variance[j]
        * (
            jac[0][j] * jac[0][j] * d_xx
            + jac[0][j] * jac[1][j] * d_xy
            + jac[1][j] * jac[1][j] * d_yy
        )
        for j in range(3)
    ]
    result += [m0 * (1.0 - jax.nn.sigmoid(entry[6]))]
    result += [
        moment[pl.ds(16 + c, TILES, stride=32), :] + moment[pl.ds(19 + c, TILES, stride=32), :]
        for c in range(3)
    ]
    for p, value in enumerate(result):
        grads[p * TILES : (p + 1) * TILES, :] = value
    placed[...] = jnp.zeros((LANES, LANES), F32)
    outgoing = jnp.zeros((LANES, LANES), F32)
    for b in range(TILES):
        mine = grads[pl.ds(b, PARAMS, stride=TILES), :]
        rank = listed(fixed_ref, RANK, b)
        for r in range(SLOTS):
            placed[r * PARAMS : (r + 1) * PARAMS, :] = jnp.where(rank == r, mine, 0.0)
        here = iota((16, LANES), 0) == rank
        row = jnp.where(here, fixed_ref[ROW + b : ROW + b + 1, :], 0.0)
        placed[SLOTS * PARAMS : SLOTS * PARAMS + 16, :] = row
        named = onehot(listed(fixed_ref, OWNER, b), LANES).astype(BF16)
        named = jnp.concatenate([named, named, named], axis=1)
        outgoing = outgoing + dot(named, side_by_side(placed[...]), NT)
    outgoing_ref[...] = outgoing
    shown.wait()


def collect_kernel(incoming_ref, sums_ref, turned):
    turned[...] = incoming_ref[...].T
    total = jnp.zeros((BLOCKS * 16, LANES), F32)
    for r in range(SLOTS):
        row = turned[SLOTS * PARAMS + r : SLOTS * PARAMS + r + 1, :].astype(I32)
        pick = onehot(row & (LANES - 1), LANES).astype(BF16)
        block = row >> 7
        value = turned[r * PARAMS : r * PARAMS + 16, :]
        spread = jnp.concatenate(
            [jnp.where(block == a, value, 0.0) for a in range(BLOCKS)], axis=0
        )
        total = total + dot(
            side_by_side(spread), jnp.concatenate([pick, pick, pick], axis=1), NT
        )
    for a in range(BLOCKS):
        sums_ref[a * PARAMS : (a + 1) * PARAMS, :] = total[a * 16 : a * 16 + PARAMS]


def adam_kernel(sums_ref, params_ref, first_ref, second_ref, new_ref, new_first_ref, new_second_ref):
    for a in range(BLOCKS):
        at = slice(a * LANES, (a + 1) * LANES)
        gradient = sum(sums_ref[i, a * PARAMS : (a + 1) * PARAMS, :] for i in range(DEPTHS))
        first = 0.9 * first_ref[:, at] + 0.1 * gradient
        second = 0.999 * second_ref[:, at] + 0.001 * gradient * gradient
        step = first / (1.0 - 0.9**10) / (jnp.sqrt(second / (1.0 - 0.999**10)) + 1e-08)
        new_ref[:, at] = params_ref[a * PARAMS : (a + 1) * PARAMS, :] - 0.05 * step
        new_first_ref[:, at] = first
        new_second_ref[:, at] = second


def call(kernel, outs, ins, scratch=(), grant=40, to=None):
    return pl.pallas_call(
        kernel,
        out_shape=[jax.ShapeDtypeStruct(shape, dtype) for shape, dtype in outs],
        in_specs=ins,
        out_specs=to or [VMEM] * len(outs),
        scratch_shapes=list(scratch),
        compiler_params=pltpu.CompilerParams(vmem_limit_bytes=grant * 2**20),
    )


def exchanged_in_plane(array):
    return lax.all_to_all(array, TILE[:2], 0, 0, tiled=True)


def exchanged(array):
    groups = [
        [zy * 4 + hi * 2 + (hi ^ g) for zy in range(LANES // 2) for hi in range(2)] for g in range(2)
    ]
    whole = lax.all_to_all(
        array.reshape(LANES, 1, LANES),
        (*TILE, DEPTH[0]),
        0,
        0,
        axis_index_groups=groups,
        tiled=True,
    )
    return whole.reshape(LANES, LANES)


def body(
    positions,
    log_scales,
    opacity_logits,
    colors,
    first_moment,
    second_moment,
    cameras,
    background,
    target,
    tile_view,
    tile_length,
    list_owner,
    list_row,
):
    square = (LANES, LANES)
    held = pltpu.VMEM(square, F32)
    plane = LANES // 2
    flat = (BLOCKS * PARAMS, LANES)
    lists = (TILES, SLAB)
    sources = (
        list_owner.reshape(lists),
        list_row.reshape(lists),
        positions,
        log_scales,
        opacity_logits,
        colors,
    )
    results = [((plane, LANES), I32), ((16, LANES), I32), (flat, F32)]
    request, listing, params = call(
        request_kernel,
        results,
        [HBM] * 6,
        [pltpu.VMEM(a.shape, a.dtype) for a in sources] + [pltpu.SemaphoreType.DMA((6,))],
        GRANT_ALL,
    )(*sources)
    asked = exchanged_in_plane(request.reshape(plane, 1, LANES)).reshape(plane, LANES)
    theirs = lax.ppermute(params, (TILE[2], DEPTH[0]), [(0, 3), (3, 0), (1, 2), (2, 1)])
    depth = lax.axis_index(DEPTH).astype(I32).reshape(1)
    loose = (
        tile_view,
        tile_length,
        cameras,
        background,
        target.transpose(1, 0, 2),
        listing,
    )
    (fixed,) = call(
        fixed_kernel,
        [((FIXED, LANES), F32)],
        [SMEM] + [HBM] * 6,
        [pltpu.SMEM(a.shape, a.dtype) for a in loose[:4]]
        + [pltpu.VMEM(a.shape, a.dtype) for a in loose[4:]]
        + [pltpu.SemaphoreType.DMA((6,))],
        GRANT_ALL,
    )(depth, *loose)
    side = lax.axis_index(TILE[2]).astype(I32).reshape(1)
    table, fixed, powers = call(
        table_kernel,
        [((2 * BLOCKS * 16, 3 * LANES), BF16), ((FIXED, LANES), F32), ((32, 1024), BF16)],
        [SMEM, VMEM, VMEM, VMEM],
    )(side, params, theirs, fixed)
    (reply,) = call(
        reply_kernel,
        [((plane, 2, LANES), F32)],
        [VMEM, VMEM],
        [pltpu.VMEM((LANES, plane), I32), held],
    )(asked, table)
    fetched = exchanged_in_plane(reply).reshape(square)
    tilted = (8 * PITCH, LANES)
    slab, alpha, weight, shade, entry = call(
        forward_kernel,
        [
            (square, F32),
            (tilted, F32),
            (tilted, F32),
            ((3, TILES * SLAB + 8, LANES), F32),
            ((TILES * 16, LANES), F32),
        ],
        [VMEM] * 3,
        [held, held],
    )(fetched, fixed, powers)
    slabs = lax.all_gather(slab[None], DEPTH, axis=0, tiled=True)
    image, outgoing = call(
        backward_kernel,
        [((3, TILES, 1024), F32), (square, F32)],
        [VMEM] * 6,
        [
            pltpu.VMEM(tilted, F32),
            held,
            pltpu.VMEM((PARAMS * TILES, LANES), F32),
            held,
            pltpu.VMEM((3 * TILES * 8, LANES), F32),
            pltpu.VMEM((3, TILES, 1024), F32),
            pltpu.SemaphoreType.DMA(()),
        ],
        to=[HBM, VMEM],
    )(slabs, alpha, weight, shade, entry, fixed)
    incoming = exchanged(outgoing)
    (sums,) = call(
        collect_kernel,
        [((BLOCKS * PARAMS, LANES), F32)],
        [VMEM],
        [held],
    )(incoming)
    sums = lax.all_gather(sums[None], DEPTH, axis=0, tiled=True)
    updated = call(adam_kernel, [(first_moment.shape, F32)] * 3, [VMEM] * 4)(
        sums, params, first_moment, second_moment
    )
    return (image.transpose(1, 0, 2), *updated)


def solution(mesh):
    torus = Mesh(mesh.devices.reshape(8, 8, 2, 2, 2), (*TILE, *DEPTH))
    split = P(None, TILE)
    placed = (
        *[split] * 6,
        P(),
        P(),
        P(TILE, None, None),
        P(TILE),
        P(TILE),
        P(DEPTH, TILE, None, None),
        P(DEPTH, TILE, None),
    )
    return jax.shard_map(
        body,
        mesh=torus,
        in_specs=placed,
        out_specs=(P(TILE, None, None), split, split, split),
        check_vma=False,
    )
```

```python
import math

import jax
import jax.numpy as jnp
from jax import lax
from jax.experimental import pallas as pl
from jax.experimental.pallas import tpu as pltpu
from jax.sharding import Mesh
from jax.sharding import PartitionSpec as P

LANES = 128
TILES = 4
SLAB = 128
DEPTHS = 4
SLOTS = 10
PARAMS = 10
BLOCKS = 16
GRANT_ALL = 60
LIVE, BACK, HERE, GOAL, OWNER, FIXED = 32, 40, 64, 72, 168, 184
RANK, ROW = OWNER + TILES, OWNER + 2 * TILES
PITCH = TILES * SLAB + 1
TILE = ("tile_z", "tile_y", "tile_x")
DEPTH = ("depth_x", "depth_core")
LOG2E = math.log2(math.e)
VMEM = pl.BlockSpec(memory_space=pltpu.VMEM)
SMEM = pl.BlockSpec(memory_space=pltpu.SMEM)
HBM = pl.BlockSpec(memory_space=pltpu.HBM)
F32 = jnp.float32
BF16 = jnp.bfloat16
I32 = jnp.int32
NT = (((1,), (1,)), ((), ()))
NN = (((1,), (0,)), ((), ()))


def iota(shape, dim):
    return lax.broadcasted_iota(I32, shape, dim)


def pieces(x):
    high = x.astype(BF16)
    rest = x - high.astype(F32)
    middle = rest.astype(BF16)
    low = (rest - middle.astype(F32)).astype(BF16)
    return high, middle, low


def side_by_side(x):
    return jnp.concatenate(pieces(x), axis=1)


def two_side_by_side(x):
    return jnp.concatenate(pieces(x)[:2], axis=1)


def dot(a, b, dims):
    return lax.dot_general(a, b, dims, preferred_element_type=F32)


def onehot(index, rows):
    return jnp.where(iota((rows, LANES), 0) == index, 1.0, 0.0)


def request_kernel(
    owner_hbm,
    row_hbm,
    position_hbm,
    scale_hbm,
    opacity_hbm,
    color_hbm,
    request_ref,
    list_ref,
    params_ref,
    owner_ref,
    row_ref,
    position,
    scale,
    opacity,
    color,
    sems,
):
    sources = (owner_hbm, row_hbm, position_hbm, scale_hbm, opacity_hbm, color_hbm)
    held = (owner_ref, row_ref, position, scale, opacity, color)
    copies = [
        pltpu.make_async_copy(source, there, sems.at[n])
        for n, (source, there) in enumerate(zip(sources, held))
    ]
    for copy in copies:
        copy.start()
    for copy in copies[:2]:
        copy.wait()
    earlier = jnp.where(iota((SLAB, SLAB), 0) < iota((SLAB, SLAB), 1), 1.0, 0.0).astype(BF16)
    before = jnp.zeros((LANES, 1), F32)
    total = jnp.zeros((LANES // 2, LANES), F32)
    for b in range(TILES):
        owner = owner_ref[b : b + 1, :]
        row = row_ref[b : b + 1, :]
        named = onehot(owner, LANES)
        count = dot(named.astype(BF16), earlier, NN) + before
        before = before + jnp.sum(named, axis=1, keepdims=True)
        rank = jnp.sum(named * count, axis=0, keepdims=True).astype(I32)
        here = iota((LANES, SLAB), 0) == (owner & 1) * 16 + rank
        high = jnp.where(here, row >> 4, 0).astype(F32).astype(BF16)
        low = jnp.where(here, row & 15, 0).astype(F32).astype(BF16)
        place = onehot(owner >> 1, LANES // 2).astype(BF16)
        total = total + 16.0 * dot(place, high, NT) + dot(place, low, NT)
        list_ref[b : b + 1, :] = owner
        list_ref[TILES + b : TILES + b + 1, :] = rank
        list_ref[2 * TILES + b : 2 * TILES + b + 1, :] = row
    list_ref[3 * TILES :, :] = jnp.zeros((TILES, LANES), I32)
    request_ref[...] = total.astype(I32)
    for copy in copies[2:]:
        copy.wait()
    for a in range(BLOCKS):
        at = slice(a * LANES, (a + 1) * LANES)
        params_ref[a * PARAMS : a * PARAMS + 3, :] = position[:, at]
        params_ref[a * PARAMS + 3 : a * PARAMS + 6, :] = scale[:, at]
        params_ref[a * PARAMS + 6 : a * PARAMS + 7, :] = opacity[:, at]
        params_ref[a * PARAMS + 7 : a * PARAMS + 10, :] = color[:, at]


def fixed_kernel(
    depth_ref,
    view_hbm,
    length_hbm,
    cams_hbm,
    back_hbm,
    target_hbm,
    list_hbm,
    fixed_ref,
    view_ref,
    length_ref,
    cams_ref,
    back_ref,
    target_ref,
    list_ref,
    sems,
):
    sources = (view_hbm, length_hbm, cams_hbm, back_hbm, target_hbm, list_hbm)
    held = (view_ref, length_ref, cams_ref, back_ref, target_ref, list_ref)
    copies = [
        pltpu.make_async_copy(source, there, sems.at[n])
        for n, (source, there) in enumerate(zip(sources, held))
    ]
    for copy in copies:
        copy.start()
    for copy in copies:
        copy.wait()
    for i in range(2):
        for j in range(4):
            at = (i * 4 + j) * TILES
            fixed_ref[at : at + TILES, :] = per_tile([cams_ref[view_ref[b], i, j] for b in range(TILES)])
    place = depth_ref[0] * SLAB + iota((TILES, LANES), 1)
    length = per_tile([length_ref[b].astype(F32) for b in range(TILES)])
    fixed_ref[LIVE : LIVE + TILES, :] = jnp.where(place.astype(F32) < length, 1.0, 0.0)
    for c in range(3):
        fixed_ref[BACK + c * 8 : BACK + c * 8 + 8, :] = jnp.full((8, LANES), back_ref[c], F32)
    fixed_ref[HERE : HERE + 8, :] = jnp.full((8, LANES), depth_ref[0].astype(F32), F32)
    for c in range(3):
        for s in range(8):
            fixed_ref[pl.ds(GOAL + c * TILES * 8 + s, TILES, stride=8), :] = target_ref[
                c, :, s * LANES : (s + 1) * LANES
            ]
    fixed_ref[OWNER : OWNER + 16, :] = list_ref[...].astype(F32)


def monomials(shape, rows):
    index, pixel = iota(shape, 0), iota(shape, 1)
    x, y = (pixel & 31) - 16, (pixel >> 5) - 16
    out = jnp.zeros(shape, I32)
    for k in range(3 * rows):
        out = jnp.where(index == k, (1, x, y, x * x, x * y, y * y)[k % rows], out)
    return out.astype(F32).astype(BF16)


def table_kernel(side_ref, mine_ref, theirs_ref, loose_ref, table_ref, fixed_ref, powers_ref):
    fixed_ref[...] = loose_ref[...]
    powers_ref[...] = monomials((32, 1024), 6)
    first = side_ref[0] == 0
    blank = jnp.zeros((16 - PARAMS, LANES), F32)
    for a in range(BLOCKS):
        mine = mine_ref[a * PARAMS : (a + 1) * PARAMS, :]
        theirs = theirs_ref[a * PARAMS : (a + 1) * PARAMS, :]
        for h in range(2):
            block = jnp.where(first, mine, theirs) if h == 0 else jnp.where(first, theirs, mine)
            at = h * BLOCKS * 16 + a * 16
            table_ref[at : at + 16, :] = side_by_side(jnp.concatenate([block, blank], axis=0))


def reply_kernel(asked_ref, table_ref, reply_ref, columns, held):
    half = LANES // 2
    columns[...] = asked_ref[...].T
    for h in range(2):
        slots = columns[h * 16 : h * 16 + 16, :]
        rows = jnp.concatenate([slots[:5], slots[5:10]], axis=1)
        table = table_ref[h * BLOCKS * 16 : (h + 1) * BLOCKS * 16, :]
        for q in range(5):
            row = rows[q : q + 1, :]
            pick = onehot(row & (LANES - 1), LANES).astype(BF16)
            found = dot(table, jnp.concatenate([pick, pick, pick], axis=0), NN)
            block = row >> 7
            value = jnp.zeros((16, LANES), F32)
            for a in range(BLOCKS):
                value = value + jnp.where(block == a, found[a * 16 : (a + 1) * 16], 0.0)
            held[q * PARAMS : q * PARAMS + 16, :] = value
        held[5 * PARAMS :, :] = jnp.zeros((LANES - 5 * PARAMS, LANES), F32)
        turned = held[...].T
        reply_ref[:, h, :] = turned[:half] + pltpu.roll(turned[half:], 5 * PARAMS, 1)


def per_tile(values):
    place = iota((TILES, LANES), 0)
    out = jnp.full((TILES, LANES), values[0], F32)
    for b in range(1, TILES):
        out = jnp.where(place == b, values[b], out)
    return out


def camera_rows(fixed_ref):
    rows = [fixed_ref[n * TILES : (n + 1) * TILES, :] for n in range(8)]
    return rows[:4], rows[4:]


def listed(fixed_ref, at, b):
    return fixed_ref[at + b : at + b + 1, :].astype(I32)


def covariance(scales, jac):
    variance = [jnp.exp(2.0 * s) for s in scales]
    xx = sum(jac[0][j] * jac[0][j] * variance[j] for j in range(3)) + 0.3
    xy = sum(jac[0][j] * jac[1][j] * variance[j] for j in range(3))
    yy = sum(jac[1][j] * jac[1][j] * variance[j] for j in range(3)) + 0.3
    return variance, xx, xy, yy, xx * yy - xy * xy


def forward_kernel(
    fetched_ref,
    fixed_ref,
    powers_ref,
    slab_ref,
    alpha_ref,
    weight_ref,
    shade_ref,
    entry_ref,
    found,
    rows,
):
    fetched = side_by_side(fetched_ref[...].T)
    for b in range(TILES):
        named = onehot(listed(fixed_ref, OWNER, b), LANES).astype(BF16)
        found[...] = dot(fetched, jnp.concatenate([named, named, named], axis=0), NN)
        rank = listed(fixed_ref, RANK, b)
        value = jnp.zeros((16, LANES), F32)
        for r in range(SLOTS):
            value = value + jnp.where(rank == r, found[r * PARAMS : r * PARAMS + 16, :], 0.0)
        entry_ref[b * 16 : (b + 1) * 16, :] = value
    entry = [entry_ref[pl.ds(p, TILES, stride=16), :] for p in range(PARAMS)]
    jac = camera_rows(fixed_ref)
    cx = sum(jac[0][j] * entry[j] for j in range(3)) + jac[0][3] - 0.5
    cy = sum(jac[1][j] * entry[j] for j in range(3)) + jac[1][3] - 0.5
    _, xx, xy, yy, det = covariance(entry[3:6], jac)
    qa = (-0.5 * LOG2E) * (yy / det)
    qb = LOG2E * (xy / det)
    qc = (-0.5 * LOG2E) * (xx / det)
    live = fixed_ref[LIVE : LIVE + TILES, :]
    height = LOG2E * jnp.log(jax.nn.sigmoid(entry[6])) - 1e5 * (1.0 - live)
    factors = [
        cx * (qa * cx + qb * cy) + qc * cy * cy + height,
        -(2.0 * qa * cx + qb * cy),
        -(2.0 * qc * cy + qb * cx),
        qa,
        qb,
        qc,
    ]
    rows[...] = jnp.zeros((LANES, LANES), F32)
    for k, factor in enumerate(factors):
        for n, piece in enumerate(pieces(factor)):
            rows[pl.ds(n * 6 + k, TILES, stride=32), :] = piece.astype(F32)
    for c in range(3):
        rows[pl.ds(18 + c, TILES, stride=32), :] = entry[7 + c]
    turned = rows[...].T
    powers = powers_ref[...]
    for b in range(TILES):
        blank = [jnp.zeros((32, 1024), BF16)] * TILES
        blank[b] = powers
        alpha = jnp.exp2(dot(turned.astype(BF16), jnp.concatenate(blank, axis=0), NN))
        for s in range(8):
            at = s * PITCH + b * SLAB
            alpha_ref[at : at + SLAB, :] = alpha[:, s * LANES : (s + 1) * LANES]
        for c in range(3):
            column = turned[:, b * 32 + 18 + c : b * 32 + 19 + c]
            shade_ref[c, b * SLAB : (b + 1) * SLAB, :] = jnp.broadcast_to(column, (SLAB, LANES))

    def step(k, carry):
        out = []
        for b in range(TILES):
            trans, red, green, blue = carry[4 * b : 4 * b + 4]
            at = b * SLAB + k
            spots = pl.ds(at, 8, stride=PITCH)
            get = lambda p: shade_ref[p, pl.ds(at, 8, stride=0), :]
            weight = alpha_ref[spots, :] * trans
            weight_ref[spots, :] = weight
            out += [
                trans - weight,
                red + weight * get(0),
                green + weight * get(1),
                blue + weight * get(2),
            ]
        return tuple(out)

    one, zero = jnp.ones((8, LANES), F32), jnp.zeros((8, LANES), F32)
    out = lax.fori_loop(0, SLAB, step, (one, zero, zero, zero) * TILES, unroll=32)
    for q in range(4 * TILES):
        slab_ref[q * 8 : (q + 1) * 8, :] = out[q]


def row_sums(rows):
    a = rows[0]
    b = a + rows[1]
    c = b + rows[2]
    d = c + rows[3]
    e = rows[7]
    f = e + rows[6]
    g = f + rows[5]
    return d + g + rows[4], e + f + g - (a + b + c + d), 7.0 * a + 5.0 * (b + e) + 3.0 * (c + f) + (d + g)


def backward_kernel(
    slabs_ref,
    alpha_ref,
    weight_ref,
    shade_ref,
    entry_ref,
    fixed_ref,
    image_hbm,
    outgoing_ref,
    slope,
    moment,
    grads,
    placed,
    picture,
    image_ref,
    sem,
):
    depth = fixed_ref[HERE : HERE + 8, :]
    back = [fixed_ref[BACK + c * 8 : BACK + c * 8 + 8, :] for c in range(3)]
    seen, behind = [], []
    for b in range(TILES):
        part = lambda i, q: slabs_ref[i, (b * 4 + q) * 8 : (b * 4 + q + 1) * 8, :]
        trans = jnp.ones((8, LANES), F32)
        start = jnp.ones((8, LANES), F32)
        color = [jnp.zeros((8, LANES), F32)] * 3
        for i in range(DEPTHS):
            start = jnp.where(depth == i, trans, start)
            color = [color[c] + trans * part(i, 1 + c) for c in range(3)]
            trans = trans * part(i, 0)
        color = [color[c] + trans * back[c] for c in range(3)]
        miss = []
        for c in range(3):
            at = slice((c * TILES + b) * 8, (c * TILES + b + 1) * 8)
            miss.append(color[c] - fixed_ref[GOAL + at.start : GOAL + at.stop, :])
            picture[at, :] = color[c]
        after = sum(back[c] * miss[c] for c in range(3))
        for i in range(DEPTHS - 1, 0, -1):
            joined = sum(part(i, 1 + c) * miss[c] for c in range(3)) + part(i, 0) * after
            after = jnp.where(i > depth, joined, after)
        seen.append([start * miss[c] for c in range(3)])
        behind.append(start * after)
    for c in range(3):
        for s in range(8):
            image_ref[c, :, s * LANES : (s + 1) * LANES] = picture[
                pl.ds(c * TILES * 8 + s, TILES, stride=8), :
            ]
    shown = pltpu.make_async_copy(image_ref, image_hbm, sem)
    shown.start()

    def step(n, carry):
        k = SLAB - 1 - n
        out = []
        for b in range(TILES):
            at = b * SLAB + k
            get = lambda p: shade_ref[p, pl.ds(at, 8, stride=0), :]
            shade = sum(get(c) * seen[b][c] for c in range(3))
            gap = shade - carry[b]
            rows = pl.ds(at, 8, stride=PITCH)
            slope[rows, :] = weight_ref[rows, :] * gap
            out.append(carry[b] + alpha_ref[rows, :] * gap)
        return tuple(out)

    lax.fori_loop(0, SLAB, step, tuple(behind), unroll=8)

    index = iota((16, LANES), 0)
    lane = iota((16, LANES), 1)
    across, down = (lane & 31) - 16, lane >> 5
    powers = []
    for rows in (
        (1, across, down, across * across, across * down, down * down),
        (0, 0, 4, 0, 4 * across, 8 * down),
        (0, 0, 0, 0, 0, 16),
    ):
        power = jnp.zeros((16, LANES), I32)
        for n, value in enumerate(rows):
            power = jnp.where(index == n, value, power)
        powers += [power.astype(F32).astype(BF16)] * 3
    powers = jnp.concatenate(powers, axis=1)
    for b in range(TILES):
        at = [slice(s * PITCH + b * SLAB, s * PITCH + (b + 1) * SLAB) for s in range(8)]
        field = jnp.concatenate(
            [side_by_side(part) for part in row_sums([slope[at[s], :] for s in range(8)])], axis=1
        )
        moment[b * 32 : b * 32 + 16, :] = dot(powers, field, NT)
        gaze, weights = [], []
        for s in range(8):
            look = jnp.concatenate(
                [*pieces(jnp.concatenate([seen[b][c][s : s + 1, :] for c in range(3)], axis=0))][:2]
                + [jnp.zeros((10, LANES), BF16)],
                axis=0,
            )
            gaze += [look, look]
            weights += pieces(weight_ref[at[s], :])[:2]
        shades = dot(jnp.concatenate(gaze, axis=1), jnp.concatenate(weights, axis=1), NT)
        moment[b * 32 + 16 : (b + 1) * 32, :] = shades
    entry = [entry_ref[pl.ds(p, TILES, stride=16), :] for p in range(PARAMS)]
    jac = camera_rows(fixed_ref)
    m0, mx, my, mxx, mxy, myy = (moment[pl.ds(n, TILES, stride=32), :] for n in range(6))
    variance, xx, xy, yy, det = covariance(entry[3:6], jac)
    cx = sum(jac[0][j] * entry[j] for j in range(3)) + jac[0][3] - 0.5
    cy = sum(jac[1][j] * entry[j] for j in range(3)) + jac[1][3] - 0.5
    sx = mx - cx * m0
    sy = my - cy * m0
    sxx = mxx - cx * (mx + sx)
    sxy = mxy - cx * my - cy * sx
    syy = myy - cy * (my + sy)
    inverse = 1.0 / det
    conic = (yy * inverse, -xy * inverse, xx * inverse)
    d_cx = conic[0] * sx + conic[1] * sy
    d_cy = conic[1] * sx + conic[2] * sy
    d_a, d_b, d_c = -0.5 * sxx, -sxy, -0.5 * syy
    d_det = -(d_a * conic[0] + d_b * conic[1] + d_c * conic[2]) * inverse
    d_xx = d_c * inverse + d_det * yy
    d_yy = d_a * inverse + d_det * xx
    d_xy = -d_b * inverse - 2.0 * xy * d_det
    result = [jac[0][j] * d_cx + jac[1][j] * d_cy for j in range(3)]
    result += [
        2.0
        * variance[j]
        * (
            jac[0][j] * jac[0][j] * d_xx
            + jac[0][j] * jac[1][j] * d_xy
            + jac[1][j] * jac[1][j] * d_yy
        )
        for j in range(3)
    ]
    result += [m0 * (1.0 - jax.nn.sigmoid(entry[6]))]
    result += [
        moment[pl.ds(16 + c, TILES, stride=32), :] + moment[pl.ds(19 + c, TILES, stride=32), :]
        for c in range(3)
    ]
    for p, value in enumerate(result):
        grads[p * TILES : (p + 1) * TILES, :] = value
    placed[...] = jnp.zeros((LANES, LANES), F32)
    outgoing = jnp.zeros((LANES, LANES), F32)
    for b in range(TILES):
        mine = grads[pl.ds(b, PARAMS, stride=TILES), :]
        rank = listed(fixed_ref, RANK, b)
        for r in range(SLOTS):
            placed[r * PARAMS : (r + 1) * PARAMS, :] = jnp.where(rank == r, mine, 0.0)
        here = iota((16, LANES), 0) == rank
        row = jnp.where(here, fixed_ref[ROW + b : ROW + b + 1, :], 0.0)
        placed[SLOTS * PARAMS : SLOTS * PARAMS + 16, :] = row
        named = onehot(listed(fixed_ref, OWNER, b), LANES).astype(BF16)
        named = jnp.concatenate([named, named], axis=1)
        outgoing = outgoing + dot(named, two_side_by_side(placed[...]), NT)
    outgoing_ref[...] = outgoing
    shown.wait()


def collect_kernel(incoming_ref, sums_ref, turned):
    turned[...] = incoming_ref[...].T
    total = jnp.zeros((BLOCKS * 16, LANES), F32)
    for r in range(SLOTS):
        row = turned[SLOTS * PARAMS + r : SLOTS * PARAMS + r + 1, :].astype(I32)
        pick = onehot(row & (LANES - 1), LANES).astype(BF16)
        block = row >> 7
        value = turned[r * PARAMS : r * PARAMS + 16, :]
        spread = jnp.concatenate(
            [jnp.where(block == a, value, 0.0) for a in range(BLOCKS)], axis=0
        )
        total = total + dot(
            two_side_by_side(spread), jnp.concatenate([pick, pick], axis=1), NT
        )
    for a in range(BLOCKS):
        sums_ref[a * PARAMS : (a + 1) * PARAMS, :] = total[a * 16 : a * 16 + PARAMS]


def adam_kernel(sums_ref, params_ref, first_ref, second_ref, new_ref, new_first_ref, new_second_ref):
    for a in range(BLOCKS):
        at = slice(a * LANES, (a + 1) * LANES)
        gradient = sum(sums_ref[i, a * PARAMS : (a + 1) * PARAMS, :] for i in range(DEPTHS))
        first = 0.9 * first_ref[:, at] + 0.1 * gradient
        second = 0.999 * second_ref[:, at] + 0.001 * gradient * gradient
        step = first / (1.0 - 0.9**10) / (jnp.sqrt(second / (1.0 - 0.999**10)) + 1e-08)
        new_ref[:, at] = params_ref[a * PARAMS : (a + 1) * PARAMS, :] - 0.05 * step
        new_first_ref[:, at] = first
        new_second_ref[:, at] = second


def call(kernel, outs, ins, scratch=(), grant=40, to=None):
    return pl.pallas_call(
        kernel,
        out_shape=[jax.ShapeDtypeStruct(shape, dtype) for shape, dtype in outs],
        in_specs=ins,
        out_specs=to or [VMEM] * len(outs),
        scratch_shapes=list(scratch),
        compiler_params=pltpu.CompilerParams(vmem_limit_bytes=grant * 2**20),
    )


def exchanged_in_plane(array):
    return lax.all_to_all(array, TILE[:2], 0, 0, tiled=True)


def exchanged(array):
    groups = [
        [zy * 4 + hi * 2 + (hi ^ g) for zy in range(LANES // 2) for hi in range(2)] for g in range(2)
    ]
    whole = lax.all_to_all(
        array.reshape(LANES, 1, LANES),
        (*TILE, DEPTH[0]),
        0,
        0,
        axis_index_groups=groups,
        tiled=True,
    )
    return whole.reshape(LANES, LANES)


def body(
    positions,
    log_scales,
    opacity_logits,
    colors,
    first_moment,
    second_moment,
    cameras,
    background,
    target,
    tile_view,
    tile_length,
    list_owner,
    list_row,
):
    square = (LANES, LANES)
    held = pltpu.VMEM(square, F32)
    plane = LANES // 2
    flat = (BLOCKS * PARAMS, LANES)
    lists = (TILES, SLAB)
    sources = (
        list_owner.reshape(lists),
        list_row.reshape(lists),
        positions,
        log_scales,
        opacity_logits,
        colors,
    )
    results = [((plane, LANES), I32), ((16, LANES), I32), (flat, F32)]
    request, listing, params = call(
        request_kernel,
        results,
        [HBM] * 6,
        [pltpu.VMEM(a.shape, a.dtype) for a in sources] + [pltpu.SemaphoreType.DMA((6,))],
        GRANT_ALL,
    )(*sources)
    asked = exchanged_in_plane(request.reshape(plane, 1, LANES)).reshape(plane, LANES)
    theirs = lax.ppermute(params, (TILE[2], DEPTH[0]), [(0, 3), (3, 0), (1, 2), (2, 1)])
    depth = lax.axis_index(DEPTH).astype(I32).reshape(1)
    loose = (
        tile_view,
        tile_length,
        cameras,
        background,
        target.transpose(1, 0, 2),
        listing,
    )
    (fixed,) = call(
        fixed_kernel,
        [((FIXED, LANES), F32)],
        [SMEM] + [HBM] * 6,
        [pltpu.SMEM(a.shape, a.dtype) for a in loose[:4]]
        + [pltpu.VMEM(a.shape, a.dtype) for a in loose[4:]]
        + [pltpu.SemaphoreType.DMA((6,))],
        GRANT_ALL,
    )(depth, *loose)
    side = lax.axis_index(TILE[2]).astype(I32).reshape(1)
    table, fixed, powers = call(
        table_kernel,
        [((2 * BLOCKS * 16, 3 * LANES), BF16), ((FIXED, LANES), F32), ((32, 1024), BF16)],
        [SMEM, VMEM, VMEM, VMEM],
    )(side, params, theirs, fixed)
    (reply,) = call(
        reply_kernel,
        [((plane, 2, LANES), F32)],
        [VMEM, VMEM],
        [pltpu.VMEM((LANES, plane), I32), held],
    )(asked, table)
    fetched = exchanged_in_plane(reply).reshape(square)
    tilted = (8 * PITCH, LANES)
    slab, alpha, weight, shade, entry = call(
        forward_kernel,
        [
            (square, F32),
            (tilted, F32),
            (tilted, F32),
            ((3, TILES * SLAB + 8, LANES), F32),
            ((TILES * 16, LANES), F32),
        ],
        [VMEM] * 3,
        [held, held],
    )(fetched, fixed, powers)
    slabs = lax.all_gather(slab[None], DEPTH, axis=0, tiled=True)
    image, outgoing = call(
        backward_kernel,
        [((3, TILES, 1024), F32), (square, F32)],
        [VMEM] * 6,
        [
            pltpu.VMEM(tilted, F32),
            held,
            pltpu.VMEM((PARAMS * TILES, LANES), F32),
            held,
            pltpu.VMEM((3 * TILES * 8, LANES), F32),
            pltpu.VMEM((3, TILES, 1024), F32),
            pltpu.SemaphoreType.DMA(()),
        ],
        to=[HBM, VMEM],
    )(slabs, alpha, weight, shade, entry, fixed)
    incoming = exchanged(outgoing)
    (sums,) = call(
        collect_kernel,
        [((BLOCKS * PARAMS, LANES), F32)],
        [VMEM],
        [held],
    )(incoming)
    sums = lax.all_gather(sums[None], DEPTH, axis=0, tiled=True)
    updated = call(adam_kernel, [(first_moment.shape, F32)] * 3, [VMEM] * 4)(
        sums, params, first_moment, second_moment
    )
    return (image.transpose(1, 0, 2), *updated)


def solution(mesh):
    torus = Mesh(mesh.devices.reshape(8, 8, 2, 2, 2), (*TILE, *DEPTH))
    split = P(None, TILE)
    placed = (
        *[split] * 6,
        P(),
        P(),
        P(TILE, None, None),
        P(TILE),
        P(TILE),
        P(DEPTH, TILE, None, None),
        P(DEPTH, TILE, None),
    )
    return jax.shard_map(
        body,
        mesh=torus,
        in_specs=placed,
        out_specs=(P(TILE, None, None), split, split, split),
        check_vma=False,
    )
```

```python
import math

import jax
import jax.numpy as jnp
from jax import lax
from jax.experimental import pallas as pl
from jax.experimental.pallas import tpu as pltpu
from jax.sharding import Mesh
from jax.sharding import PartitionSpec as P

LANES = 128
TILES = 4
SLAB = 128
DEPTHS = 4
SLOTS = 10
PARAMS = 10
BLOCKS = 16
GRANT_ALL = 60
LIVE, BACK, HERE, GOAL, OWNER, FIXED = 32, 40, 64, 72, 168, 184
RANK, ROW = OWNER + TILES, OWNER + 2 * TILES
PITCH = TILES * SLAB + 1
TILE = ("tile_z", "tile_y", "tile_x")
DEPTH = ("depth_x", "depth_core")
LOG2E = math.log2(math.e)
VMEM = pl.BlockSpec(memory_space=pltpu.VMEM)
SMEM = pl.BlockSpec(memory_space=pltpu.SMEM)
HBM = pl.BlockSpec(memory_space=pltpu.HBM)
F32 = jnp.float32
BF16 = jnp.bfloat16
I32 = jnp.int32
NT = (((1,), (1,)), ((), ()))
NN = (((1,), (0,)), ((), ()))


def iota(shape, dim):
    return lax.broadcasted_iota(I32, shape, dim)


def pieces(x):
    high = x.astype(BF16)
    rest = x - high.astype(F32)
    middle = rest.astype(BF16)
    low = (rest - middle.astype(F32)).astype(BF16)
    return high, middle, low


def side_by_side(x):
    return jnp.concatenate(pieces(x), axis=1)


def dot(a, b, dims):
    return lax.dot_general(a, b, dims, preferred_element_type=F32)


def onehot(index, rows):
    return jnp.where(iota((rows, LANES), 0) == index, 1.0, 0.0)


def request_kernel(
    owner_hbm,
    row_hbm,
    position_hbm,
    scale_hbm,
    opacity_hbm,
    color_hbm,
    request_ref,
    list_ref,
    params_ref,
    owner_ref,
    row_ref,
    position,
    scale,
    opacity,
    color,
    sems,
):
    sources = (owner_hbm, row_hbm, position_hbm, scale_hbm, opacity_hbm, color_hbm)
    held = (owner_ref, row_ref, position, scale, opacity, color)
    copies = [
        pltpu.make_async_copy(source, there, sems.at[n])
        for n, (source, there) in enumerate(zip(sources, held))
    ]
    for copy in copies:
        copy.start()
    for copy in copies[:2]:
        copy.wait()
    earlier = jnp.where(iota((SLAB, SLAB), 0) < iota((SLAB, SLAB), 1), 1.0, 0.0).astype(BF16)
    before = jnp.zeros((LANES, 1), F32)
    total = jnp.zeros((LANES // 2, LANES), F32)
    for b in range(TILES):
        owner = owner_ref[b : b + 1, :]
        row = row_ref[b : b + 1, :]
        named = onehot(owner, LANES)
        count = dot(named.astype(BF16), earlier, NN) + before
        before = before + jnp.sum(named, axis=1, keepdims=True)
        rank = jnp.sum(named * count, axis=0, keepdims=True).astype(I32)
        here = iota((LANES, SLAB), 0) == (owner & 1) * 16 + rank
        high = jnp.where(here, row >> 4, 0).astype(F32).astype(BF16)
        low = jnp.where(here, row & 15, 0).astype(F32).astype(BF16)
        place = onehot(owner >> 1, LANES // 2).astype(BF16)
        total = total + 16.0 * dot(place, high, NT) + dot(place, low, NT)
        list_ref[b : b + 1, :] = owner
        list_ref[TILES + b : TILES + b + 1, :] = rank
        list_ref[2 * TILES + b : 2 * TILES + b + 1, :] = row
    list_ref[3 * TILES :, :] = jnp.zeros((TILES, LANES), I32)
    request_ref[...] = total.astype(I32)
    for copy in copies[2:]:
        copy.wait()
    for a in range(BLOCKS):
        at = slice(a * LANES, (a + 1) * LANES)
        params_ref[a * PARAMS : a * PARAMS + 3, :] = position[:, at]
        params_ref[a * PARAMS + 3 : a * PARAMS + 6, :] = scale[:, at]
        params_ref[a * PARAMS + 6 : a * PARAMS + 7, :] = opacity[:, at]
        params_ref[a * PARAMS + 7 : a * PARAMS + 10, :] = color[:, at]


def fixed_kernel(
    depth_ref,
    view_hbm,
    length_hbm,
    cams_hbm,
    back_hbm,
    target_hbm,
    list_hbm,
    fixed_ref,
    view_ref,
    length_ref,
    cams_ref,
    back_ref,
    target_ref,
    list_ref,
    sems,
):
    sources = (view_hbm, length_hbm, cams_hbm, back_hbm, target_hbm, list_hbm)
    held = (view_ref, length_ref, cams_ref, back_ref, target_ref, list_ref)
    copies = [
        pltpu.make_async_copy(source, there, sems.at[n])
        for n, (source, there) in enumerate(zip(sources, held))
    ]
    for copy in copies:
        copy.start()
    for copy in copies:
        copy.wait()
    for i in range(2):
        for j in range(4):
            at = (i * 4 + j) * TILES
            fixed_ref[at : at + TILES, :] = per_tile([cams_ref[view_ref[b], i, j] for b in range(TILES)])
    place = depth_ref[0] * SLAB + iota((TILES, LANES), 1)
    length = per_tile([length_ref[b].astype(F32) for b in range(TILES)])
    fixed_ref[LIVE : LIVE + TILES, :] = jnp.where(place.astype(F32) < length, 1.0, 0.0)
    for c in range(3):
        fixed_ref[BACK + c * 8 : BACK + c * 8 + 8, :] = jnp.full((8, LANES), back_ref[c], F32)
    fixed_ref[HERE : HERE + 8, :] = jnp.full((8, LANES), depth_ref[0].astype(F32), F32)
    for c in range(3):
        for s in range(8):
            fixed_ref[pl.ds(GOAL + c * TILES * 8 + s, TILES, stride=8), :] = target_ref[
                c, :, s * LANES : (s + 1) * LANES
            ]
    fixed_ref[OWNER : OWNER + 16, :] = list_ref[...].astype(F32)


def monomials(shape, rows):
    index, pixel = iota(shape, 0), iota(shape, 1)
    x, y = (pixel & 31) - 16, (pixel >> 5) - 16
    out = jnp.zeros(shape, I32)
    for k in range(3 * rows):
        out = jnp.where(index == k, (1, x, y, x * x, x * y, y * y)[k % rows], out)
    return out.astype(F32).astype(BF16)


def table_kernel(side_ref, mine_ref, theirs_ref, loose_ref, table_ref, fixed_ref, powers_ref):
    fixed_ref[...] = loose_ref[...]
    powers_ref[...] = monomials((32, 1024), 6)
    first = side_ref[0] == 0
    blank = jnp.zeros((16 - PARAMS, LANES), F32)
    for a in range(BLOCKS):
        mine = mine_ref[a * PARAMS : (a + 1) * PARAMS, :]
        theirs = theirs_ref[a * PARAMS : (a + 1) * PARAMS, :]
        for h in range(2):
            block = jnp.where(first, mine, theirs) if h == 0 else jnp.where(first, theirs, mine)
            at = h * BLOCKS * 16 + a * 16
            table_ref[at : at + 16, :] = side_by_side(jnp.concatenate([block, blank], axis=0))


def reply_kernel(asked_ref, table_ref, reply_ref, columns, held):
    half = LANES // 2
    columns[...] = asked_ref[...].T
    for h in range(2):
        slots = columns[h * 16 : h * 16 + 16, :]
        rows = jnp.concatenate([slots[:5], slots[5:10]], axis=1)
        table = table_ref[h * BLOCKS * 16 : (h + 1) * BLOCKS * 16, :]
        for q in range(5):
            row = rows[q : q + 1, :]
            pick = onehot(row & (LANES - 1), LANES).astype(BF16)
            found = dot(table, jnp.concatenate([pick, pick, pick], axis=0), NN)
            block = row >> 7
            value = jnp.zeros((16, LANES), F32)
            for a in range(BLOCKS):
                value = value + jnp.where(block == a, found[a * 16 : (a + 1) * 16], 0.0)
            held[q * PARAMS : q * PARAMS + 16, :] = value
        held[5 * PARAMS :, :] = jnp.zeros((LANES - 5 * PARAMS, LANES), F32)
        turned = held[...].T
        reply_ref[:, h, :] = turned[:half] + pltpu.roll(turned[half:], 5 * PARAMS, 1)


def per_tile(values):
    place = iota((TILES, LANES), 0)
    out = jnp.full((TILES, LANES), values[0], F32)
    for b in range(1, TILES):
        out = jnp.where(place == b, values[b], out)
    return out


def camera_rows(fixed_ref):
    rows = [fixed_ref[n * TILES : (n + 1) * TILES, :] for n in range(8)]
    return rows[:4], rows[4:]


def listed(fixed_ref, at, b):
    return fixed_ref[at + b : at + b + 1, :].astype(I32)


def covariance(scales, jac):
    variance = [jnp.exp(2.0 * s) for s in scales]
    xx = sum(jac[0][j] * jac[0][j] * variance[j] for j in range(3)) + 0.3
    xy = sum(jac[0][j] * jac[1][j] * variance[j] for j in range(3))
    yy = sum(jac[1][j] * jac[1][j] * variance[j] for j in range(3)) + 0.3
    return variance, xx, xy, yy, xx * yy - xy * xy


def forward_kernel(
    fetched_ref,
    fixed_ref,
    powers_ref,
    slab_ref,
    alpha_ref,
    weight_ref,
    shade_ref,
    entry_ref,
    found,
    rows,
):
    fetched = side_by_side(fetched_ref[...].T)
    for b in range(TILES):
        named = onehot(listed(fixed_ref, OWNER, b), LANES).astype(BF16)
        found[...] = dot(fetched, jnp.concatenate([named, named, named], axis=0), NN)
        rank = listed(fixed_ref, RANK, b)
        value = jnp.zeros((16, LANES), F32)
        for r in range(SLOTS):
            value = value + jnp.where(rank == r, found[r * PARAMS : r * PARAMS + 16, :], 0.0)
        entry_ref[b * 16 : (b + 1) * 16, :] = value
    entry = [entry_ref[pl.ds(p, TILES, stride=16), :] for p in range(PARAMS)]
    jac = camera_rows(fixed_ref)
    cx = sum(jac[0][j] * entry[j] for j in range(3)) + jac[0][3] - 0.5
    cy = sum(jac[1][j] * entry[j] for j in range(3)) + jac[1][3] - 0.5
    _, xx, xy, yy, det = covariance(entry[3:6], jac)
    qa = (-0.5 * LOG2E) * (yy / det)
    qb = LOG2E * (xy / det)
    qc = (-0.5 * LOG2E) * (xx / det)
    live = fixed_ref[LIVE : LIVE + TILES, :]
    height = LOG2E * jnp.log(jax.nn.sigmoid(entry[6])) - 1e5 * (1.0 - live)
    factors = [
        cx * (qa * cx + qb * cy) + qc * cy * cy + height,
        -(2.0 * qa * cx + qb * cy),
        -(2.0 * qc * cy + qb * cx),
        qa,
        qb,
        qc,
    ]
    rows[...] = jnp.zeros((LANES, LANES), F32)
    for k, factor in enumerate(factors):
        for n, piece in enumerate(pieces(factor)):
            rows[pl.ds(n * 6 + k, TILES, stride=32), :] = piece.astype(F32)
    for c in range(3):
        rows[pl.ds(18 + c, TILES, stride=32), :] = entry[7 + c]
    turned = rows[...].T
    powers = powers_ref[...]
    for b in range(TILES):
        blank = [jnp.zeros((32, 1024), BF16)] * TILES
        blank[b] = powers
        alpha = jnp.exp2(dot(turned.astype(BF16), jnp.concatenate(blank, axis=0), NN))
        for s in range(8):
            at = s * PITCH + b * SLAB
            alpha_ref[at : at + SLAB, :] = alpha[:, s * LANES : (s + 1) * LANES]
        for c in range(3):
            column = turned[:, b * 32 + 18 + c : b * 32 + 19 + c]
            shade_ref[c, b * SLAB : (b + 1) * SLAB, :] = jnp.broadcast_to(column, (SLAB, LANES))

    def step(k, carry):
        out = []
        for b in range(TILES):
            trans, red, green, blue = carry[4 * b : 4 * b + 4]
            at = b * SLAB + k
            spots = pl.ds(at, 8, stride=PITCH)
            get = lambda p: shade_ref[p, pl.ds(at, 8, stride=0), :]
            weight = alpha_ref[spots, :] * trans
            weight_ref[spots, :] = weight
            out += [
                trans - weight,
                red + weight * get(0),
                green + weight * get(1),
                blue + weight * get(2),
            ]
        return tuple(out)

    one, zero = jnp.ones((8, LANES), F32), jnp.zeros((8, LANES), F32)
    out = lax.fori_loop(0, SLAB, step, (one, zero, zero, zero) * TILES, unroll=128)
    for q in range(4 * TILES):
        slab_ref[q * 8 : (q + 1) * 8, :] = out[q]


def row_sums(rows):
    a = rows[0]
    b = a + rows[1]
    c = b + rows[2]
    d = c + rows[3]
    e = rows[7]
    f = e + rows[6]
    g = f + rows[5]
    return d + g + rows[4], e + f + g - (a + b + c + d), 7.0 * a + 5.0 * (b + e) + 3.0 * (c + f) + (d + g)


def backward_kernel(
    slabs_ref,
    alpha_ref,
    weight_ref,
    shade_ref,
    entry_ref,
    fixed_ref,
    image_hbm,
    outgoing_ref,
    slope,
    moment,
    grads,
    placed,
    picture,
    image_ref,
    sem,
):
    depth = fixed_ref[HERE : HERE + 8, :]
    back = [fixed_ref[BACK + c * 8 : BACK + c * 8 + 8, :] for c in range(3)]
    seen, behind = [], []
    for b in range(TILES):
        part = lambda i, q: slabs_ref[i, (b * 4 + q) * 8 : (b * 4 + q + 1) * 8, :]
        trans = jnp.ones((8, LANES), F32)
        start = jnp.ones((8, LANES), F32)
        color = [jnp.zeros((8, LANES), F32)] * 3
        for i in range(DEPTHS):
            start = jnp.where(depth == i, trans, start)
            color = [color[c] + trans * part(i, 1 + c) for c in range(3)]
            trans = trans * part(i, 0)
        color = [color[c] + trans * back[c] for c in range(3)]
        miss = []
        for c in range(3):
            at = slice((c * TILES + b) * 8, (c * TILES + b + 1) * 8)
            miss.append(color[c] - fixed_ref[GOAL + at.start : GOAL + at.stop, :])
            picture[at, :] = color[c]
        after = sum(back[c] * miss[c] for c in range(3))
        for i in range(DEPTHS - 1, 0, -1):
            joined = sum(part(i, 1 + c) * miss[c] for c in range(3)) + part(i, 0) * after
            after = jnp.where(i > depth, joined, after)
        seen.append([start * miss[c] for c in range(3)])
        behind.append(start * after)
    for c in range(3):
        for s in range(8):
            image_ref[c, :, s * LANES : (s + 1) * LANES] = picture[
                pl.ds(c * TILES * 8 + s, TILES, stride=8), :
            ]
    shown = pltpu.make_async_copy(image_ref, image_hbm, sem)
    shown.start()

    def step(n, carry):
        k = SLAB - 1 - n
        out = []
        for b in range(TILES):
            at = b * SLAB + k
            get = lambda p: shade_ref[p, pl.ds(at, 8, stride=0), :]
            shade = sum(get(c) * seen[b][c] for c in range(3))
            gap = shade - carry[b]
            rows = pl.ds(at, 8, stride=PITCH)
            slope[rows, :] = weight_ref[rows, :] * gap
            alpha = alpha_ref[rows, :]
            out.append(carry[b] * (1.0 - alpha) + alpha * shade)
        return tuple(out)

    lax.fori_loop(0, SLAB, step, tuple(behind), unroll=8)

    index = iota((16, LANES), 0)
    lane = iota((16, LANES), 1)
    across, down = (lane & 31) - 16, lane >> 5
    powers = []
    for rows in (
        (1, across, down, across * across, across * down, down * down),
        (0, 0, 4, 0, 4 * across, 8 * down),
        (0, 0, 0, 0, 0, 16),
    ):
        power = jnp.zeros((16, LANES), I32)
        for n, value in enumerate(rows):
            power = jnp.where(index == n, value, power)
        powers += [power.astype(F32).astype(BF16)] * 3
    powers = jnp.concatenate(powers, axis=1)
    for b in range(TILES):
        at = [slice(s * PITCH + b * SLAB, s * PITCH + (b + 1) * SLAB) for s in range(8)]
        field = jnp.concatenate(
            [side_by_side(part) for part in row_sums([slope[at[s], :] for s in range(8)])], axis=1
        )
        moment[b * 32 : b * 32 + 16, :] = dot(powers, field, NT)
        gaze, weights = [], []
        for s in range(8):
            look = jnp.concatenate(
                [*pieces(jnp.concatenate([seen[b][c][s : s + 1, :] for c in range(3)], axis=0))][:2]
                + [jnp.zeros((10, LANES), BF16)],
                axis=0,
            )
            gaze += [look, look]
            weights += pieces(weight_ref[at[s], :])[:2]
        shades = dot(jnp.concatenate(gaze, axis=1), jnp.concatenate(weights, axis=1), NT)
        moment[b * 32 + 16 : (b + 1) * 32, :] = shades
    entry = [entry_ref[pl.ds(p, TILES, stride=16), :] for p in range(PARAMS)]
    jac = camera_rows(fixed_ref)
    m0, mx, my, mxx, mxy, myy = (moment[pl.ds(n, TILES, stride=32), :] for n in range(6))
    variance, xx, xy, yy, det = covariance(entry[3:6], jac)
    cx = sum(jac[0][j] * entry[j] for j in range(3)) + jac[0][3] - 0.5
    cy = sum(jac[1][j] * entry[j] for j in range(3)) + jac[1][3] - 0.5
    sx = mx - cx * m0
    sy = my - cy * m0
    sxx = mxx - cx * (mx + sx)
    sxy = mxy - cx * my - cy * sx
    syy = myy - cy * (my + sy)
    inverse = 1.0 / det
    conic = (yy * inverse, -xy * inverse, xx * inverse)
    d_cx = conic[0] * sx + conic[1] * sy
    d_cy = conic[1] * sx + conic[2] * sy
    d_a, d_b, d_c = -0.5 * sxx, -sxy, -0.5 * syy
    d_det = -(d_a * conic[0] + d_b * conic[1] + d_c * conic[2]) * inverse
    d_xx = d_c * inverse + d_det * yy
    d_yy = d_a * inverse + d_det * xx
    d_xy = -d_b * inverse - 2.0 * xy * d_det
    result = [jac[0][j] * d_cx + jac[1][j] * d_cy for j in range(3)]
    result += [
        2.0
        * variance[j]
        * (
            jac[0][j] * jac[0][j] * d_xx
            + jac[0][j] * jac[1][j] * d_xy
            + jac[1][j] * jac[1][j] * d_yy
        )
        for j in range(3)
    ]
    result += [m0 * (1.0 - jax.nn.sigmoid(entry[6]))]
    result += [
        moment[pl.ds(16 + c, TILES, stride=32), :] + moment[pl.ds(19 + c, TILES, stride=32), :]
        for c in range(3)
    ]
    for p, value in enumerate(result):
        grads[p * TILES : (p + 1) * TILES, :] = value
    placed[...] = jnp.zeros((LANES, LANES), F32)
    outgoing = jnp.zeros((LANES, LANES), F32)
    for b in range(TILES):
        mine = grads[pl.ds(b, PARAMS, stride=TILES), :]
        rank = listed(fixed_ref, RANK, b)
        for r in range(SLOTS):
            placed[r * PARAMS : (r + 1) * PARAMS, :] = jnp.where(rank == r, mine, 0.0)
        here = iota((16, LANES), 0) == rank
        row = jnp.where(here, fixed_ref[ROW + b : ROW + b + 1, :], 0.0)
        placed[SLOTS * PARAMS : SLOTS * PARAMS + 16, :] = row
        named = onehot(listed(fixed_ref, OWNER, b), LANES).astype(BF16)
        named = jnp.concatenate([named, named, named], axis=1)
        outgoing = outgoing + dot(named, side_by_side(placed[...]), NT)
    outgoing_ref[...] = outgoing
    shown.wait()


def collect_kernel(incoming_ref, sums_ref, turned):
    turned[...] = incoming_ref[...].T
    total = jnp.zeros((BLOCKS * 16, LANES), F32)
    for r in range(SLOTS):
        row = turned[SLOTS * PARAMS + r : SLOTS * PARAMS + r + 1, :].astype(I32)
        pick = onehot(row & (LANES - 1), LANES).astype(BF16)
        block = row >> 7
        value = turned[r * PARAMS : r * PARAMS + 16, :]
        spread = jnp.concatenate(
            [jnp.where(block == a, value, 0.0) for a in range(BLOCKS)], axis=0
        )
        total = total + dot(
            side_by_side(spread), jnp.concatenate([pick, pick, pick], axis=1), NT
        )
    for a in range(BLOCKS):
        sums_ref[a * PARAMS : (a + 1) * PARAMS, :] = total[a * 16 : a * 16 + PARAMS]


def adam_kernel(sums_ref, params_ref, first_ref, second_ref, new_ref, new_first_ref, new_second_ref):
    for a in range(BLOCKS):
        at = slice(a * LANES, (a + 1) * LANES)
        gradient = sum(sums_ref[i, a * PARAMS : (a + 1) * PARAMS, :] for i in range(DEPTHS))
        first = 0.9 * first_ref[:, at] + 0.1 * gradient
        second = 0.999 * second_ref[:, at] + 0.001 * gradient * gradient
        step = first / (1.0 - 0.9**10) / (jnp.sqrt(second / (1.0 - 0.999**10)) + 1e-08)
        new_ref[:, at] = params_ref[a * PARAMS : (a + 1) * PARAMS, :] - 0.05 * step
        new_first_ref[:, at] = first
        new_second_ref[:, at] = second


def call(kernel, outs, ins, scratch=(), grant=40, to=None):
    return pl.pallas_call(
        kernel,
        out_shape=[jax.ShapeDtypeStruct(shape, dtype) for shape, dtype in outs],
        in_specs=ins,
        out_specs=to or [VMEM] * len(outs),
        scratch_shapes=list(scratch),
        compiler_params=pltpu.CompilerParams(vmem_limit_bytes=grant * 2**20),
    )


def exchanged_in_plane(array):
    return lax.all_to_all(array, TILE[:2], 0, 0, tiled=True)


def exchanged(array):
    groups = [
        [zy * 4 + hi * 2 + (hi ^ g) for zy in range(LANES // 2) for hi in range(2)] for g in range(2)
    ]
    whole = lax.all_to_all(
        array.reshape(LANES, 1, LANES),
        (*TILE, DEPTH[0]),
        0,
        0,
        axis_index_groups=groups,
        tiled=True,
    )
    return whole.reshape(LANES, LANES)


def body(
    positions,
    log_scales,
    opacity_logits,
    colors,
    first_moment,
    second_moment,
    cameras,
    background,
    target,
    tile_view,
    tile_length,
    list_owner,
    list_row,
):
    square = (LANES, LANES)
    held = pltpu.VMEM(square, F32)
    plane = LANES // 2
    flat = (BLOCKS * PARAMS, LANES)
    lists = (TILES, SLAB)
    sources = (
        list_owner.reshape(lists),
        list_row.reshape(lists),
        positions,
        log_scales,
        opacity_logits,
        colors,
    )
    results = [((plane, LANES), I32), ((16, LANES), I32), (flat, F32)]
    request, listing, params = call(
        request_kernel,
        results,
        [HBM] * 6,
        [pltpu.VMEM(a.shape, a.dtype) for a in sources] + [pltpu.SemaphoreType.DMA((6,))],
        GRANT_ALL,
    )(*sources)
    asked = exchanged_in_plane(request.reshape(plane, 1, LANES)).reshape(plane, LANES)
    theirs = lax.ppermute(params, (TILE[2], DEPTH[0]), [(0, 3), (3, 0), (1, 2), (2, 1)])
    depth = lax.axis_index(DEPTH).astype(I32).reshape(1)
    loose = (
        tile_view,
        tile_length,
        cameras,
        background,
        target.transpose(1, 0, 2),
        listing,
    )
    (fixed,) = call(
        fixed_kernel,
        [((FIXED, LANES), F32)],
        [SMEM] + [HBM] * 6,
        [pltpu.SMEM(a.shape, a.dtype) for a in loose[:4]]
        + [pltpu.VMEM(a.shape, a.dtype) for a in loose[4:]]
        + [pltpu.SemaphoreType.DMA((6,))],
        GRANT_ALL,
    )(depth, *loose)
    side = lax.axis_index(TILE[2]).astype(I32).reshape(1)
    table, fixed, powers = call(
        table_kernel,
        [((2 * BLOCKS * 16, 3 * LANES), BF16), ((FIXED, LANES), F32), ((32, 1024), BF16)],
        [SMEM, VMEM, VMEM, VMEM],
    )(side, params, theirs, fixed)
    (reply,) = call(
        reply_kernel,
        [((plane, 2, LANES), F32)],
        [VMEM, VMEM],
        [pltpu.VMEM((LANES, plane), I32), held],
    )(asked, table)
    fetched = exchanged_in_plane(reply).reshape(square)
    tilted = (8 * PITCH, LANES)
    slab, alpha, weight, shade, entry = call(
        forward_kernel,
        [
            (square, F32),
            (tilted, F32),
            (tilted, F32),
            ((3, TILES * SLAB + 8, LANES), F32),
            ((TILES * 16, LANES), F32),
        ],
        [VMEM] * 3,
        [held, held],
    )(fetched, fixed, powers)
    slabs = lax.all_gather(slab[None], DEPTH, axis=0, tiled=True)
    image, outgoing = call(
        backward_kernel,
        [((3, TILES, 1024), F32), (square, F32)],
        [VMEM] * 6,
        [
            pltpu.VMEM(tilted, F32),
            held,
            pltpu.VMEM((PARAMS * TILES, LANES), F32),
            held,
            pltpu.VMEM((3 * TILES * 8, LANES), F32),
            pltpu.VMEM((3, TILES, 1024), F32),
            pltpu.SemaphoreType.DMA(()),
        ],
        to=[HBM, VMEM],
    )(slabs, alpha, weight, shade, entry, fixed)
    incoming = exchanged(outgoing)
    (sums,) = call(
        collect_kernel,
        [((BLOCKS * PARAMS, LANES), F32)],
        [VMEM],
        [held],
    )(incoming)
    sums = lax.all_gather(sums[None], DEPTH, axis=0, tiled=True)
    updated = call(adam_kernel, [(first_moment.shape, F32)] * 3, [VMEM] * 4)(
        sums, params, first_moment, second_moment
    )
    return (image.transpose(1, 0, 2), *updated)


def solution(mesh):
    torus = Mesh(mesh.devices.reshape(8, 8, 2, 2, 2), (*TILE, *DEPTH))
    split = P(None, TILE)
    placed = (
        *[split] * 6,
        P(),
        P(),
        P(TILE, None, None),
        P(TILE),
        P(TILE),
        P(DEPTH, TILE, None, None),
        P(DEPTH, TILE, None),
    )
    return jax.shard_map(
        body,
        mesh=torus,
        in_specs=placed,
        out_specs=(P(TILE, None, None), split, split, split),
        check_vma=False,
    )
```
